32 devices in a mesh: dp: 8 (over y, x, core), tensor: 4 (over z).
Axes of the slice: x: 2, y: 2, z: 4, core: 2. Of those that a mesh axis runs over, the one named last changes fastest.
Arguments:
- tokens: bfloat16 [8192, 2048], P(('dp', 'tensor')), may hold values from -6 to 6
- positions: int32 [8192], P('dp'), may hold values from 0 to 767, as said below
- cotangent: bfloat16 [8192, 2048], P(('dp', 'tensor')), may hold values from -18 to 18
- query_weight: float32 [2048, 2048], P('dp', 'tensor'), may hold values from -0.125 to 0.125
- query_first: float32 [2048, 2048], P('dp', 'tensor'), may hold values from -64 to 64
- query_second: float32 [2048, 2048], P('dp', 'tensor'), may hold values from 8.192 to 32.768
- keyval_weight: float32 [2, 2048, 256], P(None, ('dp', 'tensor')), may hold values from -0.125 to 0.125
- keyval_first: float32 [2, 2048, 256], P(None, ('dp', 'tensor')), may hold values from -128 to 128
- keyval_second: float32 [2, 2048, 256], P(None, ('dp', 'tensor')), may hold values from 32.768 to 131.072
- output_weight: float32 [2048, 2048], P('tensor', 'dp'), may hold values from -1 to 1
- output_first: float32 [2048, 2048], P('tensor', 'dp'), may hold values from -6 to 6
- output_second: float32 [2048, 2048], P('tensor', 'dp'), may hold values from 0.32768 to 1.31072
- gateup_weight: float32 [2, 2048, 5632], P(None, 'dp', 'tensor'), may hold values from -0.125 to 0.125
- gateup_first: float32 [2, 2048, 5632], P(None, 'dp', 'tensor'), may hold values from -20 to 20
- gateup_second: float32 [2, 2048, 5632], P(None, 'dp', 'tensor'), may hold values from 0.98304 to 4.096
- down_weight: float32 [5632, 2048], P('tensor', 'dp'), may hold values from -0.078125 to 0.078125
- down_first: float32 [5632, 2048], P('tensor', 'dp'), may hold values from -32 to 32
- down_second: float32 [5632, 2048], P('tensor', 'dp'), may hold values from 2.94912 to 11.4688
- gains: float32 [2, 2048], P(None, ('dp', 'tensor')), may hold values from 0.5 to 1.5
- gains_first: float32 [2, 2048], P(None, ('dp', 'tensor')), may hold values from -64 to 64
- gains_second: float32 [2, 2048], P(None, ('dp', 'tensor')), may hold values from 8.192 to 32.768
Outputs:
- block_out: float32 [8192, 2048], P(('dp', 'tensor'))
- layer_input_gradient: float32 [8192, 2048], P(('dp', 'tensor'))
- query_first_new: float32 [2048, 2048], P('dp', 'tensor')
- query_second_new: float32 [2048, 2048], P('dp', 'tensor')
- query_new: float32 [2048, 2048], P('dp', 'tensor')
- keyval_first_new: float32 [2, 2048, 256], P(None, ('dp', 'tensor'))
- keyval_second_new: float32 [2, 2048, 256], P(None, ('dp', 'tensor'))
- keyval_new: float32 [2, 2048, 256], P(None, ('dp', 'tensor'))
- output_first_new: float32 [2048, 2048], P('tensor', 'dp')
- output_second_new: float32 [2048, 2048], P('tensor', 'dp')
- output_new: float32 [2048, 2048], P('tensor', 'dp')
- gateup_first_new: float32 [2, 2048, 5632], P(None, 'dp', 'tensor')
- gateup_second_new: float32 [2, 2048, 5632], P(None, 'dp', 'tensor')
- gateup_new: float32 [2, 2048, 5632], P(None, 'dp', 'tensor')
- down_first_new: float32 [5632, 2048], P('tensor', 'dp')
- down_second_new: float32 [5632, 2048], P('tensor', 'dp')
- down_new: float32 [5632, 2048], P('tensor', 'dp')
- gains_first_new: float32 [2, 2048], P(None, ('dp', 'tensor'))
- gains_second_new: float32 [2, 2048], P(None, ('dp', 'tensor'))
- gains_new: float32 [2, 2048], P(None, ('dp', 'tensor'))
The draws below stay inside these ranges and needn't reach their ends.
Inputs may be any that keep to these rules, and one draw needn't show every extreme that they name: Each sequence of 1024 tokens is three documents; positions count from 0 at each document's first token and rise by one; the middle document starts within the first 256 tokens and holds exactly 768 tokens.
All inputs are finite; a program needn't handle non-finite values.
Results may differ from the reference program's by a relative error of at most 0.015.
Values may be sent and summed in bfloat16 or wider, within the bound.
No kernel may reach another device: no remote copies, remote signals or barrier semaphores. Data moves between devices by JAX's collectives and lax.ppermute only.
A program may use at most 256 MiB of HBM per device.

```python
import math
import jax
import jax.numpy as jnp
from jax import lax

D = 2048
H = 32
KVH = 4
FF = 5632
HD = 64
STEP = 10
LEN = 1024
TOKENS = 8192
GROUP = 8
KVD = 256


def draw_positions(key, part):
    key = jax.random.fold_in(key, 11)
    seq_count = TOKENS // LEN
    doc_start = jax.random.randint(key, (seq_count, 1), 1, LEN // 4 + 1)
    doc_end = doc_start + (LEN - LEN // 4)
    index_row = jnp.arange(LEN)[None, :]
    inside = jnp.where(index_row < doc_end, index_row - doc_start, index_row - doc_end)
    placed = jnp.where(index_row < doc_start, index_row, inside)
    return placed.reshape(-1).astype(jnp.int32)


def draw_cotangent(key, part):
    key = jax.random.fold_in(key, 23)
    seq_count = TOKENS // LEN
    row_ids = jnp.arange(TOKENS)
    seq_frac = (row_ids // LEN).astype(jnp.float32) / max(seq_count - 1, 1)
    pos_frac = (row_ids % LEN).astype(jnp.float32) / (LEN - 1)
    base = jnp.clip(jax.random.normal(key, (TOKENS, D), jnp.float32), -6.0, 6.0)
    factor = (1.0 + 2.0 * seq_frac) * (1.0 + 2.0 * pos_frac) / 3.0
    return (base * factor[:, None]).astype(jnp.bfloat16)


def block_levels(key, dims, split, least, largest):
    loudness = 1.0
    for dim, blocks in split:
        draws = jax.random.uniform(jax.random.fold_in(jax.random.fold_in(key, 6), dim), (blocks,), jnp.float32, least / len(split), largest / len(split))
        loudness = loudness * jnp.repeat(jnp.exp(draws), dims[dim] // blocks).reshape((-1,) + (1,) * (len(dims) - 1 - dim))
    return loudness


def gaussian(stream_key, shape, scale, limit, cuts=(), held_as=jnp.bfloat16):
    gain = block_levels(stream_key, shape, cuts, -0.22, 0.18) if cuts else 1.0
    values = jax.random.normal(stream_key, shape, jnp.float32) * scale * gain
    return jnp.minimum(jnp.maximum(values, -limit), limit).astype(held_as)


def setup_inputs(seed: int = 0) -> dict:
    streams_of = jax.random.split(jax.random.key(seed), 22)
    return {
        "tokens": gaussian(streams_of[0], (TOKENS, D), 1.0, 6.0, ((0, 32),)),
        "positions": draw_positions(jax.random.fold_in(streams_of[21], 71), 0),
        "cotangent": draw_cotangent(jax.random.fold_in(streams_of[21], 71), 0),
        "query_weight": gaussian(streams_of[3], (D, D), D ** -0.5, 0.125, ((0, 8), (1, 4)), jnp.float32),
        "query_first": gaussian(streams_of[4], (D, D), (0.11 * TOKENS ** 0.5), 64.0, ((0, 8), (1, 4)), jnp.float32),
        "query_second": jnp.clip(jnp.exp(math.log(32.768) - 1.3862944 * jax.random.uniform(streams_of[5], (D, D), jnp.float32) ** block_levels(streams_of[5], (D, D), ((0, 8), (1, 4)), -0.2, 0.2)), 8.192, 32.768),
        "keyval_weight": gaussian(streams_of[6], (2, D, KVD), D ** -0.5, 0.125, ((1, 32),), jnp.float32),
        "keyval_first": gaussian(streams_of[7], (2, D, KVD), (0.22 * TOKENS ** 0.5), 128.0, ((1, 32),), jnp.float32),
        "keyval_second": jnp.clip(jnp.exp(math.log(131.072) - 1.3862944 * jax.random.uniform(streams_of[8], (2, D, KVD), jnp.float32) ** block_levels(streams_of[8], (2, D, KVD), ((1, 32),), -0.2, 0.2)), 32.768, 131.072),
        "output_weight": gaussian(streams_of[9], (D, D), (D // 64) ** -0.5, 1.0, ((0, 4), (1, 8)), jnp.float32),
        "output_first": gaussian(streams_of[10], (D, D), (0.022 * TOKENS ** 0.5), 6.0, ((0, 4), (1, 8)), jnp.float32),
        "output_second": jnp.clip(jnp.exp(math.log(1.31072) - 1.3862944 * jax.random.uniform(streams_of[11], (D, D), jnp.float32) ** block_levels(streams_of[11], (D, D), ((0, 4), (1, 8)), -0.2, 0.2)), 0.32768, 1.31072),
        "gateup_weight": gaussian(streams_of[12], (2, D, FF), D ** -0.5, 0.125, ((1, 8), (2, 4)), jnp.float32),
        "gateup_first": gaussian(streams_of[13], (2, D, FF), (0.04 * TOKENS ** 0.5), 20.0, ((1, 8), (2, 4)), jnp.float32),
        "gateup_second": jnp.clip(jnp.exp(math.log(4.096) - 1.4271164 * jax.random.uniform(streams_of[14], (2, D, FF), jnp.float32) ** block_levels(streams_of[14], (2, D, FF), ((1, 8), (2, 4)), -0.2, 0.2)), 0.98304, 4.096),
        "down_weight": gaussian(streams_of[15], (FF, D), FF ** -0.5, 0.078125, ((0, 4), (1, 8)), jnp.float32),
        "down_first": gaussian(streams_of[16], (FF, D), (0.066 * TOKENS ** 0.5), 32.0, ((0, 4), (1, 8)), jnp.float32),
        "down_second": jnp.clip(jnp.exp(math.log(11.4688) - 1.3581234 * jax.random.uniform(streams_of[17], (FF, D), jnp.float32) ** block_levels(streams_of[17], (FF, D), ((0, 4), (1, 8)), -0.2, 0.2)), 2.94912, 11.4688),
        "gains": jnp.clip(1.0 + 0.1 * jax.random.normal(streams_of[18], (2, D), jnp.float32), 0.5, 1.5),
        "gains_first": gaussian(streams_of[19], (2, D), (0.11 * TOKENS ** 0.5), 64.0, ((1, 32),), jnp.float32),
        "gains_second": jnp.clip(jnp.exp(math.log(32.768) - 1.3862944 * jax.random.uniform(streams_of[20], (2, D), jnp.float32) ** block_levels(streams_of[20], (2, D), ((1, 32),), -0.2, 0.2)), 8.192, 32.768),
    }


EPS = 1e-05
BETA_ONE = 0.9
BETA_TWO = 0.999
ADAM_EPS = 1e-08
DECAY = 0.1
RATE_QUERY = 0.06
RATE_KEYVAL = 0.06
RATE_OUTPUT = 0.5
RATE_GATEUP = 0.06
RATE_DOWN = 0.04
RATE_GAINS = 1.5
HIGH = lax.Precision.HIGHEST

@jax.custom_vjp
def low(v):
    return lax.optimization_barrier(v.astype(jnp.bfloat16)).astype(jnp.float32)

@jax.custom_vjp
def low_back(v):
    return v

def low_keep(v):
    return (low(v), None)

def low_pass(kept, grad):
    return (grad,)

def back_keep(v):
    return (v, None)

def back_low(kept, grad):
    return (low(grad),)
low.defvjp(low_keep, low_pass)
low_back.defvjp(back_keep, back_low)

def multiply(left, right):
    return jnp.dot(left, right, precision=HIGH)

def normalize(rows_in):
    return rows_in * lax.rsqrt(lax.optimization_barrier(jnp.mean(rows_in * rows_in, -1, keepdims=True)) + EPS)

def rope_tables(positions, width):
    freqs = 10000.0 ** (-jnp.arange(0, width, 2, dtype=jnp.float32) / width)
    angles = positions.astype(jnp.float32)[:, None] * freqs[None, :]
    angles = jnp.concatenate([angles, angles], -1)
    return (jnp.cos(angles), jnp.sin(angles))

def rotate_half(values):
    half = values.shape[-1] // 2
    return jnp.concatenate([-values[..., half:], values[..., :half]], -1)

def rope(values, cosine, sine):
    return values * cosine[:, None, :] + rotate_half(values) * sine[:, None, :]

def attend(pieces):
    queries, keys, values, positions = pieces
    scores = low_back(jnp.einsum('qgd,kd->gqk', queries, keys, precision=HIGH) * HD ** (-0.5))
    row_ids = jnp.arange(LEN)
    allowed = (row_ids[None, :] <= row_ids[:, None]) & (row_ids[None, :] >= (row_ids - positions)[:, None])
    scores = jnp.where(allowed[None], scores, -1e+30)
    row_max = lax.optimization_barrier(jnp.max(scores, -1, keepdims=True))
    expo_vals = jnp.exp(scores - row_max)
    prob_low = low(expo_vals / lax.optimization_barrier(jnp.sum(expo_vals, -1, keepdims=True)))
    return jnp.einsum('gqk,kd->qgd', prob_low, values, precision=HIGH)

def forward(tokens, positions, query_weight, keyval_weight, output_weight, gateup_weight, down_weight, gains):
    gain_low = low(gains)
    first_normalized = low(normalize(tokens) * gain_low[0])
    cosine, sine = rope_tables(positions, HD)
    query_pre = low_back(multiply(first_normalized, low(query_weight)))
    queries = low(rope(query_pre.reshape(TOKENS, H, HD), cosine, sine))
    key_pre = low_back(multiply(first_normalized, low(keyval_weight[0])))
    keys = low(rope(key_pre.reshape(TOKENS, KVH, HD), cosine, sine))
    values = low(low_back(multiply(first_normalized, low(keyval_weight[1])))).reshape(TOKENS, KVH, HD)
    seq_count = TOKENS // LEN
    query_groups = queries.reshape(seq_count, LEN, KVH, GROUP, HD).transpose(0, 2, 1, 3, 4).reshape(seq_count * KVH, LEN, GROUP, HD)
    key_groups = keys.reshape(seq_count, LEN, KVH, HD).transpose(0, 2, 1, 3).reshape(seq_count * KVH, LEN, HD)
    value_groups = values.reshape(seq_count, LEN, KVH, HD).transpose(0, 2, 1, 3).reshape(seq_count * KVH, LEN, HD)
    pos_groups = jnp.repeat(positions.reshape(seq_count, LEN), KVH, 0)
    mixed = lax.map(jax.checkpoint(attend), (query_groups, key_groups, value_groups, pos_groups))
    mixed = mixed.reshape(seq_count, KVH, LEN, GROUP, HD).transpose(0, 2, 1, 3, 4).reshape(TOKENS, H * HD)
    mixed_low = low(low_back(mixed))
    residual_stream = tokens + low_back(multiply(mixed_low, low(output_weight)))
    second_normalized = low(normalize(residual_stream) * gain_low[1])
    gate_proj = low_back(multiply(second_normalized, low(gateup_weight[0])))
    up_proj = low_back(multiply(second_normalized, low(gateup_weight[1])))
    hidden_low = low(jax.nn.silu(gate_proj) * up_proj)
    return residual_stream + multiply(hidden_low, low(down_weight))

def adamw(weight, first, second, grad, rate, decay):
    first_new = BETA_ONE * first + (1.0 - BETA_ONE) * grad
    second_new = BETA_TWO * second + (1.0 - BETA_TWO) * grad * grad
    fix_one = 1.0 - BETA_ONE ** STEP
    fix_two = 1.0 - BETA_TWO ** STEP
    direction = first_new / fix_one / (jnp.sqrt(second_new / fix_two) + ADAM_EPS)
    return (first_new, second_new, weight - rate * (direction + decay * weight))

def reference(tokens, positions, cotangent, query_weight, query_first, query_second, keyval_weight, keyval_first, keyval_second, output_weight, output_first, output_second, gateup_weight, gateup_first, gateup_second, down_weight, down_first, down_second, gains, gains_first, gains_second):

    def run_layer(tok_in, w_query, w_keyval, w_output, w_gateup, w_down, w_gains):
        return forward(tok_in, positions, w_query, w_keyval, w_output, w_gateup, w_down, w_gains)
    block_out, pullback = jax.vjp(run_layer, tokens.astype(jnp.float32), query_weight, keyval_weight, output_weight, gateup_weight, down_weight, gains)
    grads = pullback(cotangent.astype(jnp.float32))
    query_up = adamw(query_weight, query_first, query_second, grads[1], RATE_QUERY, DECAY)
    keyval_up = adamw(keyval_weight, keyval_first, keyval_second, grads[2], RATE_KEYVAL, DECAY)
    output_up = adamw(output_weight, output_first, output_second, grads[3], RATE_OUTPUT, DECAY)
    gateup_up = adamw(gateup_weight, gateup_first, gateup_second, grads[4], RATE_GATEUP, DECAY)
    down_up = adamw(down_weight, down_first, down_second, grads[5], RATE_DOWN, DECAY)
    gains_up = adamw(gains, gains_first, gains_second, grads[6], RATE_GAINS, 0.0)
    return (block_out, grads[0], query_up[0], query_up[1], query_up[2], keyval_up[0], keyval_up[1], keyval_up[2], output_up[0], output_up[1], output_up[2], gateup_up[0], gateup_up[1], gateup_up[2], down_up[0], down_up[1], down_up[2], gains_up[0], gains_up[1], gains_up[2])
```

```python
import functools

import jax
import jax.numpy as jnp
from jax import lax
from jax.experimental import pallas as pl
from jax.experimental.pallas import tpu as pltpu
from jax.sharding import PartitionSpec as P

H = 32
KVH = 4
HD = 64
GROUP = 8
KVD = KVH * HD
STEP = 10
EPS = 1e-05
BETA_ONE = 0.9
BETA_TWO = 0.999
ADAM_EPS = 1e-08
DECAY = 0.1
RATE_QUERY = 0.06
RATE_KEYVAL = 0.06
RATE_OUTPUT = 0.5
RATE_GATEUP = 0.06
RATE_DOWN = 0.04
RATE_GAINS = 1.5
LOW = jnp.bfloat16
F32 = jnp.float32
TALL = 128
VMEM_LIMIT = 56 * 1024 * 1024
LONG = pl.CostEstimate(flops=2 * 10**14, bytes_accessed=10**6, transcendentals=0)


def lasting(us):
    return pl.CostEstimate(flops=int(us * 1.15e9), bytes_accessed=10**6, transcendentals=0)


def contract(left, right, dim_left, dim_right):
    return lax.dot_general(
        left, right, (((dim_left,), (dim_right,)), ((), ())), preferred_element_type=F32
    )


def ring_offsets(n):
    return [0] + [-k for k in range(1, n // 2 + 1)] + [k for k in range(1, (n - 1) // 2 + 1)]


def shift(x, n, by):
    return lax.ppermute(x, "tensor", [(i, (i + by) % n) for i in range(n)])


def ring_gather(x, n, steps=None, known=None):
    slots, used = [x], 1
    for by, hops in ((1, n // 2), (-1, (n - 1) // 2)):
        held = x
        for hop in range(hops):
            if steps is not None and hop >= steps:
                slots.append(None)
                continue
            if known is not None and known[used + hop] is not None:
                held = known[used + hop]
            else:
                held = shift(held, n, by)
            slots.append(held)
        used += hops
    return slots


def after(late, early):
    return lax.optimization_barrier((late, early))


def ring_way(slots, n, by, passed=None, hold=None):
    first, hops = (1, n // 2) if by < 0 else (1 + n // 2, (n - 1) // 2)
    held = None
    for k in range(hops, 0, -1):
        part = slots[first + k - 1]
        if held is not None:
            part = (part.astype(F32) + held.astype(F32)).astype(LOW)
            if hold is not None and k == 1:
                part, _ = after(part, hold)
            if passed is not None:
                passed.append(part)
        held = shift(part.astype(LOW), n, by)
    return held


def ring_most(slots, n):
    held = None
    for k in range(n // 2, 1, -1):
        part = slots[k] if held is None else ring_sum(slots[k], held)
        held = shift(part.astype(LOW), n, -1)
    return held


def ring_last(slots, n, held, hold=None):
    part = (slots[1] if held is None else ring_sum(slots[1], held)).astype(LOW)
    if hold is not None:
        part, _ = after(part, hold)
    return shift(part, n, -1)


def ring_sum(own, *arrived):
    total = own.astype(F32)
    for held in arrived:
        if held is not None:
            total = total + held.astype(F32)
    return total


def ring_scatter(slots, n):
    return ring_sum(slots[0], ring_way(slots, n, -1), ring_way(slots, n, 1))


def swap(x, size, bit):
    return lax.ppermute(x, "dp", [(i, i ^ bit) for i in range(size)])


def dp_plan(size, block):
    bits = [1 << i for i in range(1, size.bit_length() - 1)]
    return [bits, bits[::-1]] if block >= 256 else [bits]


def dp_order(size, block, odd):
    plan = dp_plan(size, block)
    me = lax.axis_index("dp")
    places = []
    for h, bits in enumerate(plan):
        partners = [odd]
        for bit in bits:
            partners += [p | bit for p in partners]
        places += [(me ^ p) * len(plan) + h for p in partners]
    return jnp.stack(places).astype(jnp.int32)


def dp_spread(x, size, hold):
    block = x.shape[0]
    plan = dp_plan(size, block)
    tall = block // len(plan)
    even = [x[h * tall : (h + 1) * tall] for h in range(len(plan))]
    for i in range(len(plan[0])):
        got = [swap(held, size, bits[i]) for held, bits in zip(even, plan)]
        even = [jnp.concatenate(pair, 0) for pair in zip(even, got)]
        if i == 0:
            even, _ = after(even, hold)
    return even


def dp_scatter(held, size, hold):
    plan = dp_plan(size, 2 * held.shape[0] // size)
    tall = held.shape[0] // len(plan)
    parts = [held[h * tall : (h + 1) * tall] for h in range(len(plan))]
    for i in reversed(range(len(plan[0]))):
        half = parts[0].shape[0] // 2
        got = [swap(part[half:], size, bits[i]) for part, bits in zip(parts, plan)]
        if i == len(plan[0]) - 1:
            got, _ = after(got, hold)
        parts = [ring_sum(part[:half], new).astype(LOW) for part, new in zip(parts, got)]
    return jnp.concatenate(parts, 0)


def norm_statistics(rows_in):
    inverse = lax.rsqrt(jnp.mean(rows_in * rows_in, -1, keepdims=True) + EPS)
    return rows_in * inverse, inverse


def norm_backward(grad, unit, inverse, gain):
    scaled = grad * gain
    return inverse * (scaled - unit * jnp.mean(scaled * unit, -1, keepdims=True))


def adamw(weight, first, second, grad, rate, decay):
    first_new = BETA_ONE * first + (1.0 - BETA_ONE) * grad
    second_new = BETA_TWO * second + (1.0 - BETA_TWO) * grad * grad
    fix_one = 1.0 - BETA_ONE**STEP
    fix_two = 1.0 - BETA_TWO**STEP
    direction = first_new / fix_one / (jnp.sqrt(second_new / fix_two) + ADAM_EPS)
    return first_new, second_new, weight - rate * (direction + decay * weight)


def turn(values, cosine, sine):
    upper, lower = values[: HD // 2], values[HD // 2 :]
    return jnp.concatenate([upper * cosine - lower * sine, lower * cosine + upper * sine], 0)


def begin_kernel(
    x_ref, gain_ref, weight_ref, cos_ref, sin_ref, out_ref, rows_ref, gains_ref, inverse_ref
):
    gains = gain_ref[...].astype(F32).T[: gains_ref.shape[0]]
    unit, inverse = norm_statistics(x_ref[...].astype(F32))
    rows = (unit * gains[:1]).astype(LOW)
    rows_ref[...], gains_ref[...], inverse_ref[...] = rows, gains, inverse
    wide = jnp.dot(rows, weight_ref[...], preferred_element_type=F32).T
    cosine, sine = cos_ref[...], sin_ref[...]
    for h in range(KVH):
        here = slice(h * HD, (h + 1) * HD)
        out_ref[here, :] = turn(wide[here], cosine, sine).astype(LOW)
    out_ref[KVD:, :] = wide[KVD:].astype(LOW)


def begin(x, weight, cosine, sine):
    tokens, width = x.shape
    cols = 2 * KVD
    return pl.pallas_call(
        begin_kernel,
        grid=(1,),
        in_specs=[
            pl.BlockSpec((tokens, width), lambda b: (0, 0)),
            pl.BlockSpec((width, TALL), lambda b: (0, (H * HD + cols) // TALL)),
            pl.BlockSpec((width, cols), lambda b: (0, H * HD // cols)),
            pl.BlockSpec(cosine.shape, lambda b: (0, 0)),
            pl.BlockSpec(sine.shape, lambda b: (0, 0)),
        ],
        out_specs=[
            pl.BlockSpec((cols, tokens), lambda b: (0, 0)),
            pl.BlockSpec((tokens, width), lambda b: (0, 0)),
            pl.BlockSpec((8, width), lambda b: (0, 0)),
            pl.BlockSpec((tokens, 1), lambda b: (0, 0)),
        ],
        out_shape=[
            jax.ShapeDtypeStruct((cols, tokens), LOW),
            jax.ShapeDtypeStruct((tokens, width), LOW),
            jax.ShapeDtypeStruct((8, width), F32),
            jax.ShapeDtypeStruct((tokens, 1), F32),
        ],
        compiler_params=pltpu.CompilerParams(vmem_limit_bytes=VMEM_LIMIT),
        cost_estimate=lasting(5.0),
        name="begin",
    )(x, weight, weight, cosine, sine)


def project_kernel(rows_ref, weight_ref, cos_ref, sin_ref, out_ref):
    wide = jnp.dot(rows_ref[...], weight_ref[...], preferred_element_type=F32).T
    cosine, sine = cos_ref[...], sin_ref[...]
    for h in range(wide.shape[0] // HD):
        here = slice(h * HD, (h + 1) * HD)
        out_ref[here, :] = (turn(wide[here], cosine, sine) * HD ** (-0.5)).astype(LOW)


def project(rows, weight, cosine, sine):
    tokens, width = rows.shape
    cols = 2 * KVD
    blocks = H * HD // cols
    return pl.pallas_call(
        project_kernel,
        grid=(blocks,),
        in_specs=[
            pl.BlockSpec((tokens, width), lambda b: (0, 0)),
            pl.BlockSpec((width, cols), lambda b: (0, b)),
            pl.BlockSpec(cosine.shape, lambda b: (0, 0)),
            pl.BlockSpec(sine.shape, lambda b: (0, 0)),
        ],
        out_specs=pl.BlockSpec((cols, tokens), lambda b: (b, 0)),
        out_shape=jax.ShapeDtypeStruct((blocks * cols, tokens), LOW),
        compiler_params=pltpu.CompilerParams(vmem_limit_bytes=VMEM_LIMIT),
        cost_estimate=lasting(8.0),
        name="project",
    )(rows, weight, cosine, sine)


def fill_bias(meta_ref, pos_ref, bias_ref, slots, tokens):
    query = meta_ref[2 * slots] + lax.broadcasted_iota(jnp.int32, (tokens, tokens), 1)
    least = query - pos_ref[...]
    row = lax.broadcasted_iota(jnp.int32, (tokens, tokens), 0)
    for c in range(slots):
        key = meta_ref[c] + row
        bias_ref[c] = jnp.where((key <= query) & (key >= least), 0.0, -1e30)


def attend_kernel(
    slots, heads, meta_ref, pos_ref, q_ref, kv_ref, out_ref, rows_ref, lse_ref, bias_ref
):
    tokens = q_ref.shape[1]
    block = pl.program_id(0)

    @pl.when(block == 0)
    def _():
        fill_bias(meta_ref, pos_ref, bias_ref, slots, tokens)

    start = pl.multiple_of(meta_ref[slots + block] * HD, HD)
    keys = [kv_ref[c, pl.ds(start, HD), :].T for c in range(slots)]
    values = [kv_ref[c, pl.ds(KVD + start, HD), :] for c in range(slots)]
    for h in range(heads):
        query = q_ref[h * HD : (h + 1) * HD, :]
        scores = [
            jnp.dot(keys[c], query, preferred_element_type=F32) + bias_ref[c] for c in range(slots)
        ]
        peak = functools.reduce(jnp.maximum, [jnp.max(s, 0, keepdims=True) for s in scores])
        total = jnp.zeros_like(peak)
        mixed = jnp.zeros((HD, tokens), F32)
        for c in range(slots):
            expo = jnp.exp(scores[c] - peak)
            total = total + jnp.sum(expo, 0, keepdims=True)
            mixed = mixed + jnp.dot(values[c], expo.astype(LOW), preferred_element_type=F32)
        out_ref[h * HD : (h + 1) * HD, :] = (mixed / total).astype(LOW)
        lse_ref[0, h : h + 1, :] = peak + jnp.log(total)
    rows_ref[...] = out_ref[...].T


def attend(meta, pos_row, q_t, kv_slots, slots):
    tokens = q_t.shape[1]
    heads = H // slots
    rows = heads * HD
    return pl.pallas_call(
        functools.partial(attend_kernel, slots, heads),
        grid_spec=pltpu.PrefetchScalarGridSpec(
            num_scalar_prefetch=1,
            grid=(slots,),
            in_specs=[
                pl.BlockSpec((1, tokens), lambda b, m: (0, 0)),
                pl.BlockSpec((rows, tokens), lambda b, m: (b, 0)),
                pl.BlockSpec((slots, 2 * KVD, tokens), lambda b, m: (0, 0, 0)),
            ],
            out_specs=[
                pl.BlockSpec((rows, tokens), lambda b, m: (b, 0)),
                pl.BlockSpec((tokens, rows), lambda b, m: (0, b)),
                pl.BlockSpec((1, heads, tokens), lambda b, m: (b, 0, 0)),
            ],
            scratch_shapes=[pltpu.VMEM((slots, tokens, tokens), F32)],
        ),
        out_shape=[
            jax.ShapeDtypeStruct((H * HD, tokens), LOW),
            jax.ShapeDtypeStruct((tokens, H * HD), LOW),
            jax.ShapeDtypeStruct((slots, heads, tokens), F32),
        ],
        compiler_params=pltpu.CompilerParams(vmem_limit_bytes=VMEM_LIMIT),
        cost_estimate=pl.CostEstimate(
            flops=16 * H * HD * tokens * tokens * slots,
            bytes_accessed=4 * H * HD * tokens,
            transcendentals=H * tokens * tokens * slots,
        ),
        name="attend",
    )(meta, pos_row, q_t, kv_slots)


def attend_back_kernel(slots, heads, count, meta_ref, pos_ref, q_ref, kv_ref, back_ref, *refs):
    weights, refs = refs[:count], refs[count:]
    o_ref, lse_ref, cos_ref, sin_ref, dq_ref, dkv_out_ref = refs[:6]
    bias_ref, dkv_ref, do_ref, moved_ref = refs[6:]
    tokens = q_ref.shape[1]
    block = pl.program_id(0)

    @pl.when(block == 0)
    def _():
        fill_bias(meta_ref, pos_ref, bias_ref, slots, tokens)
        dkv_ref[...] = jnp.zeros_like(dkv_ref)
        for i in range(back_ref.shape[1] // TALL):
            at = pl.multiple_of(meta_ref[2 * slots + 1 + i] * TALL, TALL)
            moved_ref[:, i * TALL : (i + 1) * TALL] = back_ref[:, pl.ds(at, TALL)]

    grad_mixed, at = 0.0, 0
    for weight in weights:
        here = slice(at, at + weight.shape[0])
        grad_mixed += jnp.dot(moved_ref[:, here], weight[...], preferred_element_type=F32)
        at += weight.shape[0]
    do_ref[...] = grad_mixed.T.astype(LOW)
    start = pl.multiple_of(meta_ref[slots + block] * HD, HD)
    keys_t = [kv_ref[c, pl.ds(start, HD), :] for c in range(slots)]
    keys = [k.T for k in keys_t]
    values = [kv_ref[c, pl.ds(KVD + start, HD), :].T for c in range(slots)]
    cosine, sine = cos_ref[...], -sin_ref[...]
    grad_keys = [jnp.zeros((HD, tokens), F32) for _ in range(slots)]
    grad_values = [jnp.zeros((HD, tokens), F32) for _ in range(slots)]
    for h in range(heads):
        here = slice(h * HD, (h + 1) * HD)
        query, grad = q_ref[here, :], do_ref[here, :]
        delta = jnp.sum(grad.astype(F32) * o_ref[here, :].astype(F32), 0, keepdims=True)
        log_total = lse_ref[0, h : h + 1, :]
        grad_query = jnp.zeros((HD, tokens), F32)
        for c in range(slots):
            scores = jnp.dot(keys[c], query, preferred_element_type=F32) + bias_ref[c]
            prob = jnp.exp(scores - log_total)
            grad_prob = jnp.dot(values[c], grad, preferred_element_type=F32)
            grad_score = (prob * (grad_prob - delta)).astype(LOW)
            grad_values[c] = grad_values[c] + contract(grad, prob.astype(LOW), 1, 1)
            grad_keys[c] = grad_keys[c] + contract(query, grad_score, 1, 1)
            grad_query = grad_query + jnp.dot(keys_t[c], grad_score, preferred_element_type=F32)
        dq_ref[here, :] = (turn(grad_query, cosine, sine) * HD ** (-0.5)).astype(LOW)
    for c in range(slots):
        dkv_ref[c, pl.ds(start, HD), :] += grad_keys[c]
        dkv_ref[c, pl.ds(KVD + start, HD), :] += grad_values[c]

    @pl.when(block == pl.num_programs(0) - 1)
    def _():
        dkv_out_ref[...] = dkv_ref[...].astype(LOW)


def attend_back(meta, pos_row, q_t, kv_slots, back, weights, o_t, lse, cosine, sine, slots):
    tokens = q_t.shape[1]
    heads = H // slots
    rows = heads * HD
    head_block = pl.BlockSpec((rows, tokens), lambda b, m: (b, 0))
    table = pl.BlockSpec(cosine.shape, lambda b, m: (0, 0))
    whole = pl.BlockSpec((slots, 2 * KVD, tokens), lambda b, m: (0, 0, 0))
    return pl.pallas_call(
        functools.partial(attend_back_kernel, slots, heads, len(weights)),
        grid_spec=pltpu.PrefetchScalarGridSpec(
            num_scalar_prefetch=1,
            grid=(slots,),
            in_specs=[
                pl.BlockSpec((1, tokens), lambda b, m: (0, 0)),
                head_block,
                whole,
                pl.BlockSpec(back.shape, lambda b, m: (0, 0)),
                *[pl.BlockSpec((w.shape[0], rows), lambda b, m: (0, b)) for w in weights],
                head_block,
                pl.BlockSpec((1, heads, tokens), lambda b, m: (b, 0, 0)),
                table,
                table,
            ],
            out_specs=[head_block, whole],
            scratch_shapes=[
                pltpu.VMEM((slots, tokens, tokens), F32),
                pltpu.VMEM((slots, 2 * KVD, tokens), F32),
                pltpu.VMEM((rows, tokens), LOW),
                pltpu.VMEM(back.shape, LOW),
            ],
        ),
        out_shape=[
            jax.ShapeDtypeStruct((H * HD, tokens), LOW),
            jax.ShapeDtypeStruct((slots, 2 * KVD, tokens), LOW),
        ],
        compiler_params=pltpu.CompilerParams(vmem_limit_bytes=VMEM_LIMIT),
        cost_estimate=LONG,
        name="attend_back",
    )(meta, pos_row, q_t, kv_slots, back, *weights, o_t, lse, cosine, sine)


def mix_kernel(count, order_ref, o_ref, x_ref, gain_ref, *refs):
    weights, (h_ref, n_ref, inverse_ref) = refs[:count], refs[count : count + 3]
    held, sems = refs[count + 3 : -1], refs[-1]
    copies = [
        pltpu.make_async_copy(src, dst, sems.at[i]) for i, (src, dst) in enumerate(zip(weights, held))
    ]
    for copy in copies:
        copy.start()
    at = 0
    for copy, weight in zip(copies, held):
        copy.wait()
        mixed = contract(o_ref[...], weight[...], 1, 1)
        for i in range(weight.shape[0] // TALL):
            here = pl.ds(pl.multiple_of(order_ref[at] * TALL, TALL), TALL)
            h_ref[:, here] = x_ref[:, here].astype(F32) + mixed[:, i * TALL : (i + 1) * TALL]
            at += 1
    unit, inverse = norm_statistics(h_ref[...])
    n_ref[...] = (unit * gain_ref[...]).astype(LOW)
    inverse_ref[...] = inverse


def mix(order, o, x, gain, weights):
    tokens, width = x.shape
    count = len(weights)
    full = pl.BlockSpec((tokens, width), lambda i, o: (0, 0))
    return pl.pallas_call(
        functools.partial(mix_kernel, count),
        grid_spec=pltpu.PrefetchScalarGridSpec(
            num_scalar_prefetch=1,
            grid=(1,),
            in_specs=[
                pl.BlockSpec(o.shape, lambda i, o: (0, 0)),
                full,
                pl.BlockSpec((1, width), lambda i, o: (0, 0)),
            ]
            + [pl.BlockSpec(memory_space=pl.ANY)] * count,
            out_specs=[full, full, pl.BlockSpec((tokens, 1), lambda i, o: (0, 0))],
            scratch_shapes=[pltpu.VMEM(weight.shape, LOW) for weight in weights]
            + [pltpu.SemaphoreType.DMA((count,))],
        ),
        out_shape=[
            jax.ShapeDtypeStruct((tokens, width), F32),
            jax.ShapeDtypeStruct((tokens, width), LOW),
            jax.ShapeDtypeStruct((tokens, 1), F32),
        ],
        compiler_params=pltpu.CompilerParams(vmem_limit_bytes=VMEM_LIMIT),
        cost_estimate=lasting(6.0),
        name="mix",
    )(order, o, x, gain, *weights)


def tail_pack_kernel(n, piece, cols, ids_ref, owned_ref, *outs):
    block, start = owned_ref.shape[0], H * HD
    span = start + 2 * KVD
    for s, out_ref in enumerate(outs):
        at = pl.multiple_of(ids_ref[s] * piece, piece)
        out_ref[:block, :] = owned_ref[:, s * cols : (s + 1) * cols]
        row = block
        for lo in range(start, span, cols):
            out_ref[row : row + piece, :] = owned_ref[pl.ds(at, piece), lo : lo + cols]
            row += piece
        gains = owned_ref[pl.ds(at, piece), span : span + 128].astype(F32).T.astype(LOW)
        out_ref[row:, :] = jnp.zeros((16, cols), LOW)
        out_ref[row : row + 16, :piece] = gains[:16]


def tail_pack(ids, owned, piece, cols):
    n, block = ids.shape[0], owned.shape[0]
    height = block + piece * (2 * KVD // cols) + 16
    return pl.pallas_call(
        functools.partial(tail_pack_kernel, n, piece, cols),
        grid_spec=pltpu.PrefetchScalarGridSpec(
            num_scalar_prefetch=1,
            grid=(1,),
            in_specs=[pl.BlockSpec(owned.shape, lambda i, o: (0, 0))],
            out_specs=[pl.BlockSpec((height, cols), lambda i, o: (0, 0))] * n,
        ),
        out_shape=[jax.ShapeDtypeStruct((height, cols), LOW)] * n,
        compiler_params=pltpu.CompilerParams(vmem_limit_bytes=VMEM_LIMIT),
        cost_estimate=lasting(2.0),
        name="tail_pack",
    )(ids, owned)


def tail_adamw_kernel(block, piece, parts, *refs):
    total = ring_sum(*[ref[...] for ref in refs[:parts]])
    states, outs = refs[parts : parts + 9], refs[parts + 9 :]
    groups = 2 * KVD // total.shape[1]
    keyval = [total[block + g * piece : block + (g + 1) * piece] for g in range(groups)]
    weight, first, second = states[:3]
    outs[0][...], outs[1][...], outs[2][...] = adamw(
        weight[...], first[...], second[...], total[:block].T, RATE_OUTPUT, DECAY
    )
    weight, first, second = states[3:6]
    for j in range(2):
        if groups == 1:
            grad = keyval[0][:, j * KVD : (j + 1) * KVD]
        else:
            grad = jnp.concatenate(keyval[j * groups // 2 : (j + 1) * groups // 2], 1)
        outs[3][j], outs[4][j], outs[5][j] = adamw(
            weight[j], first[j], second[j], grad, RATE_KEYVAL, DECAY
        )
    weight, first, second = states[6:]
    outs[6][...], outs[7][...], outs[8][...] = adamw(
        weight[...], first[...], second[...], total[-16:, :piece][:2], RATE_GAINS, 0.0
    )


def tail_adamw(parts, states, block, piece):
    vmem = pl.BlockSpec(memory_space=pltpu.VMEM)
    shapes = [states[3 * i].shape for i in range(3) for _ in range(3)]
    return pl.pallas_call(
        functools.partial(tail_adamw_kernel, block, piece, len(parts)),
        in_specs=[vmem] * (len(parts) + 9),
        out_specs=[vmem] * 9,
        out_shape=[jax.ShapeDtypeStruct(shape, F32) for shape in shapes],
        compiler_params=pltpu.CompilerParams(vmem_limit_bytes=VMEM_LIMIT),
        cost_estimate=lasting(3.0),
        name="tail_adamw",
    )(*parts, *states)


def weight_grad_kernel(count, summed, order_ref, rows_ref, x_ref, *rest):
    out_ref, left = rest[-2:]
    tall = left.shape[0] // count

    @pl.when(pl.program_id(0) == 0)
    def _():
        for i in range(count):
            start = pl.multiple_of(order_ref[i] * tall, tall)
            left[i * tall : (i + 1) * tall, :] = rows_ref[:, pl.ds(start, tall)].T

    grad = contract(left[...], x_ref[...], 1, 1)
    if summed:
        grad = grad + rest[0][...].astype(F32)
    out_ref[...] = grad.astype(LOW)


def weight_grad(
    rows, x_t, total, wide, steps, source, target, order=None, base=None, add=None, place=None
):
    tokens, width = rows.shape
    if order is None:
        order = jnp.arange(width // TALL, dtype=jnp.int32)
    count = order.shape[0]
    out_spec = pl.BlockSpec((count * TALL, wide), lambda i, o: (0, target(i)))
    in_specs = [
        pl.BlockSpec((tokens, width), lambda i, o: (0, 0)),
        pl.BlockSpec((wide, tokens), lambda i, o: (source(i), 0)),
    ]
    args, aliases = [order, rows, x_t], {}
    if add is not None:
        in_specs.append(pl.BlockSpec((count * TALL, wide), lambda i, o: (0, place(i))))
        args.append(add)
    if base is not None:
        in_specs.append(pl.BlockSpec(memory_space=pl.ANY))
        aliases = {len(args): 0}
        args.append(base)
    return pl.pallas_call(
        functools.partial(weight_grad_kernel, count, add is not None),
        grid_spec=pltpu.PrefetchScalarGridSpec(
            num_scalar_prefetch=1,
            grid=(steps,),
            in_specs=in_specs,
            out_specs=out_spec,
            scratch_shapes=[pltpu.VMEM((count * TALL, tokens), LOW)],
        ),
        out_shape=jax.ShapeDtypeStruct((count * TALL, total), LOW),
        input_output_aliases=aliases,
        compiler_params=pltpu.CompilerParams(vmem_limit_bytes=VMEM_LIMIT),
        cost_estimate=lasting(steps * wide * count / 4800),
        name="weight_grad",
    )(*args)


def gain_kernel(gain_ref, base_ref, out_ref):
    out_ref[...] = gain_ref[...].T.astype(LOW)


def put_gains(gain_grads, base, first):
    height = base.shape[0]
    return pl.pallas_call(
        gain_kernel,
        grid=(1,),
        in_specs=[
            pl.BlockSpec((128, height), lambda i: (0, 0)),
            pl.BlockSpec(memory_space=pl.ANY),
        ],
        out_specs=pl.BlockSpec((height, 128), lambda i: (0, first)),
        out_shape=jax.ShapeDtypeStruct(base.shape, LOW),
        input_output_aliases={1: 0},
        compiler_params=pltpu.CompilerParams(vmem_limit_bytes=VMEM_LIMIT),
        cost_estimate=lasting(2.0),
        name="put_gains",
    )(jnp.pad(gain_grads, ((0, 126), (0, 0))), base)


def turned_kernel(x_ref, out_ref):
    out_ref[...] = x_ref[...].T


def turned(x):
    vmem = pl.BlockSpec(memory_space=pltpu.VMEM)
    return pl.pallas_call(
        turned_kernel,
        in_specs=[vmem],
        out_specs=vmem,
        out_shape=jax.ShapeDtypeStruct(x.shape[::-1], x.dtype),
        compiler_params=pltpu.CompilerParams(vmem_limit_bytes=VMEM_LIMIT),
        cost_estimate=lasting(1.5),
        name="turned",
    )(x)


def feed_kernel(pieces, count, *refs):
    rows_refs, grad_refs = refs[:count], refs[count : 2 * count]
    weight_ref, acts_ref, back_ref = refs[2 * count : 2 * count + 3]
    gate_v, up_v, down_v, rows_v, grad_v, sems = refs[2 * count + 3 :]
    copies = []
    for i, here in enumerate(pieces):
        copies.append(
            [
                pltpu.make_async_copy(weight_ref.at[j, :, here], held.at[:, here], sems.at[j, i])
                for j, held in enumerate((gate_v, up_v, down_v))
            ]
        )
        for copy in copies[-1]:
            copy.start()
    tokens = rows_refs[0].shape[0]
    for s in range(count):
        rows_v[s * tokens : (s + 1) * tokens, :] = rows_refs[s][...]
        grad_v[s * tokens : (s + 1) * tokens, :] = grad_refs[s][...]
    for here, (gate_copy, up_copy, down_copy) in zip(pieces, copies):
        gate_copy.wait()
        gate = jnp.dot(rows_v[...], gate_v[:, here], preferred_element_type=F32)
        up_copy.wait()
        up = jnp.dot(rows_v[...], up_v[:, here], preferred_element_type=F32)
        down_copy.wait()
        grad_hidden = jnp.dot(grad_v[...], down_v[:, here], preferred_element_type=F32)
        sigmoid = jax.nn.sigmoid(gate)
        silu = gate * sigmoid
        acts_ref[2, :, here] = (silu * up).astype(LOW)
        acts_ref[1, :, here] = (grad_hidden * silu).astype(LOW)
        acts_ref[0, :, here] = (
            grad_hidden * up * sigmoid * (1.0 + gate * (1.0 - sigmoid))
        ).astype(LOW)
    width = rows_v.shape[1]
    tall = 1024
    for lo in range(0, width, tall):
        some = slice(lo, lo + tall)
        back_ref[:, some] = (
            contract(acts_ref[0], gate_v[some, :], 1, 1)
            + contract(acts_ref[1], up_v[some, :], 1, 1)
        ).astype(LOW)


def feed(rows, grads, weight):
    count = len(rows)
    tokens, width = rows[0].shape
    units = weight.shape[2]
    half = units // 256 * 128 + 128
    pieces = [slice(0, half), slice(half, units)] if units % 128 == 0 else [slice(0, units)]
    vmem = pl.BlockSpec(memory_space=pltpu.VMEM)
    anywhere = pl.BlockSpec(memory_space=pl.ANY)
    total = count * tokens
    return pl.pallas_call(
        functools.partial(feed_kernel, pieces, count),
        in_specs=[vmem] * (2 * count) + [anywhere],
        out_specs=[vmem, vmem],
        out_shape=[
            jax.ShapeDtypeStruct((3, total, units), LOW),
            jax.ShapeDtypeStruct((total, width), LOW),
        ],
        scratch_shapes=[
            pltpu.VMEM((width, units), LOW),
            pltpu.VMEM((width, units), LOW),
            pltpu.VMEM((width, units), LOW),
            pltpu.VMEM((total, width), LOW),
            pltpu.VMEM((total, width), LOW),
            pltpu.SemaphoreType.DMA((3, len(pieces))),
        ],
        compiler_params=pltpu.CompilerParams(vmem_limit_bytes=VMEM_LIMIT),
        cost_estimate=lasting(1.0),
        name="feed",
    )(*rows, *grads, weight)


def feed_grad_kernel(halves, n, *refs):
    acts, rows = refs[:halves], refs[halves : halves + n]
    out_ref, left, right = refs[-3:]
    tokens = rows[0].shape[1]

    @pl.when(pl.program_id(1) == 0)
    def _():
        at = 0
        for act in acts:
            right[at : at + act.shape[1], :] = act[0]
            at += act.shape[1]

    for s in range(n):
        left[:, s * tokens : (s + 1) * tokens] = rows[s][...]
    out_ref[0] = jnp.dot(left[...], right[...], preferred_element_type=F32).astype(LOW)


def feed_grad(acts, rows_t, first, parts, base=None):
    n, halves = len(rows_t), len(acts)
    width, tokens = rows_t[0].shape
    units = acts[0].shape[2]
    tall = 1024
    in_specs = [
        pl.BlockSpec((1, act.shape[1], units), lambda p, r: (first + p, 0, 0)) for act in acts
    ]
    in_specs += [pl.BlockSpec((tall, tokens), lambda p, r: (r, 0))] * n
    args, aliases = list(acts) + list(rows_t), {}
    if base is not None:
        in_specs.append(pl.BlockSpec(memory_space=pl.ANY))
        aliases = {len(args): 0}
        args.append(base)
    return pl.pallas_call(
        functools.partial(feed_grad_kernel, halves, n),
        grid=(parts, width // tall),
        in_specs=in_specs,
        out_specs=pl.BlockSpec((1, tall, units), lambda p, r: (first + p, r, 0)),
        out_shape=jax.ShapeDtypeStruct((3, width, units), LOW),
        scratch_shapes=[
            pltpu.VMEM((tall, n * tokens), LOW),
            pltpu.VMEM((n * tokens, units), LOW),
        ],
        input_output_aliases=aliases,
        compiler_params=pltpu.CompilerParams(vmem_limit_bytes=VMEM_LIMIT),
        cost_estimate=lasting(1.0),
        name="feed_grad",
    )(*args)


def adamw_turned_kernel(rate, weight, first, second, grad, first_out, second_out, weight_out):
    first_out[...], second_out[...], weight_out[...] = adamw(
        weight[...], first[...], second[...], grad[...].astype(F32).T, rate, DECAY
    )


def adamw_turned(weight, first, second, grad, rate):
    rows, cols = weight.shape
    tall = 128 if rows % 128 == 0 else rows
    block = pl.BlockSpec((tall, cols), lambda i: (i, 0))
    return tuple(
        pl.pallas_call(
            functools.partial(adamw_turned_kernel, rate),
            grid=(rows // tall,),
            in_specs=[block] * 3 + [pl.BlockSpec((cols, tall), lambda i: (0, i))],
            out_specs=[block] * 3,
            out_shape=[jax.ShapeDtypeStruct(weight.shape, F32)] * 3,
            compiler_params=pltpu.CompilerParams(vmem_limit_bytes=VMEM_LIMIT),
            cost_estimate=pl.CostEstimate(
                flops=12 * rows * cols, bytes_accessed=28 * rows * cols, transcendentals=0
            ),
            name="adamw_turned",
        )(weight, first, second, grad)
    )


def on_device(
    sizes,
    tokens,
    positions,
    cotangent,
    query_weight,
    query_first,
    query_second,
    keyval_weight,
    keyval_first,
    keyval_second,
    output_weight,
    output_first,
    output_second,
    gateup_weight,
    gateup_first,
    gateup_second,
    down_weight,
    down_first,
    down_second,
    gains,
    gains_first,
    gains_second,
):
    n = sizes["tensor"]
    rank = lax.axis_index("tensor")
    offsets = ring_offsets(n)
    chunk_ids = [(rank + off + n) % n for off in offsets]
    rows, width = tokens.shape
    piece = keyval_weight.shape[1]
    block, cols = query_weight.shape

    keyval_piece = jnp.concatenate(
        [
            keyval_weight[0].astype(LOW),
            keyval_weight[1].astype(LOW),
            jnp.pad(gains.T.astype(LOW), ((0, 0), (0, 126))),
        ],
        1,
    )
    keyval_slots = ring_gather(keyval_piece, n)
    query_slots = ring_gather(query_weight.astype(LOW), n)
    keyval_rows = jnp.zeros((n, piece, keyval_piece.shape[1]), LOW)
    for chunk, held in zip(chunk_ids, keyval_slots):
        keyval_rows = lax.dynamic_update_slice(keyval_rows, held[None], (chunk, 0, 0))
    keyval_rows = keyval_rows.reshape(n * piece, -1)
    attn_in = jnp.concatenate(query_slots + [keyval_rows], 1)
    feed_in = jnp.concatenate(
        [gateup_weight.astype(LOW), down_weight.T.astype(LOW)[None]], 0
    )
    attn_in, feed_in = after(attn_in, feed_in)
    attn_low = lax.all_gather(attn_in, "dp", axis=0, tiled=True)
    output_piece, _ = after(output_weight.T.astype(LOW), (query_slots, keyval_slots))
    output_slots = ring_gather(output_piece, n)
    grad_start, _ = after(cotangent, output_slots)
    grad_slots = ring_gather(grad_start, n, 1)
    feed_in, _ = after(feed_in, output_slots)
    feed_low = lax.all_gather(feed_in, "dp", axis=1, tiled=True)
    out_halves = dp_spread(
        jnp.concatenate(output_slots, 1), sizes["dp"], (attn_low, grad_slots)
    )
    out_order = jnp.concatenate([dp_order(sizes["dp"], block, odd) for odd in (0, 1)])

    span = H * HD + 2 * KVD
    own_positions = lax.dynamic_slice_in_dim(positions, rank * rows, rows, 0)
    freqs = 10000.0 ** (-jnp.arange(0, HD, 2, dtype=F32) / HD)
    angles = freqs[:, None] * own_positions.astype(F32)[None, :]
    cosine, sine = lax.optimization_barrier((jnp.cos(angles), jnp.sin(angles)))
    x = tokens.astype(F32)
    kv_t, first_normalized, gain_rows, first_inverse = begin(tokens, attn_low, cosine, sine)
    first_gain, second_gain = gain_rows[:1], gain_rows[1:2]
    q_t = project(first_normalized, attn_low, cosine, sine)
    kv_slots = jnp.stack(ring_gather(kv_t, n))
    grad_slots, kv_slots = after(grad_slots, kv_slots)
    grad_slots = ring_gather(grad_start, n, n, grad_slots)
    per_block = H // n
    meta = jnp.stack(
        [c * rows for c in chunk_ids]
        + [(c * per_block) // GROUP for c in chunk_ids]
        + [rank * rows]
    ).astype(jnp.int32)
    meta = jnp.concatenate([meta, out_order])
    pos_row = own_positions[None, :]
    mixed_t, mixed, lse = attend(meta, pos_row, q_t, kv_slots, n)
    out_halves, _ = after(out_halves, (mixed, grad_slots))
    out_pieces = out_halves + [swap(held, sizes["dp"], 1) for held in out_halves]
    residual, second_normalized, second_inverse = mix(
        out_order, mixed, tokens, second_gain, out_pieces
    )
    second_normalized, grad_slots = after(second_normalized, grad_slots)

    rows_slots = ring_gather(second_normalized, n, 1)
    grads_t = [turned(x) for x in grad_slots]
    groups = [[s for s in range(n) if abs(offsets[s]) == k] for k in range(n // 2 + 1)]
    order = sum(groups, [])
    rows_t, acts, part_slots, last = [None] * n, [], [None] * n, [grads_t]
    for k, group in enumerate(groups):
        if k == 2:
            rows_slots = ring_gather(second_normalized, n, n, rows_slots)
        chunks, _ = after([rows_slots[s] for s in group], last)
        for i, s in enumerate(group):
            rows_t[s] = turned(chunks[i])
        if k + 1 < len(groups):
            chunks, _ = after(chunks, [rows_t[s] for s in group])
        act, part = feed(chunks, [grad_slots[s] for s in group], feed_low)
        acts.append(act)
        last = part
        for i, s in enumerate(group):
            part_slots[s] = part[i * rows : (i + 1) * rows]
        if k == 0:
            for s in groups[1]:
                rows_slots[s], _ = after(rows_slots[s], part)
    acts, _ = after(acts, last)
    grad_mlp = feed_grad(acts, [rows_t[s] for s in order], 0, 2)
    from_left = ring_way(part_slots, n, 1)
    from_right = ring_way(part_slots, n, -1, None, grad_mlp[0, :8, :128])
    grad_mlp = feed_grad(acts, [grads_t[s] for s in order], 2, 1, grad_mlp)
    second_grad = ring_sum(part_slots[0], from_left, from_right)
    mlp_parts = [contract(act[2], feed_low[2], 1, 1).astype(LOW) for act in acts]
    second_grad, (_, mlp_parts) = after(second_grad, (grad_mlp, mlp_parts))
    owned_mlp = lax.psum_scatter(grad_mlp, "dp", scatter_dimension=1, tiled=True)

    second_unit = residual * second_inverse
    residual_grad = cotangent.astype(F32) + norm_backward(
        second_grad, second_unit, second_inverse, second_gain
    )
    second_gain_grad = jnp.sum(second_grad * second_unit, 0)
    back = residual_grad.astype(LOW)
    mlp_slots = [None] * n
    for group, part in zip(groups, mlp_parts):
        for i, s in enumerate(group):
            mlp_slots[s] = part[i * rows : (i + 1) * rows]
    block_far, block_left = ring_most(mlp_slots, n), ring_way(mlp_slots, n, 1)
    grad_q_t, grad_kv = attend_back(
        meta, pos_row, q_t, kv_slots, back, out_pieces, mixed_t, lse, cosine, sine, n
    )
    (grad_q_t, grad_kv), _ = after((grad_q_t, grad_kv), (block_far, block_left))

    places = [dp_order(sizes["dp"], block, odd) for odd in (0, 1)]
    partner = swap(
        weight_grad(
            first_normalized, grad_q_t, n * cols, cols, n, lambda i: i, lambda i: i, places[1]
        ),
        sizes["dp"],
        1,
    )
    kv_parts = [grad_kv[s] for s in range(n)]
    own_kv = ring_scatter(kv_parts, n)
    out_rows, _ = after(back, grad_q_t)
    held_cols, heads_cols = attn_low.shape[1], H * HD // (2 * KVD)
    grad_pack = weight_grad(
        out_rows, mixed_t, held_cols, 2 * KVD, heads_cols, lambda i: i, lambda i: i
    )
    own_kv, _ = after(own_kv, partner)
    grad_k = own_kv[:KVD].reshape(KVH, 2, HD // 2, rows)
    upper, lower = grad_k[:, 0], grad_k[:, 1]
    grad_k = jnp.stack([upper * cosine + lower * sine, lower * cosine - upper * sine], 1)
    grad_kv_t = jnp.concatenate(
        [grad_k.reshape(KVD, rows).astype(LOW), own_kv[KVD:].astype(LOW)], 0
    )
    grad_pack = weight_grad(
        first_normalized, grad_kv_t, held_cols, 2 * KVD, 1, lambda i: 0, lambda i: heads_cols,
        None, grad_pack,
    )
    grad_qkv_t = jnp.concatenate(
        [grad_q_t, grad_kv_t, jnp.zeros((held_cols - span, rows), LOW)], 0
    )
    first_grad = contract(grad_qkv_t, attn_low, 0, 1)
    first_unit = x * first_inverse
    first_gain_grad = jnp.sum(first_grad * first_unit, 0)
    grad_pack = put_gains(
        jnp.stack([first_gain_grad, second_gain_grad]), grad_pack, span // 128
    )
    grad_pack, owned_mlp = after(grad_pack, owned_mlp)
    owned_pack = lax.psum_scatter(grad_pack, "dp", scatter_dimension=0, tiled=True)
    layer_input_gradient = residual_grad + norm_backward(
        first_grad, first_unit, first_inverse, first_gain
    )

    query_slots, last = [None] * n, grad_pack
    for s in order[::-1]:
        query_rows, _ = after(first_normalized, last)
        last = query_slots[s] = weight_grad(
            query_rows, grad_q_t, cols, cols, 1, lambda i, s=s: s, lambda i: 0, places[0], None,
            partner, lambda i, s=s: s,
        )
    query_far, query_left = ring_most(query_slots, n), ring_way(query_slots, n, 1)
    query_right = ring_last(query_slots, n, query_far)
    query_sum = ring_sum(query_slots[0], query_left, query_right).astype(LOW)
    block_right = ring_last(mlp_slots, n, block_far, query_right)
    block_out = residual + ring_sum(mlp_slots[0], block_left, block_right)

    owned_gateup, owned_down = owned_mlp[:2], owned_mlp[2]
    gateup_up = adamw(
        gateup_weight, gateup_first, gateup_second, owned_gateup.astype(F32), RATE_GATEUP, DECAY
    )
    down_up = adamw_turned(down_weight, down_first, down_second, owned_down, RATE_DOWN)
    own_query = dp_scatter(query_sum, sizes["dp"], (gateup_up, down_up)).astype(F32)
    query_up = adamw(query_weight, query_first, query_second, own_query, RATE_QUERY, DECAY)

    slots = tail_pack(jnp.stack(chunk_ids).astype(jnp.int32), owned_pack, piece, cols)
    parts = [slots[0], ring_way(slots, n, -1), ring_way(slots, n, 1)]
    states = [output_weight, output_first, output_second, keyval_weight, keyval_first]
    states += [keyval_second, gains, gains_first, gains_second]
    parts = [part for part in parts if part is not None]
    last = tail_adamw(parts, states, block, piece)
    output_up, keyval_up, gains_up = tuple(last[:3]), tuple(last[3:6]), tuple(last[6:])
    return (
        (block_out, layer_input_gradient)
        + query_up
        + keyval_up
        + output_up
        + gateup_up
        + down_up
        + gains_up
    )


def solution(mesh):
    rows = P(("dp", "tensor"), None)
    grid = P("dp", "tensor")
    cross = P("tensor", "dp")
    pair = P(None, ("dp", "tensor"), None)
    stacked = P(None, "dp", "tensor")
    narrow = P(None, ("dp", "tensor"))
    states = (grid,) * 3 + (pair,) * 3 + (cross,) * 3 + (stacked,) * 3 + (cross,) * 3 + (narrow,) * 3
    return jax.shard_map(
        functools.partial(on_device, dict(mesh.shape)),
        mesh=mesh,
        in_specs=(rows, P("dp"), rows) + states,
        out_specs=(rows, rows) + states,
        check_vma=False,
    )
```

```python
import functools

import jax
import jax.numpy as jnp
from jax import lax
from jax.experimental import pallas as pl
from jax.experimental.pallas import tpu as pltpu
from jax.sharding import PartitionSpec as P

H = 32
KVH = 4
HD = 64
GROUP = 8
KVD = KVH * HD
STEP = 10
EPS = 1e-05
BETA_ONE = 0.9
BETA_TWO = 0.999
ADAM_EPS = 1e-08
DECAY = 0.1
RATE_QUERY = 0.06
RATE_KEYVAL = 0.06
RATE_OUTPUT = 0.5
RATE_GATEUP = 0.06
RATE_DOWN = 0.04
RATE_GAINS = 1.5
LOW = jnp.bfloat16
F32 = jnp.float32
TALL = 128
VMEM_LIMIT = 56 * 1024 * 1024
LONG = pl.CostEstimate(flops=2 * 10**14, bytes_accessed=10**6, transcendentals=0)


def lasting(us):
    return pl.CostEstimate(flops=int(us * 1.15e9), bytes_accessed=10**6, transcendentals=0)


def contract(left, right, dim_left, dim_right):
    return lax.dot_general(
        left, right, (((dim_left,), (dim_right,)), ((), ())), preferred_element_type=F32
    )


def ring_offsets(n):
    return [0] + [-k for k in range(1, n // 2 + 1)] + [k for k in range(1, (n - 1) // 2 + 1)]


def shift(x, n, by):
    return lax.ppermute(x, "tensor", [(i, (i + by) % n) for i in range(n)])


def ring_gather(x, n, steps=None, known=None):
    slots, used = [x], 1
    for by, hops in ((1, n // 2), (-1, (n - 1) // 2)):
        held = x
        for hop in range(hops):
            if steps is not None and hop >= steps:
                slots.append(None)
                continue
            if known is not None and known[used + hop] is not None:
                held = known[used + hop]
            else:
                held = shift(held, n, by)
            slots.append(held)
        used += hops
    return slots


def after(late, early):
    return lax.optimization_barrier((late, early))


def ring_way(slots, n, by, passed=None, hold=None):
    first, hops = (1, n // 2) if by < 0 else (1 + n // 2, (n - 1) // 2)
    held = None
    for k in range(hops, 0, -1):
        part = slots[first + k - 1]
        if held is not None:
            part = (part.astype(F32) + held.astype(F32)).astype(LOW)
            if hold is not None and k == 1:
                part, _ = after(part, hold)
            if passed is not None:
                passed.append(part)
        held = shift(part.astype(LOW), n, by)
    return held


def ring_most(slots, n):
    held = None
    for k in range(n // 2, 1, -1):
        part = slots[k] if held is None else ring_sum(slots[k], held)
        held = shift(part.astype(LOW), n, -1)
    return held


def ring_last(slots, n, held, hold=None):
    part = (slots[1] if held is None else ring_sum(slots[1], held)).astype(LOW)
    if hold is not None:
        part, _ = after(part, hold)
    return shift(part, n, -1)


def ring_sum(own, *arrived):
    total = own.astype(F32)
    for held in arrived:
        if held is not None:
            total = total + held.astype(F32)
    return total


def ring_scatter(slots, n):
    return ring_sum(slots[0], ring_way(slots, n, -1), ring_way(slots, n, 1))


def swap(x, size, bit):
    return lax.ppermute(x, "dp", [(i, i ^ bit) for i in range(size)])


def dp_plan(size, block):
    bits = [1 << i for i in range(1, size.bit_length() - 1)]
    return [bits, bits[::-1]] if block >= 256 else [bits]


def dp_order(size, block, odd):
    plan = dp_plan(size, block)
    me = lax.axis_index("dp")
    places = []
    for h, bits in enumerate(plan):
        partners = [odd]
        for bit in bits:
            partners += [p | bit for p in partners]
        places += [(me ^ p) * len(plan) + h for p in partners]
    return jnp.stack(places).astype(jnp.int32)


def dp_spread(x, size, hold):
    block = x.shape[0]
    plan = dp_plan(size, block)
    tall = block // len(plan)
    even = [x[h * tall : (h + 1) * tall] for h in range(len(plan))]
    for i in range(len(plan[0])):
        got = [swap(held, size, bits[i]) for held, bits in zip(even, plan)]
        even = [jnp.concatenate(pair, 0) for pair in zip(even, got)]
        if i == 0:
            even, _ = after(even, hold)
    return even


def dp_scatter(held, size, hold):
    plan = dp_plan(size, 2 * held.shape[0] // size)
    tall = held.shape[0] // len(plan)
    parts = [held[h * tall : (h + 1) * tall] for h in range(len(plan))]
    for i in reversed(range(len(plan[0]))):
        half = parts[0].shape[0] // 2
        got = [swap(part[half:], size, bits[i]) for part, bits in zip(parts, plan)]
        if i == len(plan[0]) - 1:
            got, _ = after(got, hold)
        parts = [ring_sum(part[:half], new).astype(LOW) for part, new in zip(parts, got)]
    return jnp.concatenate(parts, 0)


def norm_statistics(rows_in):
    inverse = lax.rsqrt(jnp.mean(rows_in * rows_in, -1, keepdims=True) + EPS)
    return rows_in * inverse, inverse


def norm_backward(grad, unit, inverse, gain):
    scaled = grad * gain
    return inverse * (scaled - unit * jnp.mean(scaled * unit, -1, keepdims=True))


def adamw(weight, first, second, grad, rate, decay):
    first_new = BETA_ONE * first + (1.0 - BETA_ONE) * grad
    second_new = BETA_TWO * second + (1.0 - BETA_TWO) * grad * grad
    fix_one = 1.0 - BETA_ONE**STEP
    fix_two = 1.0 - BETA_TWO**STEP
    direction = first_new / fix_one / (jnp.sqrt(second_new / fix_two) + ADAM_EPS)
    return first_new, second_new, weight - rate * (direction + decay * weight)


def turn(values, cosine, sine):
    upper, lower = values[: HD // 2], values[HD // 2 :]
    return jnp.concatenate([upper * cosine - lower * sine, lower * cosine + upper * sine], 0)


def first_pack_kernel(cols, query_ref, keyval_ref, gains_ref, out_ref):
    block, piece = query_ref.shape[0], keyval_ref.shape[1]
    out_ref[block:, :] = jnp.zeros((out_ref.shape[0] - block, cols), LOW)
    out_ref[:block, :] = query_ref[...].astype(LOW)
    row = block
    for lo in range(0, 2 * KVD, cols):
        for j in range(0, cols, KVD):
            at = (lo + j) // KVD
            out_ref[row : row + piece, j : j + KVD] = keyval_ref[at].astype(LOW)
        row += piece
    out_ref[row : row + 2, :piece] = gains_ref[...].astype(LOW)


def first_pack(query, keyval, gains):
    block, cols = query.shape
    piece = keyval.shape[1]
    vmem = pl.BlockSpec(memory_space=pltpu.VMEM)
    height = block + piece * (2 * KVD // cols) + 16
    return pl.pallas_call(
        functools.partial(first_pack_kernel, cols),
        in_specs=[vmem] * 3,
        out_specs=vmem,
        out_shape=jax.ShapeDtypeStruct((height, cols), LOW),
        compiler_params=pltpu.CompilerParams(vmem_limit_bytes=VMEM_LIMIT),
        cost_estimate=lasting(2.0),
        name="first_pack",
    )(query, keyval, gains)


def first_join_kernel(n, piece, ids_ref, *refs):
    slots, out_ref = refs[:n], refs[n]
    block, cols = out_ref.shape[0], slots[0].shape[1]
    span = n * cols + 2 * KVD
    out_ref[:, span:] = jnp.zeros((block, out_ref.shape[1] - span), LOW)
    for s, slot in enumerate(slots):
        at = pl.multiple_of(ids_ref[s] * piece, piece)
        out_ref[:, s * cols : (s + 1) * cols] = slot[:block, :]
        row = block
        for lo in range(n * cols, span, cols):
            out_ref[pl.ds(at, piece), lo : lo + cols] = slot[row : row + piece, :]
            row += piece
        gains = slot[row : row + 16, :128].astype(F32).T.astype(LOW)
        out_ref[pl.ds(at, piece), span : span + 16] = gains[:piece]


def first_join(ids, slots, block, piece):
    n = len(slots)
    cols = slots[0].shape[1]
    width = n * cols + 2 * KVD + 128
    return pl.pallas_call(
        functools.partial(first_join_kernel, n, piece),
        grid_spec=pltpu.PrefetchScalarGridSpec(
            num_scalar_prefetch=1,
            grid=(1,),
            in_specs=[pl.BlockSpec(slots[0].shape, lambda i, o: (0, 0))] * n,
            out_specs=pl.BlockSpec((block, width), lambda i, o: (0, 0)),
        ),
        out_shape=jax.ShapeDtypeStruct((block, width), LOW),
        compiler_params=pltpu.CompilerParams(vmem_limit_bytes=VMEM_LIMIT),
        cost_estimate=lasting(2.0),
        name="first_join",
    )(ids, *slots)


def begin_kernel(
    x_ref, gain_ref, weight_ref, cos_ref, sin_ref, out_ref, rows_ref, gains_ref, inverse_ref
):
    gains = gain_ref[...].astype(F32).T[: gains_ref.shape[0]]
    unit, inverse = norm_statistics(x_ref[...].astype(F32))
    rows = (unit * gains[:1]).astype(LOW)
    rows_ref[...], gains_ref[...], inverse_ref[...] = rows, gains, inverse
    wide = jnp.dot(rows, weight_ref[...], preferred_element_type=F32).T
    cosine, sine = cos_ref[...], sin_ref[...]
    for h in range(KVH):
        here = slice(h * HD, (h + 1) * HD)
        out_ref[here, :] = turn(wide[here], cosine, sine).astype(LOW)
    out_ref[KVD:, :] = wide[KVD:].astype(LOW)


def begin(x, weight, cosine, sine):
    tokens, width = x.shape
    cols = 2 * KVD
    return pl.pallas_call(
        begin_kernel,
        grid=(1,),
        in_specs=[
            pl.BlockSpec((tokens, width), lambda b: (0, 0)),
            pl.BlockSpec((width, TALL), lambda b: (0, (H * HD + cols) // TALL)),
            pl.BlockSpec((width, cols), lambda b: (0, H * HD // cols)),
            pl.BlockSpec(cosine.shape, lambda b: (0, 0)),
            pl.BlockSpec(sine.shape, lambda b: (0, 0)),
        ],
        out_specs=[
            pl.BlockSpec((cols, tokens), lambda b: (0, 0)),
            pl.BlockSpec((tokens, width), lambda b: (0, 0)),
            pl.BlockSpec((8, width), lambda b: (0, 0)),
            pl.BlockSpec((tokens, 1), lambda b: (0, 0)),
        ],
        out_shape=[
            jax.ShapeDtypeStruct((cols, tokens), LOW),
            jax.ShapeDtypeStruct((tokens, width), LOW),
            jax.ShapeDtypeStruct((8, width), F32),
            jax.ShapeDtypeStruct((tokens, 1), F32),
        ],
        compiler_params=pltpu.CompilerParams(vmem_limit_bytes=VMEM_LIMIT),
        cost_estimate=lasting(5.0),
        name="begin",
    )(x, weight, weight, cosine, sine)


def project_kernel(rows_ref, weight_ref, cos_ref, sin_ref, out_ref):
    wide = jnp.dot(rows_ref[...], weight_ref[...], preferred_element_type=F32).T
    cosine, sine = cos_ref[...], sin_ref[...]
    for h in range(wide.shape[0] // HD):
        here = slice(h * HD, (h + 1) * HD)
        out_ref[here, :] = (turn(wide[here], cosine, sine) * HD ** (-0.5)).astype(LOW)


def project(rows, weight, cosine, sine):
    tokens, width = rows.shape
    cols = 2 * KVD
    blocks = H * HD // cols
    return pl.pallas_call(
        project_kernel,
        grid=(blocks,),
        in_specs=[
            pl.BlockSpec((tokens, width), lambda b: (0, 0)),
            pl.BlockSpec((width, cols), lambda b: (0, b)),
            pl.BlockSpec(cosine.shape, lambda b: (0, 0)),
            pl.BlockSpec(sine.shape, lambda b: (0, 0)),
        ],
        out_specs=pl.BlockSpec((cols, tokens), lambda b: (b, 0)),
        out_shape=jax.ShapeDtypeStruct((blocks * cols, tokens), LOW),
        compiler_params=pltpu.CompilerParams(vmem_limit_bytes=VMEM_LIMIT),
        cost_estimate=lasting(8.0),
        name="project",
    )(rows, weight, cosine, sine)


def fill_bias(meta_ref, pos_ref, bias_ref, slots, tokens):
    query = meta_ref[2 * slots] + lax.broadcasted_iota(jnp.int32, (tokens, tokens), 1)
    least = query - pos_ref[...]
    row = lax.broadcasted_iota(jnp.int32, (tokens, tokens), 0)
    for c in range(slots):
        key = meta_ref[c] + row
        bias_ref[c] = jnp.where((key <= query) & (key >= least), 0.0, -1e30)


def attend_kernel(
    slots, heads, meta_ref, pos_ref, q_ref, kv_ref, out_ref, rows_ref, lse_ref, bias_ref
):
    tokens = q_ref.shape[1]
    block = pl.program_id(0)

    @pl.when(block == 0)
    def _():
        fill_bias(meta_ref, pos_ref, bias_ref, slots, tokens)

    start = pl.multiple_of(meta_ref[slots + block] * HD, HD)
    keys = [kv_ref[c, pl.ds(start, HD), :].T for c in range(slots)]
    values = [kv_ref[c, pl.ds(KVD + start, HD), :] for c in range(slots)]
    for h in range(heads):
        query = q_ref[h * HD : (h + 1) * HD, :]
        scores = [
            jnp.dot(keys[c], query, preferred_element_type=F32) + bias_ref[c] for c in range(slots)
        ]
        peak = functools.reduce(jnp.maximum, [jnp.max(s, 0, keepdims=True) for s in scores])
        total = jnp.zeros_like(peak)
        mixed = jnp.zeros((HD, tokens), F32)
        for c in range(slots):
            expo = jnp.exp(scores[c] - peak)
            total = total + jnp.sum(expo, 0, keepdims=True)
            mixed = mixed + jnp.dot(values[c], expo.astype(LOW), preferred_element_type=F32)
        out_ref[h * HD : (h + 1) * HD, :] = (mixed / total).astype(LOW)
        lse_ref[0, h : h + 1, :] = peak + jnp.log(total)
    rows_ref[...] = out_ref[...].T


def attend(meta, pos_row, q_t, kv_slots, slots):
    tokens = q_t.shape[1]
    heads = H // slots
    rows = heads * HD
    return pl.pallas_call(
        functools.partial(attend_kernel, slots, heads),
        grid_spec=pltpu.PrefetchScalarGridSpec(
            num_scalar_prefetch=1,
            grid=(slots,),
            in_specs=[
                pl.BlockSpec((1, tokens), lambda b, m: (0, 0)),
                pl.BlockSpec((rows, tokens), lambda b, m: (b, 0)),
                pl.BlockSpec((slots, 2 * KVD, tokens), lambda b, m: (0, 0, 0)),
            ],
            out_specs=[
                pl.BlockSpec((rows, tokens), lambda b, m: (b, 0)),
                pl.BlockSpec((tokens, rows), lambda b, m: (0, b)),
                pl.BlockSpec((1, heads, tokens), lambda b, m: (b, 0, 0)),
            ],
            scratch_shapes=[pltpu.VMEM((slots, tokens, tokens), F32)],
        ),
        out_shape=[
            jax.ShapeDtypeStruct((H * HD, tokens), LOW),
            jax.ShapeDtypeStruct((tokens, H * HD), LOW),
            jax.ShapeDtypeStruct((slots, heads, tokens), F32),
        ],
        compiler_params=pltpu.CompilerParams(vmem_limit_bytes=VMEM_LIMIT),
        cost_estimate=pl.CostEstimate(
            flops=16 * H * HD * tokens * tokens * slots,
            bytes_accessed=4 * H * HD * tokens,
            transcendentals=H * tokens * tokens * slots,
        ),
        name="attend",
    )(meta, pos_row, q_t, kv_slots)


def attend_back_kernel(slots, heads, count, meta_ref, pos_ref, q_ref, kv_ref, back_ref, *refs):
    weights, refs = refs[:count], refs[count:]
    o_ref, lse_ref, cos_ref, sin_ref, dq_ref, dkv_out_ref = refs[:6]
    bias_ref, dkv_ref, do_ref, moved_ref = refs[6:]
    tokens = q_ref.shape[1]
    block = pl.program_id(0)

    @pl.when(block == 0)
    def _():
        fill_bias(meta_ref, pos_ref, bias_ref, slots, tokens)
        dkv_ref[...] = jnp.zeros_like(dkv_ref)
        for i in range(back_ref.shape[1] // TALL):
            at = pl.multiple_of(meta_ref[2 * slots + 1 + i] * TALL, TALL)
            moved_ref[:, i * TALL : (i + 1) * TALL] = back_ref[:, pl.ds(at, TALL)]

    grad_mixed, at = 0.0, 0
    for weight in weights:
        here = slice(at, at + weight.shape[0])
        grad_mixed += jnp.dot(moved_ref[:, here], weight[...], preferred_element_type=F32)
        at += weight.shape[0]
    do_ref[...] = grad_mixed.T.astype(LOW)
    start = pl.multiple_of(meta_ref[slots + block] * HD, HD)
    keys_t = [kv_ref[c, pl.ds(start, HD), :] for c in range(slots)]
    keys = [k.T for k in keys_t]
    values = [kv_ref[c, pl.ds(KVD + start, HD), :].T for c in range(slots)]
    cosine, sine = cos_ref[...], -sin_ref[...]
    grad_keys = [jnp.zeros((HD, tokens), F32) for _ in range(slots)]
    grad_values = [jnp.zeros((HD, tokens), F32) for _ in range(slots)]
    for h in range(heads):
        here = slice(h * HD, (h + 1) * HD)
        query, grad = q_ref[here, :], do_ref[here, :]
        delta = jnp.sum(grad.astype(F32) * o_ref[here, :].astype(F32), 0, keepdims=True)
        log_total = lse_ref[0, h : h + 1, :]
        grad_query = jnp.zeros((HD, tokens), F32)
        for c in range(slots):
            scores = jnp.dot(keys[c], query, preferred_element_type=F32) + bias_ref[c]
            prob = jnp.exp(scores - log_total)
            grad_prob = jnp.dot(values[c], grad, preferred_element_type=F32)
            grad_score = (prob * (grad_prob - delta)).astype(LOW)
            grad_values[c] = grad_values[c] + contract(grad, prob.astype(LOW), 1, 1)
            grad_keys[c] = grad_keys[c] + contract(query, grad_score, 1, 1)
            grad_query = grad_query + jnp.dot(keys_t[c], grad_score, preferred_element_type=F32)
        dq_ref[here, :] = (turn(grad_query, cosine, sine) * HD ** (-0.5)).astype(LOW)
    for c in range(slots):
        dkv_ref[c, pl.ds(start, HD), :] += grad_keys[c]
        dkv_ref[c, pl.ds(KVD + start, HD), :] += grad_values[c]

    @pl.when(block == pl.num_programs(0) - 1)
    def _():
        dkv_out_ref[...] = dkv_ref[...].astype(LOW)


def attend_back(meta, pos_row, q_t, kv_slots, back, weights, o_t, lse, cosine, sine, slots):
    tokens = q_t.shape[1]
    heads = H // slots
    rows = heads * HD
    head_block = pl.BlockSpec((rows, tokens), lambda b, m: (b, 0))
    table = pl.BlockSpec(cosine.shape, lambda b, m: (0, 0))
    whole = pl.BlockSpec((slots, 2 * KVD, tokens), lambda b, m: (0, 0, 0))
    return pl.pallas_call(
        functools.partial(attend_back_kernel, slots, heads, len(weights)),
        grid_spec=pltpu.PrefetchScalarGridSpec(
            num_scalar_prefetch=1,
            grid=(slots,),
            in_specs=[
                pl.BlockSpec((1, tokens), lambda b, m: (0, 0)),
                head_block,
                whole,
                pl.BlockSpec(back.shape, lambda b, m: (0, 0)),
                *[pl.BlockSpec((w.shape[0], rows), lambda b, m: (0, b)) for w in weights],
                head_block,
                pl.BlockSpec((1, heads, tokens), lambda b, m: (b, 0, 0)),
                table,
                table,
            ],
            out_specs=[head_block, whole],
            scratch_shapes=[
                pltpu.VMEM((slots, tokens, tokens), F32),
                pltpu.VMEM((slots, 2 * KVD, tokens), F32),
                pltpu.VMEM((rows, tokens), LOW),
                pltpu.VMEM(back.shape, LOW),
            ],
        ),
        out_shape=[
            jax.ShapeDtypeStruct((H * HD, tokens), LOW),
            jax.ShapeDtypeStruct((slots, 2 * KVD, tokens), LOW),
        ],
        compiler_params=pltpu.CompilerParams(vmem_limit_bytes=VMEM_LIMIT),
        cost_estimate=LONG,
        name="attend_back",
    )(meta, pos_row, q_t, kv_slots, back, *weights, o_t, lse, cosine, sine)


def mix_kernel(count, order_ref, o_ref, x_ref, gain_ref, *refs):
    weights, (h_ref, n_ref, inverse_ref) = refs[:count], refs[count : count + 3]
    held, sems = refs[count + 3 : -1], refs[-1]
    copies = [
        pltpu.make_async_copy(src, dst, sems.at[i]) for i, (src, dst) in enumerate(zip(weights, held))
    ]
    for copy in copies:
        copy.start()
    at = 0
    for copy, weight in zip(copies, held):
        copy.wait()
        mixed = contract(o_ref[...], weight[...], 1, 1)
        for i in range(weight.shape[0] // TALL):
            here = pl.ds(pl.multiple_of(order_ref[at] * TALL, TALL), TALL)
            h_ref[:, here] = x_ref[:, here].astype(F32) + mixed[:, i * TALL : (i + 1) * TALL]
            at += 1
    unit, inverse = norm_statistics(h_ref[...])
    n_ref[...] = (unit * gain_ref[...]).astype(LOW)
    inverse_ref[...] = inverse


def mix(order, o, x, gain, weights):
    tokens, width = x.shape
    count = len(weights)
    full = pl.BlockSpec((tokens, width), lambda i, o: (0, 0))
    return pl.pallas_call(
        functools.partial(mix_kernel, count),
        grid_spec=pltpu.PrefetchScalarGridSpec(
            num_scalar_prefetch=1,
            grid=(1,),
            in_specs=[
                pl.BlockSpec(o.shape, lambda i, o: (0, 0)),
                full,
                pl.BlockSpec((1, width), lambda i, o: (0, 0)),
            ]
            + [pl.BlockSpec(memory_space=pl.ANY)] * count,
            out_specs=[full, full, pl.BlockSpec((tokens, 1), lambda i, o: (0, 0))],
            scratch_shapes=[pltpu.VMEM(weight.shape, LOW) for weight in weights]
            + [pltpu.SemaphoreType.DMA((count,))],
        ),
        out_shape=[
            jax.ShapeDtypeStruct((tokens, width), F32),
            jax.ShapeDtypeStruct((tokens, width), LOW),
            jax.ShapeDtypeStruct((tokens, 1), F32),
        ],
        compiler_params=pltpu.CompilerParams(vmem_limit_bytes=VMEM_LIMIT),
        cost_estimate=lasting(6.0),
        name="mix",
    )(order, o, x, gain, *weights)


def tail_pack_kernel(n, piece, cols, ids_ref, owned_ref, gain_ref, *outs):
    block, start = owned_ref.shape[0], H * HD
    span = start + 2 * KVD
    for s, out_ref in enumerate(outs):
        at = pl.multiple_of(ids_ref[s] * piece, piece)
        out_ref[:block, :] = owned_ref[:, s * cols : (s + 1) * cols]
        row = block
        for lo in range(start, span, cols):
            out_ref[row : row + piece, :] = owned_ref[pl.ds(at, piece), lo : lo + cols]
            row += piece
        gains = gain_ref[pl.ds(at, piece), :].T.astype(LOW)
        out_ref[row:, :] = jnp.zeros((16, cols), LOW)
        out_ref[row : row + 16, :piece] = gains[:16]


def tail_pack(ids, owned, gain_cols, piece, cols):
    n, block = ids.shape[0], owned.shape[0]
    height = block + piece * (2 * KVD // cols) + 16
    return pl.pallas_call(
        functools.partial(tail_pack_kernel, n, piece, cols),
        grid_spec=pltpu.PrefetchScalarGridSpec(
            num_scalar_prefetch=1,
            grid=(1,),
            in_specs=[
                pl.BlockSpec(owned.shape, lambda i, o: (0, 0)),
                pl.BlockSpec(gain_cols.shape, lambda i, o: (0, 0)),
            ],
            out_specs=[pl.BlockSpec((height, cols), lambda i, o: (0, 0))] * n,
        ),
        out_shape=[jax.ShapeDtypeStruct((height, cols), LOW)] * n,
        compiler_params=pltpu.CompilerParams(vmem_limit_bytes=VMEM_LIMIT),
        cost_estimate=lasting(2.0),
        name="tail_pack",
    )(ids, owned, gain_cols)


def tail_adamw_kernel(block, piece, parts, *refs):
    total = ring_sum(*[ref[...] for ref in refs[:parts]])
    states, outs = refs[parts : parts + 9], refs[parts + 9 :]
    groups = 2 * KVD // total.shape[1]
    keyval = [total[block + g * piece : block + (g + 1) * piece] for g in range(groups)]
    weight, first, second = states[:3]
    outs[0][...], outs[1][...], outs[2][...] = adamw(
        weight[...], first[...], second[...], total[:block].T, RATE_OUTPUT, DECAY
    )
    weight, first, second = states[3:6]
    for j in range(2):
        if groups == 1:
            grad = keyval[0][:, j * KVD : (j + 1) * KVD]
        else:
            grad = jnp.concatenate(keyval[j * groups // 2 : (j + 1) * groups // 2], 1)
        outs[3][j], outs[4][j], outs[5][j] = adamw(
            weight[j], first[j], second[j], grad, RATE_KEYVAL, DECAY
        )
    weight, first, second = states[6:]
    outs[6][...], outs[7][...], outs[8][...] = adamw(
        weight[...], first[...], second[...], total[-16:, :piece][:2], RATE_GAINS, 0.0
    )


def tail_adamw(parts, states, block, piece):
    vmem = pl.BlockSpec(memory_space=pltpu.VMEM)
    shapes = [states[3 * i].shape for i in range(3) for _ in range(3)]
    return pl.pallas_call(
        functools.partial(tail_adamw_kernel, block, piece, len(parts)),
        in_specs=[vmem] * (len(parts) + 9),
        out_specs=[vmem] * 9,
        out_shape=[jax.ShapeDtypeStruct(shape, F32) for shape in shapes],
        compiler_params=pltpu.CompilerParams(vmem_limit_bytes=VMEM_LIMIT),
        cost_estimate=lasting(3.0),
        name="tail_adamw",
    )(*parts, *states)


def weight_grad_kernel(count, summed, order_ref, rows_ref, x_ref, *rest):
    out_ref, left = rest[-2:]
    tall = left.shape[0] // count

    @pl.when(pl.program_id(0) == 0)
    def _():
        for i in range(count):
            start = pl.multiple_of(order_ref[i] * tall, tall)
            left[i * tall : (i + 1) * tall, :] = rows_ref[:, pl.ds(start, tall)].T

    grad = contract(left[...], x_ref[...], 1, 1)
    if summed:
        grad = grad + rest[0][...].astype(F32)
    out_ref[...] = grad.astype(LOW)


def weight_grad(
    rows, x_t, total, wide, steps, source, target, order=None, base=None, add=None, place=None
):
    tokens, width = rows.shape
    if order is None:
        order = jnp.arange(width // TALL, dtype=jnp.int32)
    count = order.shape[0]
    out_spec = pl.BlockSpec((count * TALL, wide), lambda i, o: (0, target(i)))
    in_specs = [
        pl.BlockSpec((tokens, width), lambda i, o: (0, 0)),
        pl.BlockSpec((wide, tokens), lambda i, o: (source(i), 0)),
    ]
    args, aliases = [order, rows, x_t], {}
    if add is not None:
        in_specs.append(pl.BlockSpec((count * TALL, wide), lambda i, o: (0, place(i))))
        args.append(add)
    if base is not None:
        in_specs.append(pl.BlockSpec(memory_space=pl.ANY))
        aliases = {len(args): 0}
        args.append(base)
    return pl.pallas_call(
        functools.partial(weight_grad_kernel, count, add is not None),
        grid_spec=pltpu.PrefetchScalarGridSpec(
            num_scalar_prefetch=1,
            grid=(steps,),
            in_specs=in_specs,
            out_specs=out_spec,
            scratch_shapes=[pltpu.VMEM((count * TALL, tokens), LOW)],
        ),
        out_shape=jax.ShapeDtypeStruct((count * TALL, total), LOW),
        input_output_aliases=aliases,
        compiler_params=pltpu.CompilerParams(vmem_limit_bytes=VMEM_LIMIT),
        cost_estimate=lasting(steps * wide * count / 4800),
        name="weight_grad",
    )(*args)


def turned_kernel(x_ref, out_ref):
    out_ref[...] = x_ref[...].T


def turned(x):
    vmem = pl.BlockSpec(memory_space=pltpu.VMEM)
    return pl.pallas_call(
        turned_kernel,
        in_specs=[vmem],
        out_specs=vmem,
        out_shape=jax.ShapeDtypeStruct(x.shape[::-1], x.dtype),
        compiler_params=pltpu.CompilerParams(vmem_limit_bytes=VMEM_LIMIT),
        cost_estimate=lasting(1.5),
        name="turned",
    )(x)


def feed_kernel(pieces, count, *refs):
    rows_refs, grad_refs = refs[:count], refs[count : 2 * count]
    weight_ref, acts_ref, back_ref = refs[2 * count : 2 * count + 3]
    gate_v, up_v, down_v, rows_v, grad_v, sems = refs[2 * count + 3 :]
    copies = []
    for i, here in enumerate(pieces):
        copies.append(
            [
                pltpu.make_async_copy(weight_ref.at[j, :, here], held.at[:, here], sems.at[j, i])
                for j, held in enumerate((gate_v, up_v, down_v))
            ]
        )
        for copy in copies[-1]:
            copy.start()
    tokens = rows_refs[0].shape[0]
    for s in range(count):
        rows_v[s * tokens : (s + 1) * tokens, :] = rows_refs[s][...]
        grad_v[s * tokens : (s + 1) * tokens, :] = grad_refs[s][...]
    for here, (gate_copy, up_copy, down_copy) in zip(pieces, copies):
        gate_copy.wait()
        gate = jnp.dot(rows_v[...], gate_v[:, here], preferred_element_type=F32)
        up_copy.wait()
        up = jnp.dot(rows_v[...], up_v[:, here], preferred_element_type=F32)
        down_copy.wait()
        grad_hidden = jnp.dot(grad_v[...], down_v[:, here], preferred_element_type=F32)
        sigmoid = jax.nn.sigmoid(gate)
        silu = gate * sigmoid
        acts_ref[2, :, here] = (silu * up).astype(LOW)
        acts_ref[1, :, here] = (grad_hidden * silu).astype(LOW)
        acts_ref[0, :, here] = (
            grad_hidden * up * sigmoid * (1.0 + gate * (1.0 - sigmoid))
        ).astype(LOW)
    width = rows_v.shape[1]
    tall = 1024
    for lo in range(0, width, tall):
        some = slice(lo, lo + tall)
        back_ref[:, some] = (
            contract(acts_ref[0], gate_v[some, :], 1, 1)
            + contract(acts_ref[1], up_v[some, :], 1, 1)
        ).astype(LOW)


def feed(rows, grads, weight):
    count = len(rows)
    tokens, width = rows[0].shape
    units = weight.shape[2]
    half = units // 256 * 128 + 128
    pieces = [slice(0, half), slice(half, units)] if units % 128 == 0 else [slice(0, units)]
    vmem = pl.BlockSpec(memory_space=pltpu.VMEM)
    anywhere = pl.BlockSpec(memory_space=pl.ANY)
    total = count * tokens
    return pl.pallas_call(
        functools.partial(feed_kernel, pieces, count),
        in_specs=[vmem] * (2 * count) + [anywhere],
        out_specs=[vmem, vmem],
        out_shape=[
            jax.ShapeDtypeStruct((3, total, units), LOW),
            jax.ShapeDtypeStruct((total, width), LOW),
        ],
        scratch_shapes=[
            pltpu.VMEM((width, units), LOW),
            pltpu.VMEM((width, units), LOW),
            pltpu.VMEM((width, units), LOW),
            pltpu.VMEM((total, width), LOW),
            pltpu.VMEM((total, width), LOW),
            pltpu.SemaphoreType.DMA((3, len(pieces))),
        ],
        compiler_params=pltpu.CompilerParams(vmem_limit_bytes=VMEM_LIMIT),
        cost_estimate=lasting(1.0),
        name="feed",
    )(*rows, *grads, weight)


def feed_grad_kernel(halves, n, *refs):
    acts, rows = refs[:halves], refs[halves : halves + n]
    out_ref, left, right = refs[-3:]
    tokens = rows[0].shape[1]

    @pl.when(pl.program_id(1) == 0)
    def _():
        at = 0
        for act in acts:
            right[at : at + act.shape[1], :] = act[0]
            at += act.shape[1]

    for s in range(n):
        left[:, s * tokens : (s + 1) * tokens] = rows[s][...]
    out_ref[0] = jnp.dot(left[...], right[...], preferred_element_type=F32).astype(LOW)


def feed_grad(acts, rows_t, first, parts, base=None):
    n, halves = len(rows_t), len(acts)
    width, tokens = rows_t[0].shape
    units = acts[0].shape[2]
    tall = 1024
    in_specs = [
        pl.BlockSpec((1, act.shape[1], units), lambda p, r: (first + p, 0, 0)) for act in acts
    ]
    in_specs += [pl.BlockSpec((tall, tokens), lambda p, r: (r, 0))] * n
    args, aliases = list(acts) + list(rows_t), {}
    if base is not None:
        in_specs.append(pl.BlockSpec(memory_space=pl.ANY))
        aliases = {len(args): 0}
        args.append(base)
    return pl.pallas_call(
        functools.partial(feed_grad_kernel, halves, n),
        grid=(parts, width // tall),
        in_specs=in_specs,
        out_specs=pl.BlockSpec((1, tall, units), lambda p, r: (first + p, r, 0)),
        out_shape=jax.ShapeDtypeStruct((3, width, units), LOW),
        scratch_shapes=[
            pltpu.VMEM((tall, n * tokens), LOW),
            pltpu.VMEM((n * tokens, units), LOW),
        ],
        input_output_aliases=aliases,
        compiler_params=pltpu.CompilerParams(vmem_limit_bytes=VMEM_LIMIT),
        cost_estimate=lasting(1.0),
        name="feed_grad",
    )(*args)


def adamw_turned_kernel(rate, weight, first, second, grad, first_out, second_out, weight_out):
    first_out[...], second_out[...], weight_out[...] = adamw(
        weight[...], first[...], second[...], grad[...].astype(F32).T, rate, DECAY
    )


def adamw_turned(weight, first, second, grad, rate):
    rows, cols = weight.shape
    tall = 128 if rows % 128 == 0 else rows
    block = pl.BlockSpec((tall, cols), lambda i: (i, 0))
    return tuple(
        pl.pallas_call(
            functools.partial(adamw_turned_kernel, rate),
            grid=(rows // tall,),
            in_specs=[block] * 3 + [pl.BlockSpec((cols, tall), lambda i: (0, i))],
            out_specs=[block] * 3,
            out_shape=[jax.ShapeDtypeStruct(weight.shape, F32)] * 3,
            compiler_params=pltpu.CompilerParams(vmem_limit_bytes=VMEM_LIMIT),
            cost_estimate=pl.CostEstimate(
                flops=12 * rows * cols, bytes_accessed=28 * rows * cols, transcendentals=0
            ),
            name="adamw_turned",
        )(weight, first, second, grad)
    )


def on_device(
    sizes,
    tokens,
    positions,
    cotangent,
    query_weight,
    query_first,
    query_second,
    keyval_weight,
    keyval_first,
    keyval_second,
    output_weight,
    output_first,
    output_second,
    gateup_weight,
    gateup_first,
    gateup_second,
    down_weight,
    down_first,
    down_second,
    gains,
    gains_first,
    gains_second,
):
    n = sizes["tensor"]
    rank = lax.axis_index("tensor")
    offsets = ring_offsets(n)
    chunk_ids = [(rank + off + n) % n for off in offsets]
    rows, width = tokens.shape
    piece = keyval_weight.shape[1]
    block, cols = query_weight.shape

    ids = jnp.stack(chunk_ids).astype(jnp.int32)
    first_slots = ring_gather(first_pack(query_weight, keyval_weight, gains), n)
    attn_in = first_join(ids, first_slots, block, piece)
    feed_in = jnp.concatenate(
        [gateup_weight.astype(LOW), down_weight.T.astype(LOW)[None]], 0
    )
    attn_in, feed_in = after(attn_in, feed_in)
    attn_low = lax.all_gather(attn_in, "dp", axis=0, tiled=True)
    output_piece, _ = after(output_weight.T.astype(LOW), first_slots)
    output_slots = ring_gather(output_piece, n)
    grad_start, _ = after(cotangent, output_slots)
    grad_slots = ring_gather(grad_start, n, 1)
    feed_in, _ = after(feed_in, output_slots)
    feed_low = lax.all_gather(feed_in, "dp", axis=1, tiled=True)
    out_halves = dp_spread(
        jnp.concatenate(output_slots, 1), sizes["dp"], (attn_low, grad_slots)
    )
    out_order = jnp.concatenate([dp_order(sizes["dp"], block, odd) for odd in (0, 1)])

    span = H * HD + 2 * KVD
    own_positions = lax.dynamic_slice_in_dim(positions, rank * rows, rows, 0)
    freqs = 10000.0 ** (-jnp.arange(0, HD, 2, dtype=F32) / HD)
    angles = freqs[:, None] * own_positions.astype(F32)[None, :]
    cosine, sine = lax.optimization_barrier((jnp.cos(angles), jnp.sin(angles)))
    x = tokens.astype(F32)
    kv_t, first_normalized, gain_rows, first_inverse = begin(tokens, attn_low, cosine, sine)
    first_gain, second_gain = gain_rows[:1], gain_rows[1:2]
    q_t = project(first_normalized, attn_low, cosine, sine)
    kv_slots = jnp.stack(ring_gather(kv_t, n))
    grad_slots, kv_slots = after(grad_slots, kv_slots)
    grad_slots = ring_gather(grad_start, n, n, grad_slots)
    per_block = H // n
    meta = jnp.stack(
        [c * rows for c in chunk_ids]
        + [(c * per_block) // GROUP for c in chunk_ids]
        + [rank * rows]
    ).astype(jnp.int32)
    meta = jnp.concatenate([meta, out_order])
    pos_row = own_positions[None, :]
    mixed_t, mixed, lse = attend(meta, pos_row, q_t, kv_slots, n)
    out_halves, _ = after(out_halves, (mixed, grad_slots))
    out_pieces = out_halves + [swap(held, sizes["dp"], 1) for held in out_halves]
    residual, second_normalized, second_inverse = mix(
        out_order, mixed, tokens, second_gain, out_pieces
    )
    second_normalized, grad_slots = after(second_normalized, grad_slots)

    rows_slots = ring_gather(second_normalized, n, 1)
    grads_t = [turned(x) for x in grad_slots]
    groups = [[s for s in range(n) if abs(offsets[s]) == k] for k in range(n // 2 + 1)]
    order = sum(groups, [])
    rows_t, acts, part_slots, last = [None] * n, [], [None] * n, [grads_t]
    for k, group in enumerate(groups):
        if k == 2:
            rows_slots = ring_gather(second_normalized, n, n, rows_slots)
        chunks, _ = after([rows_slots[s] for s in group], last)
        for i, s in enumerate(group):
            rows_t[s] = turned(chunks[i])
        if k + 1 < len(groups):
            chunks, _ = after(chunks, [rows_t[s] for s in group])
        act, part = feed(chunks, [grad_slots[s] for s in group], feed_low)
        acts.append(act)
        last = part
        for i, s in enumerate(group):
            part_slots[s] = part[i * rows : (i + 1) * rows]
        if k == 0:
            for s in groups[1]:
                rows_slots[s], _ = after(rows_slots[s], part)
    acts, _ = after(acts, last)
    grad_mlp = feed_grad(acts, [rows_t[s] for s in order], 0, 2)
    from_left = ring_way(part_slots, n, 1)
    passed = []
    from_right = ring_way(part_slots, n, -1, passed, grad_mlp[0, :8, :128])
    acts, _ = after(acts, passed)
    grad_mlp = feed_grad(acts, [grads_t[s] for s in order], 2, 1, grad_mlp)
    second_grad = ring_sum(part_slots[0], from_left, from_right)
    mlp_parts = [contract(act[2], feed_low[2], 1, 1).astype(LOW) for act in acts]
    second_grad, (_, mlp_parts) = after(second_grad, (grad_mlp, mlp_parts))
    owned_mlp = lax.psum_scatter(grad_mlp, "dp", scatter_dimension=1, tiled=True)

    second_unit = residual * second_inverse
    residual_grad = cotangent.astype(F32) + norm_backward(
        second_grad, second_unit, second_inverse, second_gain
    )
    second_gain_grad = jnp.sum(second_grad * second_unit, 0)
    back = residual_grad.astype(LOW)
    mlp_slots = [None] * n
    for group, part in zip(groups, mlp_parts):
        for i, s in enumerate(group):
            mlp_slots[s] = part[i * rows : (i + 1) * rows]
    block_far, block_left = ring_most(mlp_slots, n), ring_way(mlp_slots, n, 1)
    grad_q_t, grad_kv = attend_back(
        meta, pos_row, q_t, kv_slots, back, out_pieces, mixed_t, lse, cosine, sine, n
    )
    (grad_q_t, grad_kv), _ = after((grad_q_t, grad_kv), (block_far, block_left))

    places = [dp_order(sizes["dp"], block, odd) for odd in (0, 1)]
    kv_parts = [grad_kv[s] for s in range(n)]
    kv_left, passed = ring_way(kv_parts, n, 1), []
    own_kv = ring_sum(kv_parts[0], ring_way(kv_parts, n, -1, passed), kv_left)
    query_rows, _ = after(first_normalized, (passed, kv_left))
    partner = weight_grad(
        query_rows, grad_q_t, n * cols, cols, n, lambda i: i, lambda i: i, places[1]
    )
    partner = swap(partner, sizes["dp"], 1)
    out_rows, _ = after(back, grad_q_t)
    heads_cols = H * HD // (2 * KVD)
    grad_pack = weight_grad(
        out_rows, mixed_t, span, 2 * KVD, heads_cols, lambda i: i, lambda i: i
    )
    own_kv, _ = after(own_kv, partner)
    grad_k = own_kv[:KVD].reshape(KVH, 2, HD // 2, rows)
    upper, lower = grad_k[:, 0], grad_k[:, 1]
    grad_k = jnp.stack([upper * cosine + lower * sine, lower * cosine - upper * sine], 1)
    grad_kv_t = jnp.concatenate(
        [grad_k.reshape(KVD, rows).astype(LOW), own_kv[KVD:].astype(LOW)], 0
    )
    grad_pack = weight_grad(
        first_normalized, grad_kv_t, span, 2 * KVD, 1, lambda i: 0, lambda i: heads_cols,
        None, grad_pack,
    )
    grad_pack, owned_mlp = after(grad_pack, owned_mlp)
    owned_pack = lax.psum_scatter(grad_pack, "dp", scatter_dimension=0, tiled=True)

    query_slots, last = [None] * n, grad_pack
    for s in order[::-1]:
        query_rows, _ = after(first_normalized, last)
        last = query_slots[s] = weight_grad(
            query_rows, grad_q_t, cols, cols, 1, lambda i, s=s: s, lambda i: 0, places[0], None,
            partner, lambda i, s=s: s,
        )
    query_far, query_left = ring_most(query_slots, n), ring_way(query_slots, n, 1)
    owned_gateup, owned_down = owned_mlp[:2], owned_mlp[2]
    gateup_up = adamw(
        gateup_weight, gateup_first, gateup_second, owned_gateup.astype(F32), RATE_GATEUP, DECAY
    )
    down_up = adamw_turned(down_weight, down_first, down_second, owned_down, RATE_DOWN)
    query_right = ring_last(query_slots, n, query_far, (gateup_up, down_up))
    query_sum = ring_sum(query_slots[0], query_left, query_right).astype(LOW)
    block_right = ring_last(mlp_slots, n, block_far, query_right)
    block_out = residual + ring_sum(mlp_slots[0], block_left, block_right)
    own_query = dp_scatter(query_sum, sizes["dp"], ()).astype(F32)
    query_up = adamw(query_weight, query_first, query_second, own_query, RATE_QUERY, DECAY)

    (back_q_t, back_kv_t), _ = after((grad_q_t, grad_kv_t), query_slots)
    grad_qkv_t = jnp.concatenate(
        [back_q_t, back_kv_t, jnp.zeros((attn_low.shape[1] - span, rows), LOW)], 0
    )
    first_grad = contract(grad_qkv_t, attn_low, 0, 1)
    first_unit = x * first_inverse
    first_gain_grad = jnp.sum(first_grad * first_unit, 0)
    layer_input_gradient = residual_grad + norm_backward(
        first_grad, first_unit, first_inverse, first_gain
    )
    gain_grads, bit = jnp.stack([first_gain_grad, second_gain_grad]), 1
    while bit < sizes["dp"]:
        gain_grads = gain_grads + swap(gain_grads, sizes["dp"], bit)
        bit *= 2
    gain_grads = lax.dynamic_slice_in_dim(gain_grads, lax.axis_index("dp") * block, block, 1)
    gain_cols = jnp.pad(gain_grads.T, ((0, 0), (0, 126)))

    slots = tail_pack(ids, owned_pack, gain_cols, piece, cols)
    parts = [slots[0], ring_way(slots, n, -1), ring_way(slots, n, 1)]
    states = [output_weight, output_first, output_second, keyval_weight, keyval_first]
    states += [keyval_second, gains, gains_first, gains_second]
    parts = [part for part in parts if part is not None]
    last = tail_adamw(parts, states, block, piece)
    output_up, keyval_up, gains_up = tuple(last[:3]), tuple(last[3:6]), tuple(last[6:])
    return (
        (block_out, layer_input_gradient)
        + query_up
        + keyval_up
        + output_up
        + gateup_up
        + down_up
        + gains_up
    )


def solution(mesh):
    rows = P(("dp", "tensor"), None)
    grid = P("dp", "tensor")
    cross = P("tensor", "dp")
    pair = P(None, ("dp", "tensor"), None)
    stacked = P(None, "dp", "tensor")
    narrow = P(None, ("dp", "tensor"))
    states = (grid,) * 3 + (pair,) * 3 + (cross,) * 3 + (stacked,) * 3 + (cross,) * 3 + (narrow,) * 3
    return jax.shard_map(
        functools.partial(on_device, dict(mesh.shape)),
        mesh=mesh,
        in_specs=(rows, P("dp"), rows) + states,
        out_specs=(rows, rows) + states,
        check_vma=False,
    )
```

```python
import functools

import jax
import jax.numpy as jnp
from jax import lax
from jax.experimental import pallas as pl
from jax.experimental.pallas import tpu as pltpu
from jax.sharding import PartitionSpec as P

H = 32
KVH = 4
HD = 64
GROUP = 8
KVD = KVH * HD
STEP = 10
EPS = 1e-05
BETA_ONE = 0.9
BETA_TWO = 0.999
ADAM_EPS = 1e-08
DECAY = 0.1
RATE_QUERY = 0.06
RATE_KEYVAL = 0.06
RATE_OUTPUT = 0.5
RATE_GATEUP = 0.06
RATE_DOWN = 0.04
RATE_GAINS = 1.5
LOW = jnp.bfloat16
F32 = jnp.float32
TALL = 128
VMEM_LIMIT = 56 * 1024 * 1024
LONG = pl.CostEstimate(flops=2 * 10**14, bytes_accessed=10**6, transcendentals=0)


def lasting(us):
    return pl.CostEstimate(flops=int(us * 1.15e9), bytes_accessed=10**6, transcendentals=0)


def contract(left, right, dim_left, dim_right):
    return lax.dot_general(
        left, right, (((dim_left,), (dim_right,)), ((), ())), preferred_element_type=F32
    )


def ring_offsets(n):
    return [0] + [-k for k in range(1, n // 2 + 1)] + [k for k in range(1, (n - 1) // 2 + 1)]


def shift(x, n, by):
    return lax.ppermute(x, "tensor", [(i, (i + by) % n) for i in range(n)])


def ring_gather(x, n, steps=None, known=None):
    slots, used = [x], 1
    for by, hops in ((1, n // 2), (-1, (n - 1) // 2)):
        held = x
        for hop in range(hops):
            if steps is not None and hop >= steps:
                slots.append(None)
                continue
            if known is not None and known[used + hop] is not None:
                held = known[used + hop]
            else:
                held = shift(held, n, by)
            slots.append(held)
        used += hops
    return slots


def after(late, early):
    return lax.optimization_barrier((late, early))


def ring_way(slots, n, by, passed=None, hold=None):
    first, hops = (1, n // 2) if by < 0 else (1 + n // 2, (n - 1) // 2)
    held = None
    for k in range(hops, 0, -1):
        part = slots[first + k - 1]
        if held is not None:
            part = (part.astype(F32) + held.astype(F32)).astype(LOW)
            if hold is not None and k == 1:
                part, _ = after(part, hold)
            if passed is not None:
                passed.append(part)
        held = shift(part.astype(LOW), n, by)
    return held


def ring_most(slots, n):
    held = None
    for k in range(n // 2, 1, -1):
        part = slots[k] if held is None else ring_sum(slots[k], held)
        held = shift(part.astype(LOW), n, -1)
    return held


def ring_last(slots, n, held, hold=None):
    part = (slots[1] if held is None else ring_sum(slots[1], held)).astype(LOW)
    if hold is not None:
        part, _ = after(part, hold)
    return shift(part, n, -1)


def ring_sum(own, *arrived):
    total = own.astype(F32)
    for held in arrived:
        if held is not None:
            total = total + held.astype(F32)
    return total


def ring_scatter(slots, n):
    return ring_sum(slots[0], ring_way(slots, n, -1), ring_way(slots, n, 1))


def swap(x, size, bit):
    return lax.ppermute(x, "dp", [(i, i ^ bit) for i in range(size)])


def dp_plan(size, block):
    bits = [1 << i for i in range(1, size.bit_length() - 1)]
    return [bits, bits[::-1]] if block >= 256 else [bits]


def dp_order(size, block, odd):
    plan = dp_plan(size, block)
    me = lax.axis_index("dp")
    places = []
    for h, bits in enumerate(plan):
        partners = [odd]
        for bit in bits:
            partners += [p | bit for p in partners]
        places += [(me ^ p) * len(plan) + h for p in partners]
    return jnp.stack(places).astype(jnp.int32)


def dp_spread(x, size, hold):
    block = x.shape[0]
    plan = dp_plan(size, block)
    tall = block // len(plan)
    even = [x[h * tall : (h + 1) * tall] for h in range(len(plan))]
    for i in range(len(plan[0])):
        got = [swap(held, size, bits[i]) for held, bits in zip(even, plan)]
        even = [jnp.concatenate(pair, 0) for pair in zip(even, got)]
        if i == 0:
            even, _ = after(even, hold)
    return even


def dp_scatter(held, size, hold):
    plan = dp_plan(size, 2 * held.shape[0] // size)
    tall = held.shape[0] // len(plan)
    parts = [held[h * tall : (h + 1) * tall] for h in range(len(plan))]
    for i in reversed(range(len(plan[0]))):
        half = parts[0].shape[0] // 2
        got = [swap(part[half:], size, bits[i]) for part, bits in zip(parts, plan)]
        if i == len(plan[0]) - 1:
            got, _ = after(got, hold)
        parts = [ring_sum(part[:half], new).astype(LOW) for part, new in zip(parts, got)]
    return jnp.concatenate(parts, 0)


def norm_statistics(rows_in):
    inverse = lax.rsqrt(jnp.mean(rows_in * rows_in, -1, keepdims=True) + EPS)
    return rows_in * inverse, inverse


def norm_backward(grad, unit, inverse, gain):
    scaled = grad * gain
    return inverse * (scaled - unit * jnp.mean(scaled * unit, -1, keepdims=True))


def adamw(weight, first, second, grad, rate, decay):
    first_new = BETA_ONE * first + (1.0 - BETA_ONE) * grad
    second_new = BETA_TWO * second + (1.0 - BETA_TWO) * grad * grad
    fix_one = 1.0 - BETA_ONE**STEP
    fix_two = 1.0 - BETA_TWO**STEP
    direction = first_new / fix_one / (jnp.sqrt(second_new / fix_two) + ADAM_EPS)
    return first_new, second_new, weight - rate * (direction + decay * weight)


def turn(values, cosine, sine):
    upper, lower = values[: HD // 2], values[HD // 2 :]
    return jnp.concatenate([upper * cosine - lower * sine, lower * cosine + upper * sine], 0)


def first_pack_kernel(cols, query_ref, keyval_ref, gains_ref, out_ref):
    block, piece = query_ref.shape[0], keyval_ref.shape[1]
    out_ref[block:, :] = jnp.zeros((out_ref.shape[0] - block, cols), LOW)
    out_ref[:block, :] = query_ref[...].astype(LOW)
    row = block
    for lo in range(0, 2 * KVD, cols):
        for j in range(0, cols, KVD):
            at = (lo + j) // KVD
            out_ref[row : row + piece, j : j + KVD] = keyval_ref[at].astype(LOW)
        row += piece
    out_ref[row : row + 2, :piece] = gains_ref[...].astype(LOW)


def first_pack(query, keyval, gains):
    block, cols = query.shape
    piece = keyval.shape[1]
    vmem = pl.BlockSpec(memory_space=pltpu.VMEM)
    height = block + piece * (2 * KVD // cols) + 16
    return pl.pallas_call(
        functools.partial(first_pack_kernel, cols),
        in_specs=[vmem] * 3,
        out_specs=vmem,
        out_shape=jax.ShapeDtypeStruct((height, cols), LOW),
        compiler_params=pltpu.CompilerParams(vmem_limit_bytes=VMEM_LIMIT),
        cost_estimate=lasting(2.0),
        name="first_pack",
    )(query, keyval, gains)


def first_join_kernel(n, piece, ids_ref, *refs):
    slots, out_ref = refs[:n], refs[n]
    block, cols = out_ref.shape[0], slots[0].shape[1]
    span = n * cols + 2 * KVD
    out_ref[:, span:] = jnp.zeros((block, out_ref.shape[1] - span), LOW)
    for s, slot in enumerate(slots):
        at = pl.multiple_of(ids_ref[s] * piece, piece)
        out_ref[:, s * cols : (s + 1) * cols] = slot[:block, :]
        row = block
        for lo in range(n * cols, span, cols):
            out_ref[pl.ds(at, piece), lo : lo + cols] = slot[row : row + piece, :]
            row += piece
        gains = slot[row : row + 16, :128].astype(F32).T.astype(LOW)
        out_ref[pl.ds(at, piece), span : span + 16] = gains[:piece]


def first_join(ids, slots, block, piece):
    n = len(slots)
    cols = slots[0].shape[1]
    width = n * cols + 2 * KVD + 128
    return pl.pallas_call(
        functools.partial(first_join_kernel, n, piece),
        grid_spec=pltpu.PrefetchScalarGridSpec(
            num_scalar_prefetch=1,
            grid=(1,),
            in_specs=[pl.BlockSpec(slots[0].shape, lambda i, o: (0, 0))] * n,
            out_specs=pl.BlockSpec((block, width), lambda i, o: (0, 0)),
        ),
        out_shape=jax.ShapeDtypeStruct((block, width), LOW),
        compiler_params=pltpu.CompilerParams(vmem_limit_bytes=VMEM_LIMIT),
        cost_estimate=lasting(2.0),
        name="first_join",
    )(ids, *slots)


def begin_kernel(
    x_ref, gain_ref, weight_ref, cos_ref, sin_ref, out_ref, rows_ref, gains_ref, inverse_ref
):
    gains = gain_ref[...].astype(F32).T[: gains_ref.shape[0]]
    unit, inverse = norm_statistics(x_ref[...].astype(F32))
    rows = (unit * gains[:1]).astype(LOW)
    rows_ref[...], gains_ref[...], inverse_ref[...] = rows, gains, inverse
    wide = jnp.dot(rows, weight_ref[...], preferred_element_type=F32).T
    cosine, sine = cos_ref[...], sin_ref[...]
    for h in range(KVH):
        here = slice(h * HD, (h + 1) * HD)
        out_ref[here, :] = turn(wide[here], cosine, sine).astype(LOW)
    out_ref[KVD:, :] = wide[KVD:].astype(LOW)


def begin(x, weight, cosine, sine):
    tokens, width = x.shape
    cols = 2 * KVD
    return pl.pallas_call(
        begin_kernel,
        grid=(1,),
        in_specs=[
            pl.BlockSpec((tokens, width), lambda b: (0, 0)),
            pl.BlockSpec((width, TALL), lambda b: (0, (H * HD + cols) // TALL)),
            pl.BlockSpec((width, cols), lambda b: (0, H * HD // cols)),
            pl.BlockSpec(cosine.shape, lambda b: (0, 0)),
            pl.BlockSpec(sine.shape, lambda b: (0, 0)),
        ],
        out_specs=[
            pl.BlockSpec((cols, tokens), lambda b: (0, 0)),
            pl.BlockSpec((tokens, width), lambda b: (0, 0)),
            pl.BlockSpec((8, width), lambda b: (0, 0)),
            pl.BlockSpec((tokens, 1), lambda b: (0, 0)),
        ],
        out_shape=[
            jax.ShapeDtypeStruct((cols, tokens), LOW),
            jax.ShapeDtypeStruct((tokens, width), LOW),
            jax.ShapeDtypeStruct((8, width), F32),
            jax.ShapeDtypeStruct((tokens, 1), F32),
        ],
        compiler_params=pltpu.CompilerParams(vmem_limit_bytes=VMEM_LIMIT),
        cost_estimate=lasting(5.0),
        name="begin",
    )(x, weight, weight, cosine, sine)


def project_kernel(rows_ref, weight_ref, cos_ref, sin_ref, out_ref):
    wide = jnp.dot(rows_ref[...], weight_ref[...], preferred_element_type=F32).T
    cosine, sine = cos_ref[...], sin_ref[...]
    for h in range(wide.shape[0] // HD):
        here = slice(h * HD, (h + 1) * HD)
        out_ref[here, :] = (turn(wide[here], cosine, sine) * HD ** (-0.5)).astype(LOW)


def project(rows, weight, cosine, sine):
    tokens, width = rows.shape
    cols = 2 * KVD
    blocks = H * HD // cols
    return pl.pallas_call(
        project_kernel,
        grid=(blocks,),
        in_specs=[
            pl.BlockSpec((tokens, width), lambda b: (0, 0)),
            pl.BlockSpec((width, cols), lambda b: (0, b)),
            pl.BlockSpec(cosine.shape, lambda b: (0, 0)),
            pl.BlockSpec(sine.shape, lambda b: (0, 0)),
        ],
        out_specs=pl.BlockSpec((cols, tokens), lambda b: (b, 0)),
        out_shape=jax.ShapeDtypeStruct((blocks * cols, tokens), LOW),
        compiler_params=pltpu.CompilerParams(vmem_limit_bytes=VMEM_LIMIT),
        cost_estimate=lasting(8.0),
        name="project",
    )(rows, weight, cosine, sine)


def fill_bias(meta_ref, pos_ref, bias_ref, slots, tokens):
    query = meta_ref[2 * slots] + lax.broadcasted_iota(jnp.int32, (tokens, tokens), 1)
    least = query - pos_ref[...]
    row = lax.broadcasted_iota(jnp.int32, (tokens, tokens), 0)
    for c in range(slots):
        key = meta_ref[c] + row
        bias_ref[c] = jnp.where((key <= query) & (key >= least), 0.0, -1e30)


def attend_kernel(
    slots, heads, meta_ref, pos_ref, q_ref, kv_ref, out_ref, rows_ref, lse_ref, bias_ref
):
    tokens = q_ref.shape[1]
    block = pl.program_id(0)

    @pl.when(block == 0)
    def _():
        fill_bias(meta_ref, pos_ref, bias_ref, slots, tokens)

    start = pl.multiple_of(meta_ref[slots + block] * HD, HD)
    keys = [kv_ref[c, pl.ds(start, HD), :].T for c in range(slots)]
    values = [kv_ref[c, pl.ds(KVD + start, HD), :] for c in range(slots)]
    for h in range(heads):
        query = q_ref[h * HD : (h + 1) * HD, :]
        scores = [
            jnp.dot(keys[c], query, preferred_element_type=F32) + bias_ref[c] for c in range(slots)
        ]
        peak = functools.reduce(jnp.maximum, [jnp.max(s, 0, keepdims=True) for s in scores])
        total = jnp.zeros_like(peak)
        mixed = jnp.zeros((HD, tokens), F32)
        for c in range(slots):
            expo = jnp.exp(scores[c] - peak)
            total = total + jnp.sum(expo, 0, keepdims=True)
            mixed = mixed + jnp.dot(values[c], expo.astype(LOW), preferred_element_type=F32)
        out_ref[h * HD : (h + 1) * HD, :] = (mixed / total).astype(LOW)
        lse_ref[0, h : h + 1, :] = peak + jnp.log(total)
    rows_ref[...] = out_ref[...].T


def attend(meta, pos_row, q_t, kv_slots, slots):
    tokens = q_t.shape[1]
    heads = H // slots
    rows = heads * HD
    return pl.pallas_call(
        functools.partial(attend_kernel, slots, heads),
        grid_spec=pltpu.PrefetchScalarGridSpec(
            num_scalar_prefetch=1,
            grid=(slots,),
            in_specs=[
                pl.BlockSpec((1, tokens), lambda b, m: (0, 0)),
                pl.BlockSpec((rows, tokens), lambda b, m: (b, 0)),
                pl.BlockSpec((slots, 2 * KVD, tokens), lambda b, m: (0, 0, 0)),
            ],
            out_specs=[
                pl.BlockSpec((rows, tokens), lambda b, m: (b, 0)),
                pl.BlockSpec((tokens, rows), lambda b, m: (0, b)),
                pl.BlockSpec((1, heads, tokens), lambda b, m: (b, 0, 0)),
            ],
            scratch_shapes=[pltpu.VMEM((slots, tokens, tokens), F32)],
        ),
        out_shape=[
            jax.ShapeDtypeStruct((H * HD, tokens), LOW),
            jax.ShapeDtypeStruct((tokens, H * HD), LOW),
            jax.ShapeDtypeStruct((slots, heads, tokens), F32),
        ],
        compiler_params=pltpu.CompilerParams(vmem_limit_bytes=VMEM_LIMIT),
        cost_estimate=pl.CostEstimate(
            flops=16 * H * HD * tokens * tokens * slots,
            bytes_accessed=4 * H * HD * tokens,
            transcendentals=H * tokens * tokens * slots,
        ),
        name="attend",
    )(meta, pos_row, q_t, kv_slots)


def attend_back_kernel(slots, heads, count, meta_ref, pos_ref, q_ref, kv_ref, back_ref, *refs):
    weights, refs = refs[:count], refs[count:]
    o_ref, lse_ref, cos_ref, sin_ref, dq_ref, dkv_out_ref = refs[:6]
    bias_ref, dkv_ref, do_ref, moved_ref = refs[6:]
    tokens = q_ref.shape[1]
    block = pl.program_id(0)

    @pl.when(block == 0)
    def _():
        fill_bias(meta_ref, pos_ref, bias_ref, slots, tokens)
        dkv_ref[...] = jnp.zeros_like(dkv_ref)
        for i in range(back_ref.shape[1] // TALL):
            at = pl.multiple_of(meta_ref[2 * slots + 1 + i] * TALL, TALL)
            moved_ref[:, i * TALL : (i + 1) * TALL] = back_ref[:, pl.ds(at, TALL)]

    grad_mixed, at = 0.0, 0
    for weight in weights:
        here = slice(at, at + weight.shape[0])
        grad_mixed += jnp.dot(moved_ref[:, here], weight[...], preferred_element_type=F32)
        at += weight.shape[0]
    do_ref[...] = grad_mixed.T.astype(LOW)
    start = pl.multiple_of(meta_ref[slots + block] * HD, HD)
    keys_t = [kv_ref[c, pl.ds(start, HD), :] for c in range(slots)]
    keys = [k.T for k in keys_t]
    values = [kv_ref[c, pl.ds(KVD + start, HD), :].T for c in range(slots)]
    cosine, sine = cos_ref[...], -sin_ref[...]
    grad_keys = [jnp.zeros((HD, tokens), F32) for _ in range(slots)]
    grad_values = [jnp.zeros((HD, tokens), F32) for _ in range(slots)]
    for h in range(heads):
        here = slice(h * HD, (h + 1) * HD)
        query, grad = q_ref[here, :], do_ref[here, :]
        delta = jnp.sum(grad.astype(F32) * o_ref[here, :].astype(F32), 0, keepdims=True)
        log_total = lse_ref[0, h : h + 1, :]
        grad_query = jnp.zeros((HD, tokens), F32)
        for c in range(slots):
            scores = jnp.dot(keys[c], query, preferred_element_type=F32) + bias_ref[c]
            prob = jnp.exp(scores - log_total)
            grad_prob = jnp.dot(values[c], grad, preferred_element_type=F32)
            grad_score = (prob * (grad_prob - delta)).astype(LOW)
            grad_values[c] = grad_values[c] + contract(grad, prob.astype(LOW), 1, 1)
            grad_keys[c] = grad_keys[c] + contract(query, grad_score, 1, 1)
            grad_query = grad_query + jnp.dot(keys_t[c], grad_score, preferred_element_type=F32)
        dq_ref[here, :] = (turn(grad_query, cosine, sine) * HD ** (-0.5)).astype(LOW)
    for c in range(slots):
        dkv_ref[c, pl.ds(start, HD), :] += grad_keys[c]
        dkv_ref[c, pl.ds(KVD + start, HD), :] += grad_values[c]

    @pl.when(block == pl.num_programs(0) - 1)
    def _():
        dkv_out_ref[...] = dkv_ref[...].astype(LOW)


def attend_back(meta, pos_row, q_t, kv_slots, back, weights, o_t, lse, cosine, sine, slots):
    tokens = q_t.shape[1]
    heads = H // slots
    rows = heads * HD
    head_block = pl.BlockSpec((rows, tokens), lambda b, m: (b, 0))
    table = pl.BlockSpec(cosine.shape, lambda b, m: (0, 0))
    whole = pl.BlockSpec((slots, 2 * KVD, tokens), lambda b, m: (0, 0, 0))
    return pl.pallas_call(
        functools.partial(attend_back_kernel, slots, heads, len(weights)),
        grid_spec=pltpu.PrefetchScalarGridSpec(
            num_scalar_prefetch=1,
            grid=(slots,),
            in_specs=[
                pl.BlockSpec((1, tokens), lambda b, m: (0, 0)),
                head_block,
                whole,
                pl.BlockSpec(back.shape, lambda b, m: (0, 0)),
                *[pl.BlockSpec((w.shape[0], rows), lambda b, m: (0, b)) for w in weights],
                head_block,
                pl.BlockSpec((1, heads, tokens), lambda b, m: (b, 0, 0)),
                table,
                table,
            ],
            out_specs=[head_block, whole],
            scratch_shapes=[
                pltpu.VMEM((slots, tokens, tokens), F32),
                pltpu.VMEM((slots, 2 * KVD, tokens), F32),
                pltpu.VMEM((rows, tokens), LOW),
                pltpu.VMEM(back.shape, LOW),
            ],
        ),
        out_shape=[
            jax.ShapeDtypeStruct((H * HD, tokens), LOW),
            jax.ShapeDtypeStruct((slots, 2 * KVD, tokens), LOW),
        ],
        compiler_params=pltpu.CompilerParams(vmem_limit_bytes=VMEM_LIMIT),
        cost_estimate=LONG,
        name="attend_back",
    )(meta, pos_row, q_t, kv_slots, back, *weights, o_t, lse, cosine, sine)


def mix_kernel(count, order_ref, o_ref, x_ref, gain_ref, *refs):
    weights, (h_ref, n_ref, inverse_ref) = refs[:count], refs[count : count + 3]
    held, sems = refs[count + 3 : -1], refs[-1]
    copies = [
        pltpu.make_async_copy(src, dst, sems.at[i]) for i, (src, dst) in enumerate(zip(weights, held))
    ]
    for copy in copies:
        copy.start()
    at = 0
    for copy, weight in zip(copies, held):
        copy.wait()
        mixed = contract(o_ref[...], weight[...], 1, 1)
        for i in range(weight.shape[0] // TALL):
            here = pl.ds(pl.multiple_of(order_ref[at] * TALL, TALL), TALL)
            h_ref[:, here] = x_ref[:, here].astype(F32) + mixed[:, i * TALL : (i + 1) * TALL]
            at += 1
    unit, inverse = norm_statistics(h_ref[...])
    n_ref[...] = (unit * gain_ref[...]).astype(LOW)
    inverse_ref[...] = inverse


def mix(order, o, x, gain, weights):
    tokens, width = x.shape
    count = len(weights)
    full = pl.BlockSpec((tokens, width), lambda i, o: (0, 0))
    return pl.pallas_call(
        functools.partial(mix_kernel, count),
        grid_spec=pltpu.PrefetchScalarGridSpec(
            num_scalar_prefetch=1,
            grid=(1,),
            in_specs=[
                pl.BlockSpec(o.shape, lambda i, o: (0, 0)),
                full,
                pl.BlockSpec((1, width), lambda i, o: (0, 0)),
            ]
            + [pl.BlockSpec(memory_space=pl.ANY)] * count,
            out_specs=[full, full, pl.BlockSpec((tokens, 1), lambda i, o: (0, 0))],
            scratch_shapes=[pltpu.VMEM(weight.shape, LOW) for weight in weights]
            + [pltpu.SemaphoreType.DMA((count,))],
        ),
        out_shape=[
            jax.ShapeDtypeStruct((tokens, width), F32),
            jax.ShapeDtypeStruct((tokens, width), LOW),
            jax.ShapeDtypeStruct((tokens, 1), F32),
        ],
        compiler_params=pltpu.CompilerParams(vmem_limit_bytes=VMEM_LIMIT),
        cost_estimate=lasting(6.0),
        name="mix",
    )(order, o, x, gain, *weights)


def tail_pack_kernel(n, piece, cols, ids_ref, owned_ref, gain_ref, *outs):
    block, start = owned_ref.shape[0], H * HD
    span = start + 2 * KVD
    for s, out_ref in enumerate(outs):
        at = pl.multiple_of(ids_ref[s] * piece, piece)
        out_ref[:block, :] = owned_ref[:, s * cols : (s + 1) * cols]
        row = block
        for lo in range(start, span, cols):
            out_ref[row : row + piece, :] = owned_ref[pl.ds(at, piece), lo : lo + cols]
            row += piece
        gains = gain_ref[pl.ds(at, piece), :].T.astype(LOW)
        out_ref[row:, :] = jnp.zeros((16, cols), LOW)
        out_ref[row : row + 16, :piece] = gains[:16]


def tail_pack(ids, owned, gain_cols, piece, cols):
    n, block = ids.shape[0], owned.shape[0]
    height = block + piece * (2 * KVD // cols) + 16
    return pl.pallas_call(
        functools.partial(tail_pack_kernel, n, piece, cols),
        grid_spec=pltpu.PrefetchScalarGridSpec(
            num_scalar_prefetch=1,
            grid=(1,),
            in_specs=[
                pl.BlockSpec(owned.shape, lambda i, o: (0, 0)),
                pl.BlockSpec(gain_cols.shape, lambda i, o: (0, 0)),
            ],
            out_specs=[pl.BlockSpec((height, cols), lambda i, o: (0, 0))] * n,
        ),
        out_shape=[jax.ShapeDtypeStruct((height, cols), LOW)] * n,
        compiler_params=pltpu.CompilerParams(vmem_limit_bytes=VMEM_LIMIT),
        cost_estimate=lasting(2.0),
        name="tail_pack",
    )(ids, owned, gain_cols)


def tail_adamw_kernel(block, piece, parts, *refs):
    total = ring_sum(*[ref[...] for ref in refs[:parts]])
    states, outs = refs[parts : parts + 9], refs[parts + 9 :]
    groups = 2 * KVD // total.shape[1]
    keyval = [total[block + g * piece : block + (g + 1) * piece] for g in range(groups)]
    weight, first, second = states[:3]
    outs[0][...], outs[1][...], outs[2][...] = adamw(
        weight[...], first[...], second[...], total[:block].T, RATE_OUTPUT, DECAY
    )
    weight, first, second = states[3:6]
    for j in range(2):
        if groups == 1:
            grad = keyval[0][:, j * KVD : (j + 1) * KVD]
        else:
            grad = jnp.concatenate(keyval[j * groups // 2 : (j + 1) * groups // 2], 1)
        outs[3][j], outs[4][j], outs[5][j] = adamw(
            weight[j], first[j], second[j], grad, RATE_KEYVAL, DECAY
        )
    weight, first, second = states[6:]
    outs[6][...], outs[7][...], outs[8][...] = adamw(
        weight[...], first[...], second[...], total[-16:, :piece][:2], RATE_GAINS, 0.0
    )


def tail_adamw(parts, states, block, piece):
    vmem = pl.BlockSpec(memory_space=pltpu.VMEM)
    shapes = [states[3 * i].shape for i in range(3) for _ in range(3)]
    return pl.pallas_call(
        functools.partial(tail_adamw_kernel, block, piece, len(parts)),
        in_specs=[vmem] * (len(parts) + 9),
        out_specs=[vmem] * 9,
        out_shape=[jax.ShapeDtypeStruct(shape, F32) for shape in shapes],
        compiler_params=pltpu.CompilerParams(vmem_limit_bytes=VMEM_LIMIT),
        cost_estimate=lasting(3.0),
        name="tail_adamw",
    )(*parts, *states)


def weight_grad_kernel(count, summed, order_ref, rows_ref, x_ref, *rest):
    out_ref, left = rest[-2:]
    tall = left.shape[0] // count

    @pl.when(pl.program_id(0) == 0)
    def _():
        for i in range(count):
            start = pl.multiple_of(order_ref[i] * tall, tall)
            left[i * tall : (i + 1) * tall, :] = rows_ref[:, pl.ds(start, tall)].T

    grad = contract(left[...], x_ref[...], 1, 1)
    if summed:
        grad = grad + rest[0][...].astype(F32)
    out_ref[...] = grad.astype(LOW)


def weight_grad(
    rows, x_t, total, wide, steps, source, target, order=None, base=None, add=None, place=None
):
    tokens, width = rows.shape
    if order is None:
        order = jnp.arange(width // TALL, dtype=jnp.int32)
    count = order.shape[0]
    out_spec = pl.BlockSpec((count * TALL, wide), lambda i, o: (0, target(i)))
    in_specs = [
        pl.BlockSpec((tokens, width), lambda i, o: (0, 0)),
        pl.BlockSpec((wide, tokens), lambda i, o: (source(i), 0)),
    ]
    args, aliases = [order, rows, x_t], {}
    if add is not None:
        in_specs.append(pl.BlockSpec((count * TALL, wide), lambda i, o: (0, place(i))))
        args.append(add)
    if base is not None:
        in_specs.append(pl.BlockSpec(memory_space=pl.ANY))
        aliases = {len(args): 0}
        args.append(base)
    return pl.pallas_call(
        functools.partial(weight_grad_kernel, count, add is not None),
        grid_spec=pltpu.PrefetchScalarGridSpec(
            num_scalar_prefetch=1,
            grid=(steps,),
            in_specs=in_specs,
            out_specs=out_spec,
            scratch_shapes=[pltpu.VMEM((count * TALL, tokens), LOW)],
        ),
        out_shape=jax.ShapeDtypeStruct((count * TALL, total), LOW),
        input_output_aliases=aliases,
        compiler_params=pltpu.CompilerParams(vmem_limit_bytes=VMEM_LIMIT),
        cost_estimate=lasting(steps * wide * count / 4800),
        name="weight_grad",
    )(*args)


def turned_kernel(x_ref, out_ref):
    out_ref[...] = x_ref[...].T


def turned(x):
    vmem = pl.BlockSpec(memory_space=pltpu.VMEM)
    return pl.pallas_call(
        turned_kernel,
        in_specs=[vmem],
        out_specs=vmem,
        out_shape=jax.ShapeDtypeStruct(x.shape[::-1], x.dtype),
        compiler_params=pltpu.CompilerParams(vmem_limit_bytes=VMEM_LIMIT),
        cost_estimate=lasting(1.5),
        name="turned",
    )(x)


def feed_kernel(pieces, count, *refs):
    rows_refs, grad_refs = refs[:count], refs[count : 2 * count]
    weight_ref, acts_ref, back_ref = refs[2 * count : 2 * count + 3]
    gate_v, up_v, down_v, rows_v, grad_v, sems = refs[2 * count + 3 :]
    copies = []
    for i, here in enumerate(pieces):
        copies.append(
            [
                pltpu.make_async_copy(weight_ref.at[j, :, here], held.at[:, here], sems.at[j, i])
                for j, held in enumerate((gate_v, up_v, down_v))
            ]
        )
        for copy in copies[-1]:
            copy.start()
    tokens = rows_refs[0].shape[0]
    for s in range(count):
        rows_v[s * tokens : (s + 1) * tokens, :] = rows_refs[s][...]
        grad_v[s * tokens : (s + 1) * tokens, :] = grad_refs[s][...]
    for here, (gate_copy, up_copy, down_copy) in zip(pieces, copies):
        gate_copy.wait()
        gate = jnp.dot(rows_v[...], gate_v[:, here], preferred_element_type=F32)
        up_copy.wait()
        up = jnp.dot(rows_v[...], up_v[:, here], preferred_element_type=F32)
        down_copy.wait()
        grad_hidden = jnp.dot(grad_v[...], down_v[:, here], preferred_element_type=F32)
        sigmoid = jax.nn.sigmoid(gate)
        silu = gate * sigmoid
        acts_ref[2, :, here] = (silu * up).astype(LOW)
        acts_ref[1, :, here] = (grad_hidden * silu).astype(LOW)
        acts_ref[0, :, here] = (
            grad_hidden * up * sigmoid * (1.0 + gate * (1.0 - sigmoid))
        ).astype(LOW)
    width = rows_v.shape[1]
    tall = 1024
    for lo in range(0, width, tall):
        some = slice(lo, lo + tall)
        back_ref[:, some] = (
            contract(acts_ref[0], gate_v[some, :], 1, 1)
            + contract(acts_ref[1], up_v[some, :], 1, 1)
        ).astype(LOW)


def feed(rows, grads, weight):
    count = len(rows)
    tokens, width = rows[0].shape
    units = weight.shape[2]
    half = units // 256 * 128 + 128
    pieces = [slice(0, half), slice(half, units)] if units % 128 == 0 else [slice(0, units)]
    vmem = pl.BlockSpec(memory_space=pltpu.VMEM)
    anywhere = pl.BlockSpec(memory_space=pl.ANY)
    total = count * tokens
    return pl.pallas_call(
        functools.partial(feed_kernel, pieces, count),
        in_specs=[vmem] * (2 * count) + [anywhere],
        out_specs=[vmem, vmem],
        out_shape=[
            jax.ShapeDtypeStruct((3, total, units), LOW),
            jax.ShapeDtypeStruct((total, width), LOW),
        ],
        scratch_shapes=[
            pltpu.VMEM((width, units), LOW),
            pltpu.VMEM((width, units), LOW),
            pltpu.VMEM((width, units), LOW),
            pltpu.VMEM((total, width), LOW),
            pltpu.VMEM((total, width), LOW),
            pltpu.SemaphoreType.DMA((3, len(pieces))),
        ],
        compiler_params=pltpu.CompilerParams(vmem_limit_bytes=VMEM_LIMIT),
        cost_estimate=lasting(1.0),
        name="feed",
    )(*rows, *grads, weight)


def feed_grad_kernel(halves, n, *refs):
    acts, rows = refs[:halves], refs[halves : halves + n]
    out_ref, left, right = refs[-3:]
    tokens = rows[0].shape[1]

    @pl.when(pl.program_id(1) == 0)
    def _():
        at = 0
        for act in acts:
            right[at : at + act.shape[1], :] = act[0]
            at += act.shape[1]

    for s in range(n):
        left[:, s * tokens : (s + 1) * tokens] = rows[s][...]
    out_ref[0] = jnp.dot(left[...], right[...], preferred_element_type=F32).astype(LOW)


def feed_grad(acts, rows_t, first, parts, base=None):
    n, halves = len(rows_t), len(acts)
    width, tokens = rows_t[0].shape
    units = acts[0].shape[2]
    tall = 1024
    in_specs = [
        pl.BlockSpec((1, act.shape[1], units), lambda p, r: (first + p, 0, 0)) for act in acts
    ]
    in_specs += [pl.BlockSpec((tall, tokens), lambda p, r: (r, 0))] * n
    args, aliases = list(acts) + list(rows_t), {}
    if base is not None:
        in_specs.append(pl.BlockSpec(memory_space=pl.ANY))
        aliases = {len(args): 0}
        args.append(base)
    return pl.pallas_call(
        functools.partial(feed_grad_kernel, halves, n),
        grid=(parts, width // tall),
        in_specs=in_specs,
        out_specs=pl.BlockSpec((1, tall, units), lambda p, r: (first + p, r, 0)),
        out_shape=jax.ShapeDtypeStruct((3, width, units), LOW),
        scratch_shapes=[
            pltpu.VMEM((tall, n * tokens), LOW),
            pltpu.VMEM((n * tokens, units), LOW),
        ],
        input_output_aliases=aliases,
        compiler_params=pltpu.CompilerParams(vmem_limit_bytes=VMEM_LIMIT),
        cost_estimate=lasting(1.0),
        name="feed_grad",
    )(*args)


def adamw_turned_kernel(rate, weight, first, second, grad, first_out, second_out, weight_out):
    first_out[...], second_out[...], weight_out[...] = adamw(
        weight[...], first[...], second[...], grad[...].astype(F32).T, rate, DECAY
    )


def adamw_turned(weight, first, second, grad, rate):
    rows, cols = weight.shape
    tall = 128 if rows % 128 == 0 else rows
    block = pl.BlockSpec((tall, cols), lambda i: (i, 0))
    return tuple(
        pl.pallas_call(
            functools.partial(adamw_turned_kernel, rate),
            grid=(rows // tall,),
            in_specs=[block] * 3 + [pl.BlockSpec((cols, tall), lambda i: (0, i))],
            out_specs=[block] * 3,
            out_shape=[jax.ShapeDtypeStruct(weight.shape, F32)] * 3,
            compiler_params=pltpu.CompilerParams(vmem_limit_bytes=VMEM_LIMIT),
            cost_estimate=pl.CostEstimate(
                flops=12 * rows * cols, bytes_accessed=28 * rows * cols, transcendentals=0
            ),
            name="adamw_turned",
        )(weight, first, second, grad)
    )


def on_device(
    sizes,
    tokens,
    positions,
    cotangent,
    query_weight,
    query_first,
    query_second,
    keyval_weight,
    keyval_first,
    keyval_second,
    output_weight,
    output_first,
    output_second,
    gateup_weight,
    gateup_first,
    gateup_second,
    down_weight,
    down_first,
    down_second,
    gains,
    gains_first,
    gains_second,
):
    n = sizes["tensor"]
    rank = lax.axis_index("tensor")
    offsets = ring_offsets(n)
    chunk_ids = [(rank + off + n) % n for off in offsets]
    rows, width = tokens.shape
    piece = keyval_weight.shape[1]
    block, cols = query_weight.shape

    ids = jnp.stack(chunk_ids).astype(jnp.int32)
    first_slots = ring_gather(first_pack(query_weight, keyval_weight, gains), n)
    attn_in = first_join(ids, first_slots, block, piece)
    feed_in = jnp.concatenate(
        [gateup_weight.astype(LOW), down_weight.T.astype(LOW)[None]], 0
    )
    attn_in, feed_in = after(attn_in, feed_in)
    attn_low = lax.all_gather(attn_in, "dp", axis=0, tiled=True)
    output_piece, _ = after(output_weight.T.astype(LOW), first_slots)
    output_slots = ring_gather(output_piece, n)
    grad_start, _ = after(cotangent, output_slots)
    grad_slots = ring_gather(grad_start, n, 1)
    feed_in, _ = after(feed_in, output_slots)
    feed_low = lax.all_gather(feed_in, "dp", axis=1, tiled=True)
    out_halves = dp_spread(
        jnp.concatenate(output_slots, 1), sizes["dp"], (attn_low, grad_slots)
    )
    out_order = jnp.concatenate([dp_order(sizes["dp"], block, odd) for odd in (0, 1)])

    span = H * HD + 2 * KVD
    own_positions = lax.dynamic_slice_in_dim(positions, rank * rows, rows, 0)
    freqs = 10000.0 ** (-jnp.arange(0, HD, 2, dtype=F32) / HD)
    angles = freqs[:, None] * own_positions.astype(F32)[None, :]
    cosine, sine = lax.optimization_barrier((jnp.cos(angles), jnp.sin(angles)))
    x = tokens.astype(F32)
    kv_t, first_normalized, gain_rows, first_inverse = begin(tokens, attn_low, cosine, sine)
    first_gain, second_gain = gain_rows[:1], gain_rows[1:2]
    q_t = project(first_normalized, attn_low, cosine, sine)
    kv_slots = jnp.stack(ring_gather(kv_t, n))
    grad_slots, kv_slots = after(grad_slots, kv_slots)
    grad_slots = ring_gather(grad_start, n, n, grad_slots)
    per_block = H // n
    meta = jnp.stack(
        [c * rows for c in chunk_ids]
        + [(c * per_block) // GROUP for c in chunk_ids]
        + [rank * rows]
    ).astype(jnp.int32)
    meta = jnp.concatenate([meta, out_order])
    pos_row = own_positions[None, :]
    mixed_t, mixed, lse = attend(meta, pos_row, q_t, kv_slots, n)
    out_halves, _ = after(out_halves, (mixed, grad_slots))
    out_pieces = out_halves + [swap(held, sizes["dp"], 1) for held in out_halves]
    residual, second_normalized, second_inverse = mix(
        out_order, mixed, tokens, second_gain, out_pieces
    )
    second_normalized, grad_slots = after(second_normalized, grad_slots)

    rows_slots = ring_gather(second_normalized, n, 1)
    grads_t = [turned(x) for x in grad_slots]
    groups = [[s for s in range(n) if abs(offsets[s]) == k] for k in range(n // 2 + 1)]
    order = sum(groups, [])
    rows_t, acts, part_slots, last = [None] * n, [], [None] * n, [grads_t]
    for k, group in enumerate(groups):
        if k == 2:
            rows_slots = ring_gather(second_normalized, n, n, rows_slots)
        chunks, _ = after([rows_slots[s] for s in group], last)
        for i, s in enumerate(group):
            rows_t[s] = turned(chunks[i])
        if k + 1 < len(groups):
            chunks, _ = after(chunks, [rows_t[s] for s in group])
        act, part = feed(chunks, [grad_slots[s] for s in group], feed_low)
        acts.append(act)
        last = part
        for i, s in enumerate(group):
            part_slots[s] = part[i * rows : (i + 1) * rows]
        if k == 0:
            for s in groups[1]:
                rows_slots[s], _ = after(rows_slots[s], part)
    acts, _ = after(acts, last)
    grad_mlp = feed_grad(acts, [rows_t[s] for s in order], 0, 2)
    from_left = ring_way(part_slots, n, 1)
    passed = []
    from_right = ring_way(part_slots, n, -1, passed, grad_mlp[0, :8, :128])
    acts, _ = after(acts, passed)
    grad_mlp = feed_grad(acts, [grads_t[s] for s in order], 2, 1, grad_mlp)
    second_grad = ring_sum(part_slots[0], from_left, from_right)
    mlp_parts = [contract(act[2], feed_low[2], 1, 1).astype(LOW) for act in acts[1:]]
    second_grad, (_, mlp_parts) = after(second_grad, (grad_mlp, mlp_parts))
    owned_mlp = lax.psum_scatter(grad_mlp, "dp", scatter_dimension=1, tiled=True)

    second_unit = residual * second_inverse
    residual_grad = cotangent.astype(F32) + norm_backward(
        second_grad, second_unit, second_inverse, second_gain
    )
    second_gain_grad = jnp.sum(second_grad * second_unit, 0)
    back = residual_grad.astype(LOW)
    mlp_slots = [None] * n
    for group, part in zip(groups[1:], mlp_parts):
        for i, s in enumerate(group):
            mlp_slots[s] = part[i * rows : (i + 1) * rows]
    block_far, block_left = ring_most(mlp_slots, n), ring_way(mlp_slots, n, 1)
    grad_q_t, grad_kv = attend_back(
        meta, pos_row, q_t, kv_slots, back, out_pieces, mixed_t, lse, cosine, sine, n
    )
    (grad_q_t, grad_kv), _ = after((grad_q_t, grad_kv), (block_far, block_left))

    places = [dp_order(sizes["dp"], block, odd) for odd in (0, 1)]
    kv_parts = [grad_kv[s] for s in range(n)]
    kv_left, passed = ring_way(kv_parts, n, 1), []
    own_kv = ring_sum(kv_parts[0], ring_way(kv_parts, n, -1, passed), kv_left)
    query_rows, _ = after(first_normalized, (passed, kv_left))
    partner = weight_grad(
        query_rows, grad_q_t, n * cols, cols, n, lambda i: i, lambda i: i, places[1]
    )
    partner = swap(partner, sizes["dp"], 1)
    out_rows, _ = after(back, grad_q_t)
    heads_cols = H * HD // (2 * KVD)
    grad_pack = weight_grad(
        out_rows, mixed_t, span, 2 * KVD, heads_cols, lambda i: i, lambda i: i
    )
    own_kv, _ = after(own_kv, partner)
    grad_k = own_kv[:KVD].reshape(KVH, 2, HD // 2, rows)
    upper, lower = grad_k[:, 0], grad_k[:, 1]
    grad_k = jnp.stack([upper * cosine + lower * sine, lower * cosine - upper * sine], 1)
    grad_kv_t = jnp.concatenate(
        [grad_k.reshape(KVD, rows).astype(LOW), own_kv[KVD:].astype(LOW)], 0
    )
    grad_pack = weight_grad(
        first_normalized, grad_kv_t, span, 2 * KVD, 1, lambda i: 0, lambda i: heads_cols,
        None, grad_pack,
    )
    query_slots, last, own_act = [None] * n, grad_pack, acts[0][2]
    for s in order[::-1]:
        if s == order[n // 2 - 1]:
            own_act, _ = after(own_act, last)
            mlp_slots[0] = contract(own_act, feed_low[2], 1, 1).astype(LOW)
            grad_pack, (owned_mlp, _, _) = after(grad_pack, (owned_mlp, last, mlp_slots[0]))
            owned_pack = lax.psum_scatter(grad_pack, "dp", scatter_dimension=0, tiled=True)
            owned_gateup, owned_down = owned_mlp[:2], owned_mlp[2]
            gateup_up = adamw(
                gateup_weight, gateup_first, gateup_second, owned_gateup.astype(F32), RATE_GATEUP,
                DECAY,
            )
            down_up = adamw_turned(down_weight, down_first, down_second, owned_down, RATE_DOWN)
            last = (last, gateup_up, down_up)
        query_rows, _ = after(first_normalized, last)
        last = query_slots[s] = weight_grad(
            query_rows, grad_q_t, cols, cols, 1, lambda i, s=s: s, lambda i: 0, places[0], None,
            partner, lambda i, s=s: s,
        )
    query_far, query_left = ring_most(query_slots, n), ring_way(query_slots, n, 1)
    query_right = ring_last(query_slots, n, query_far)
    query_sum = ring_sum(query_slots[0], query_left, query_right).astype(LOW)
    block_right = ring_last(mlp_slots, n, block_far, query_right)
    (back_q_t, back_kv_t), _ = after((grad_q_t, grad_kv_t), query_slots)
    grad_qkv_t = jnp.concatenate(
        [back_q_t, back_kv_t, jnp.zeros((attn_low.shape[1] - span, rows), LOW)], 0
    )
    first_grad = contract(grad_qkv_t, attn_low, 0, 1)
    first_unit = x * first_inverse
    first_gain_grad = jnp.sum(first_grad * first_unit, 0)
    layer_input_gradient = residual_grad + norm_backward(
        first_grad, first_unit, first_inverse, first_gain
    )
    gain_grads, bit = jnp.stack([first_gain_grad, second_gain_grad]), 1
    while bit < sizes["dp"]:
        gain_grads = gain_grads + swap(gain_grads, sizes["dp"], bit)
        bit *= 2
    gain_grads = lax.dynamic_slice_in_dim(gain_grads, lax.axis_index("dp") * block, block, 1)
    gain_cols = jnp.pad(gain_grads.T, ((0, 0), (0, 126)))

    slots = tail_pack(ids, owned_pack, gain_cols, piece, cols)
    query_sum, _ = after(query_sum, slots[0])
    own_query = dp_scatter(query_sum, sizes["dp"], ()).astype(F32)
    query_up = adamw(query_weight, query_first, query_second, own_query, RATE_QUERY, DECAY)
    parts = [slots[0], ring_way(slots, n, -1), ring_way(slots, n, 1)]
    block_right, _ = after(block_right, parts[1])
    block_out = residual + ring_sum(mlp_slots[0], block_left, block_right)
    states = [output_weight, output_first, output_second, keyval_weight, keyval_first]
    states += [keyval_second, gains, gains_first, gains_second]
    parts = [part for part in parts if part is not None]
    last = tail_adamw(parts, states, block, piece)
    output_up, keyval_up, gains_up = tuple(last[:3]), tuple(last[3:6]), tuple(last[6:])
    return (
        (block_out, layer_input_gradient)
        + query_up
        + keyval_up
        + output_up
        + gateup_up
        + down_up
        + gains_up
    )


def solution(mesh):
    rows = P(("dp", "tensor"), None)
    grid = P("dp", "tensor")
    cross = P("tensor", "dp")
    pair = P(None, ("dp", "tensor"), None)
    stacked = P(None, "dp", "tensor")
    narrow = P(None, ("dp", "tensor"))
    states = (grid,) * 3 + (pair,) * 3 + (cross,) * 3 + (stacked,) * 3 + (cross,) * 3 + (narrow,) * 3
    return jax.shard_map(
        functools.partial(on_device, dict(mesh.shape)),
        mesh=mesh,
        in_specs=(rows, P("dp"), rows) + states,
        out_specs=(rows, rows) + states,
        check_vma=False,
    )
```

```python
import functools

import jax
import jax.numpy as jnp
from jax import lax
from jax.experimental import pallas as pl
from jax.experimental.pallas import tpu as pltpu
from jax.sharding import PartitionSpec as P

H = 32
KVH = 4
HD = 64
GROUP = 8
KVD = KVH * HD
STEP = 10
EPS = 1e-05
BETA_ONE = 0.9
BETA_TWO = 0.999
ADAM_EPS = 1e-08
DECAY = 0.1
RATE_QUERY = 0.06
RATE_KEYVAL = 0.06
RATE_OUTPUT = 0.5
RATE_GATEUP = 0.06
RATE_DOWN = 0.04
RATE_GAINS = 1.5
LOW = jnp.bfloat16
F32 = jnp.float32
TALL = 128
VMEM_LIMIT = 56 * 1024 * 1024
LONG = pl.CostEstimate(flops=2 * 10**14, bytes_accessed=10**6, transcendentals=0)


def lasting(us):
    return pl.CostEstimate(flops=int(us * 1.15e9), bytes_accessed=10**6, transcendentals=0)


def contract(left, right, dim_left, dim_right):
    return lax.dot_general(
        left, right, (((dim_left,), (dim_right,)), ((), ())), preferred_element_type=F32
    )


def ring_offsets(n):
    return [0] + [-k for k in range(1, n // 2 + 1)] + [k for k in range(1, (n - 1) // 2 + 1)]


def shift(x, n, by):
    return lax.ppermute(x, "tensor", [(i, (i + by) % n) for i in range(n)])


def ring_gather(x, n, steps=None, known=None):
    slots, used = [x], 1
    for by, hops in ((1, n // 2), (-1, (n - 1) // 2)):
        held = x
        for hop in range(hops):
            if steps is not None and hop >= steps:
                slots.append(None)
                continue
            if known is not None and known[used + hop] is not None:
                held = known[used + hop]
            else:
                held = shift(held, n, by)
            slots.append(held)
        used += hops
    return slots


def after(late, early):
    return lax.optimization_barrier((late, early))


def ring_way(slots, n, by, passed=None, hold=None):
    first, hops = (1, n // 2) if by < 0 else (1 + n // 2, (n - 1) // 2)
    held = None
    for k in range(hops, 0, -1):
        part = slots[first + k - 1]
        if held is not None:
            part = (part.astype(F32) + held.astype(F32)).astype(LOW)
            if hold is not None and k == 1:
                part, _ = after(part, hold)
            if passed is not None:
                passed.append(part)
        held = shift(part.astype(LOW), n, by)
    return held


def ring_most(slots, n):
    held = None
    for k in range(n // 2, 1, -1):
        part = slots[k] if held is None else ring_sum(slots[k], held)
        held = shift(part.astype(LOW), n, -1)
    return held


def ring_last(slots, n, held, hold=None):
    part = (slots[1] if held is None else ring_sum(slots[1], held)).astype(LOW)
    if hold is not None:
        part, _ = after(part, hold)
    return shift(part, n, -1)


def ring_sum(own, *arrived):
    total = own.astype(F32)
    for held in arrived:
        if held is not None:
            total = total + held.astype(F32)
    return total


def ring_scatter(slots, n):
    return ring_sum(slots[0], ring_way(slots, n, -1), ring_way(slots, n, 1))


def swap(x, size, bit):
    return lax.ppermute(x, "dp", [(i, i ^ bit) for i in range(size)])


def dp_plan(size, block):
    bits = [1 << i for i in range(1, size.bit_length() - 1)]
    return [bits, bits[::-1]] if block >= 256 else [bits]


def dp_order(size, block, odd):
    plan = dp_plan(size, block)
    me = lax.axis_index("dp")
    places = []
    for h, bits in enumerate(plan):
        partners = [odd]
        for bit in bits:
            partners += [p | bit for p in partners]
        places += [(me ^ p) * len(plan) + h for p in partners]
    return jnp.stack(places).astype(jnp.int32)


def dp_spread(x, size, hold):
    block = x.shape[0]
    plan = dp_plan(size, block)
    tall = block // len(plan)
    even = [x[h * tall : (h + 1) * tall] for h in range(len(plan))]
    for i in range(len(plan[0])):
        got = [swap(held, size, bits[i]) for held, bits in zip(even, plan)]
        even = [jnp.concatenate(pair, 0) for pair in zip(even, got)]
        if i == 0:
            even, _ = after(even, hold)
    return even


def dp_scatter(held, size, hold):
    plan = dp_plan(size, 2 * held.shape[0] // size)
    tall = held.shape[0] // len(plan)
    parts = [held[h * tall : (h + 1) * tall] for h in range(len(plan))]
    for i in reversed(range(len(plan[0]))):
        half = parts[0].shape[0] // 2
        got = [swap(part[half:], size, bits[i]) for part, bits in zip(parts, plan)]
        if i == len(plan[0]) - 1:
            got, _ = after(got, hold)
        parts = [ring_sum(part[:half], new).astype(LOW) for part, new in zip(parts, got)]
    return jnp.concatenate(parts, 0)


def norm_statistics(rows_in):
    inverse = lax.rsqrt(jnp.mean(rows_in * rows_in, -1, keepdims=True) + EPS)
    return rows_in * inverse, inverse


def norm_backward(grad, unit, inverse, gain):
    scaled = grad * gain
    return inverse * (scaled - unit * jnp.mean(scaled * unit, -1, keepdims=True))


def adamw(weight, first, second, grad, rate, decay):
    first_new = BETA_ONE * first + (1.0 - BETA_ONE) * grad
    second_new = BETA_TWO * second + (1.0 - BETA_TWO) * grad * grad
    fix_one = 1.0 - BETA_ONE**STEP
    fix_two = 1.0 - BETA_TWO**STEP
    direction = first_new / fix_one / (jnp.sqrt(second_new / fix_two) + ADAM_EPS)
    return first_new, second_new, weight - rate * (direction + decay * weight)


def turn(values, cosine, sine):
    upper, lower = values[: HD // 2], values[HD // 2 :]
    return jnp.concatenate([upper * cosine - lower * sine, lower * cosine + upper * sine], 0)


def first_pack_kernel(cols, query_ref, keyval_ref, gains_ref, out_ref):
    block, piece = query_ref.shape[0], keyval_ref.shape[1]
    out_ref[block:, :] = jnp.zeros((out_ref.shape[0] - block, cols), LOW)
    out_ref[:block, :] = query_ref[...].astype(LOW)
    row = block
    for lo in range(0, 2 * KVD, cols):
        for j in range(0, cols, KVD):
            at = (lo + j) // KVD
            out_ref[row : row + piece, j : j + KVD] = keyval_ref[at].astype(LOW)
        row += piece
    out_ref[row : row + 2, :piece] = gains_ref[...].astype(LOW)


def first_pack(query, keyval, gains):
    block, cols = query.shape
    piece = keyval.shape[1]
    vmem = pl.BlockSpec(memory_space=pltpu.VMEM)
    height = block + piece * (2 * KVD // cols) + 16
    return pl.pallas_call(
        functools.partial(first_pack_kernel, cols),
        in_specs=[vmem] * 3,
        out_specs=vmem,
        out_shape=jax.ShapeDtypeStruct((height, cols), LOW),
        compiler_params=pltpu.CompilerParams(vmem_limit_bytes=VMEM_LIMIT),
        cost_estimate=lasting(2.0),
        name="first_pack",
    )(query, keyval, gains)


def first_join_kernel(n, piece, ids_ref, *refs):
    slots, out_ref = refs[:n], refs[n]
    block, cols = out_ref.shape[0], slots[0].shape[1]
    span = n * cols + 2 * KVD
    out_ref[:, span:] = jnp.zeros((block, out_ref.shape[1] - span), LOW)
    for s, slot in enumerate(slots):
        at = pl.multiple_of(ids_ref[s] * piece, piece)
        out_ref[:, s * cols : (s + 1) * cols] = slot[:block, :]
        row = block
        for lo in range(n * cols, span, cols):
            out_ref[pl.ds(at, piece), lo : lo + cols] = slot[row : row + piece, :]
            row += piece
        gains = slot[row : row + 16, :128].astype(F32).T.astype(LOW)
        out_ref[pl.ds(at, piece), span : span + 16] = gains[:piece]


def first_join(ids, slots, block, piece):
    n = len(slots)
    cols = slots[0].shape[1]
    width = n * cols + 2 * KVD + 128
    return pl.pallas_call(
        functools.partial(first_join_kernel, n, piece),
        grid_spec=pltpu.PrefetchScalarGridSpec(
            num_scalar_prefetch=1,
            grid=(1,),
            in_specs=[pl.BlockSpec(slots[0].shape, lambda i, o: (0, 0))] * n,
            out_specs=pl.BlockSpec((block, width), lambda i, o: (0, 0)),
        ),
        out_shape=jax.ShapeDtypeStruct((block, width), LOW),
        compiler_params=pltpu.CompilerParams(vmem_limit_bytes=VMEM_LIMIT),
        cost_estimate=lasting(2.0),
        name="first_join",
    )(ids, *slots)


def begin_kernel(
    x_ref, gain_ref, weight_ref, cos_ref, sin_ref, out_ref, rows_ref, gains_ref, inverse_ref
):
    gains = gain_ref[...].astype(F32).T[: gains_ref.shape[0]]
    unit, inverse = norm_statistics(x_ref[...].astype(F32))
    rows = (unit * gains[:1]).astype(LOW)
    rows_ref[...], gains_ref[...], inverse_ref[...] = rows, gains, inverse
    wide = jnp.dot(rows, weight_ref[...], preferred_element_type=F32).T
    cosine, sine = cos_ref[...], sin_ref[...]
    for h in range(KVH):
        here = slice(h * HD, (h + 1) * HD)
        out_ref[here, :] = turn(wide[here], cosine, sine).astype(LOW)
    out_ref[KVD:, :] = wide[KVD:].astype(LOW)


def begin(x, weight, cosine, sine):
    tokens, width = x.shape
    cols = 2 * KVD
    return pl.pallas_call(
        begin_kernel,
        grid=(1,),
        in_specs=[
            pl.BlockSpec((tokens, width), lambda b: (0, 0)),
            pl.BlockSpec((width, TALL), lambda b: (0, (H * HD + cols) // TALL)),
            pl.BlockSpec((width, cols), lambda b: (0, H * HD // cols)),
            pl.BlockSpec(cosine.shape, lambda b: (0, 0)),
            pl.BlockSpec(sine.shape, lambda b: (0, 0)),
        ],
        out_specs=[
            pl.BlockSpec((cols, tokens), lambda b: (0, 0)),
            pl.BlockSpec((tokens, width), lambda b: (0, 0)),
            pl.BlockSpec((8, width), lambda b: (0, 0)),
            pl.BlockSpec((tokens, 1), lambda b: (0, 0)),
        ],
        out_shape=[
            jax.ShapeDtypeStruct((cols, tokens), LOW),
            jax.ShapeDtypeStruct((tokens, width), LOW),
            jax.ShapeDtypeStruct((8, width), F32),
            jax.ShapeDtypeStruct((tokens, 1), F32),
        ],
        compiler_params=pltpu.CompilerParams(vmem_limit_bytes=VMEM_LIMIT),
        cost_estimate=lasting(5.0),
        name="begin",
    )(x, weight, weight, cosine, sine)


def project_kernel(rows_ref, weight_ref, cos_ref, sin_ref, out_ref):
    wide = jnp.dot(rows_ref[...], weight_ref[...], preferred_element_type=F32).T
    cosine, sine = cos_ref[...], sin_ref[...]
    for h in range(wide.shape[0] // HD):
        here = slice(h * HD, (h + 1) * HD)
        out_ref[here, :] = (turn(wide[here], cosine, sine) * HD ** (-0.5)).astype(LOW)


def project(rows, weight, cosine, sine):
    tokens, width = rows.shape
    cols = 2 * KVD
    blocks = H * HD // cols
    return pl.pallas_call(
        project_kernel,
        grid=(blocks,),
        in_specs=[
            pl.BlockSpec((tokens, width), lambda b: (0, 0)),
            pl.BlockSpec((width, cols), lambda b: (0, b)),
            pl.BlockSpec(cosine.shape, lambda b: (0, 0)),
            pl.BlockSpec(sine.shape, lambda b: (0, 0)),
        ],
        out_specs=pl.BlockSpec((cols, tokens), lambda b: (b, 0)),
        out_shape=jax.ShapeDtypeStruct((blocks * cols, tokens), LOW),
        compiler_params=pltpu.CompilerParams(vmem_limit_bytes=VMEM_LIMIT),
        cost_estimate=lasting(8.0),
        name="project",
    )(rows, weight, cosine, sine)


def fill_bias(meta_ref, pos_ref, bias_ref, slots, tokens):
    query = meta_ref[2 * slots] + lax.broadcasted_iota(jnp.int32, (tokens, tokens), 1)
    least = query - pos_ref[...]
    row = lax.broadcasted_iota(jnp.int32, (tokens, tokens), 0)
    for c in range(slots):
        key = meta_ref[c] + row
        bias_ref[c] = jnp.where((key <= query) & (key >= least), 0.0, -1e30)


def attend_kernel(
    slots, heads, meta_ref, pos_ref, q_ref, kv_ref, out_ref, rows_ref, lse_ref, bias_ref
):
    tokens = q_ref.shape[1]
    block = pl.program_id(0)

    @pl.when(block == 0)
    def _():
        fill_bias(meta_ref, pos_ref, bias_ref, slots, tokens)

    start = pl.multiple_of(meta_ref[slots + block] * HD, HD)
    keys = [kv_ref[c, pl.ds(start, HD), :].T for c in range(slots)]
    values = [kv_ref[c, pl.ds(KVD + start, HD), :] for c in range(slots)]
    for h in range(heads):
        query = q_ref[h * HD : (h + 1) * HD, :]
        scores = [
            jnp.dot(keys[c], query, preferred_element_type=F32) + bias_ref[c] for c in range(slots)
        ]
        peak = functools.reduce(jnp.maximum, [jnp.max(s, 0, keepdims=True) for s in scores])
        total = jnp.zeros_like(peak)
        mixed = jnp.zeros((HD, tokens), F32)
        for c in range(slots):
            expo = jnp.exp(scores[c] - peak)
            total = total + jnp.sum(expo, 0, keepdims=True)
            mixed = mixed + jnp.dot(values[c], expo.astype(LOW), preferred_element_type=F32)
        out_ref[h * HD : (h + 1) * HD, :] = (mixed / total).astype(LOW)
        lse_ref[0, h : h + 1, :] = peak + jnp.log(total)
    rows_ref[...] = out_ref[...].T


def attend(meta, pos_row, q_t, kv_slots, slots):
    tokens = q_t.shape[1]
    heads = H // slots
    rows = heads * HD
    return pl.pallas_call(
        functools.partial(attend_kernel, slots, heads),
        grid_spec=pltpu.PrefetchScalarGridSpec(
            num_scalar_prefetch=1,
            grid=(slots,),
            in_specs=[
                pl.BlockSpec((1, tokens), lambda b, m: (0, 0)),
                pl.BlockSpec((rows, tokens), lambda b, m: (b, 0)),
                pl.BlockSpec((slots, 2 * KVD, tokens), lambda b, m: (0, 0, 0)),
            ],
            out_specs=[
                pl.BlockSpec((rows, tokens), lambda b, m: (b, 0)),
                pl.BlockSpec((tokens, rows), lambda b, m: (0, b)),
                pl.BlockSpec((1, heads, tokens), lambda b, m: (b, 0, 0)),
            ],
            scratch_shapes=[pltpu.VMEM((slots, tokens, tokens), F32)],
        ),
        out_shape=[
            jax.ShapeDtypeStruct((H * HD, tokens), LOW),
            jax.ShapeDtypeStruct((tokens, H * HD), LOW),
            jax.ShapeDtypeStruct((slots, heads, tokens), F32),
        ],
        compiler_params=pltpu.CompilerParams(vmem_limit_bytes=VMEM_LIMIT),
        cost_estimate=pl.CostEstimate(
            flops=16 * H * HD * tokens * tokens * slots,
            bytes_accessed=4 * H * HD * tokens,
            transcendentals=H * tokens * tokens * slots,
        ),
        name="attend",
    )(meta, pos_row, q_t, kv_slots)


def attend_back_kernel(slots, heads, count, meta_ref, pos_ref, q_ref, kv_ref, back_ref, *refs):
    weights, refs = refs[:count], refs[count:]
    o_ref, lse_ref, cos_ref, sin_ref, dq_ref, dkv_out_ref = refs[:6]
    bias_ref, dkv_ref, do_ref, moved_ref = refs[6:]
    tokens = q_ref.shape[1]
    block = pl.program_id(0)

    @pl.when(block == 0)
    def _():
        fill_bias(meta_ref, pos_ref, bias_ref, slots, tokens)
        dkv_ref[...] = jnp.zeros_like(dkv_ref)
        for i in range(back_ref.shape[1] // TALL):
            at = pl.multiple_of(meta_ref[2 * slots + 1 + i] * TALL, TALL)
            moved_ref[:, i * TALL : (i + 1) * TALL] = back_ref[:, pl.ds(at, TALL)]

    grad_mixed, at = 0.0, 0
    for weight in weights:
        here = slice(at, at + weight.shape[0])
        grad_mixed += jnp.dot(moved_ref[:, here], weight[...], preferred_element_type=F32)
        at += weight.shape[0]
    do_ref[...] = grad_mixed.T.astype(LOW)
    start = pl.multiple_of(meta_ref[slots + block] * HD, HD)
    keys_t = [kv_ref[c, pl.ds(start, HD), :] for c in range(slots)]
    keys = [k.T for k in keys_t]
    values = [kv_ref[c, pl.ds(KVD + start, HD), :].T for c in range(slots)]
    cosine, sine = cos_ref[...], -sin_ref[...]
    grad_keys = [jnp.zeros((HD, tokens), F32) for _ in range(slots)]
    grad_values = [jnp.zeros((HD, tokens), F32) for _ in range(slots)]
    for h in range(heads):
        here = slice(h * HD, (h + 1) * HD)
        query, grad = q_ref[here, :], do_ref[here, :]
        delta = jnp.sum(grad.astype(F32) * o_ref[here, :].astype(F32), 0, keepdims=True)
        log_total = lse_ref[0, h : h + 1, :]
        grad_query = jnp.zeros((HD, tokens), F32)
        for c in range(slots):
            scores = jnp.dot(keys[c], query, preferred_element_type=F32) + bias_ref[c]
            prob = jnp.exp(scores - log_total)
            grad_prob = jnp.dot(values[c], grad, preferred_element_type=F32)
            grad_score = (prob * (grad_prob - delta)).astype(LOW)
            grad_values[c] = grad_values[c] + contract(grad, prob.astype(LOW), 1, 1)
            grad_keys[c] = grad_keys[c] + contract(query, grad_score, 1, 1)
            grad_query = grad_query + jnp.dot(keys_t[c], grad_score, preferred_element_type=F32)
        dq_ref[here, :] = (turn(grad_query, cosine, sine) * HD ** (-0.5)).astype(LOW)
    for c in range(slots):
        dkv_ref[c, pl.ds(start, HD), :] += grad_keys[c]
        dkv_ref[c, pl.ds(KVD + start, HD), :] += grad_values[c]

    @pl.when(block == pl.num_programs(0) - 1)
    def _():
        dkv_out_ref[...] = dkv_ref[...].astype(LOW)


def attend_back(meta, pos_row, q_t, kv_slots, back, weights, o_t, lse, cosine, sine, slots):
    tokens = q_t.shape[1]
    heads = H // slots
    rows = heads * HD
    head_block = pl.BlockSpec((rows, tokens), lambda b, m: (b, 0))
    table = pl.BlockSpec(cosine.shape, lambda b, m: (0, 0))
    whole = pl.BlockSpec((slots, 2 * KVD, tokens), lambda b, m: (0, 0, 0))
    return pl.pallas_call(
        functools.partial(attend_back_kernel, slots, heads, len(weights)),
        grid_spec=pltpu.PrefetchScalarGridSpec(
            num_scalar_prefetch=1,
            grid=(slots,),
            in_specs=[
                pl.BlockSpec((1, tokens), lambda b, m: (0, 0)),
                head_block,
                whole,
                pl.BlockSpec(back.shape, lambda b, m: (0, 0)),
                *[pl.BlockSpec((w.shape[0], rows), lambda b, m: (0, b)) for w in weights],
                head_block,
                pl.BlockSpec((1, heads, tokens), lambda b, m: (b, 0, 0)),
                table,
                table,
            ],
            out_specs=[head_block, whole],
            scratch_shapes=[
                pltpu.VMEM((slots, tokens, tokens), F32),
                pltpu.VMEM((slots, 2 * KVD, tokens), F32),
                pltpu.VMEM((rows, tokens), LOW),
                pltpu.VMEM(back.shape, LOW),
            ],
        ),
        out_shape=[
            jax.ShapeDtypeStruct((H * HD, tokens), LOW),
            jax.ShapeDtypeStruct((slots, 2 * KVD, tokens), LOW),
        ],
        compiler_params=pltpu.CompilerParams(vmem_limit_bytes=VMEM_LIMIT),
        cost_estimate=LONG,
        name="attend_back",
    )(meta, pos_row, q_t, kv_slots, back, *weights, o_t, lse, cosine, sine)


def mix_kernel(count, order_ref, o_ref, x_ref, gain_ref, *refs):
    weights, (h_ref, n_ref, inverse_ref) = refs[:count], refs[count : count + 3]
    held, sems = refs[count + 3 : -1], refs[-1]
    copies = [
        pltpu.make_async_copy(src, dst, sems.at[i]) for i, (src, dst) in enumerate(zip(weights, held))
    ]
    for copy in copies:
        copy.start()
    at = 0
    for copy, weight in zip(copies, held):
        copy.wait()
        mixed = contract(o_ref[...], weight[...], 1, 1)
        for i in range(weight.shape[0] // TALL):
            here = pl.ds(pl.multiple_of(order_ref[at] * TALL, TALL), TALL)
            h_ref[:, here] = x_ref[:, here].astype(F32) + mixed[:, i * TALL : (i + 1) * TALL]
            at += 1
    unit, inverse = norm_statistics(h_ref[...])
    n_ref[...] = (unit * gain_ref[...]).astype(LOW)
    inverse_ref[...] = inverse


def mix(order, o, x, gain, weights):
    tokens, width = x.shape
    count = len(weights)
    full = pl.BlockSpec((tokens, width), lambda i, o: (0, 0))
    return pl.pallas_call(
        functools.partial(mix_kernel, count),
        grid_spec=pltpu.PrefetchScalarGridSpec(
            num_scalar_prefetch=1,
            grid=(1,),
            in_specs=[
                pl.BlockSpec(o.shape, lambda i, o: (0, 0)),
                full,
                pl.BlockSpec((1, width), lambda i, o: (0, 0)),
            ]
            + [pl.BlockSpec(memory_space=pl.ANY)] * count,
            out_specs=[full, full, pl.BlockSpec((tokens, 1), lambda i, o: (0, 0))],
            scratch_shapes=[pltpu.VMEM(weight.shape, LOW) for weight in weights]
            + [pltpu.SemaphoreType.DMA((count,))],
        ),
        out_shape=[
            jax.ShapeDtypeStruct((tokens, width), F32),
            jax.ShapeDtypeStruct((tokens, width), LOW),
            jax.ShapeDtypeStruct((tokens, 1), F32),
        ],
        compiler_params=pltpu.CompilerParams(vmem_limit_bytes=VMEM_LIMIT),
        cost_estimate=lasting(6.0),
        name="mix",
    )(order, o, x, gain, *weights)


def tail_pack_kernel(n, piece, cols, ids_ref, owned_ref, gain_ref, *outs):
    block, start = owned_ref.shape[0], H * HD
    span = start + 2 * KVD
    for s, out_ref in enumerate(outs):
        at = pl.multiple_of(ids_ref[s] * piece, piece)
        out_ref[:block, :] = owned_ref[:, s * cols : (s + 1) * cols]
        row = block
        for lo in range(start, span, cols):
            out_ref[row : row + piece, :] = owned_ref[pl.ds(at, piece), lo : lo + cols]
            row += piece
        gains = gain_ref[pl.ds(at, piece), :].T.astype(LOW)
        out_ref[row:, :] = jnp.zeros((16, cols), LOW)
        out_ref[row : row + 16, :piece] = gains[:16]


def tail_pack(ids, owned, gain_cols, piece, cols):
    n, block = ids.shape[0], owned.shape[0]
    height = block + piece * (2 * KVD // cols) + 16
    return pl.pallas_call(
        functools.partial(tail_pack_kernel, n, piece, cols),
        grid_spec=pltpu.PrefetchScalarGridSpec(
            num_scalar_prefetch=1,
            grid=(1,),
            in_specs=[
                pl.BlockSpec(owned.shape, lambda i, o: (0, 0)),
                pl.BlockSpec(gain_cols.shape, lambda i, o: (0, 0)),
            ],
            out_specs=[pl.BlockSpec((height, cols), lambda i, o: (0, 0))] * n,
        ),
        out_shape=[jax.ShapeDtypeStruct((height, cols), LOW)] * n,
        compiler_params=pltpu.CompilerParams(vmem_limit_bytes=VMEM_LIMIT),
        cost_estimate=lasting(2.0),
        name="tail_pack",
    )(ids, owned, gain_cols)


def tail_adamw_kernel(block, piece, parts, *refs):
    total = ring_sum(*[ref[...] for ref in refs[:parts]])
    states, outs = refs[parts : parts + 9], refs[parts + 9 :]
    groups = 2 * KVD // total.shape[1]
    keyval = [total[block + g * piece : block + (g + 1) * piece] for g in range(groups)]
    weight, first, second = states[:3]
    outs[0][...], outs[1][...], outs[2][...] = adamw(
        weight[...], first[...], second[...], total[:block].T, RATE_OUTPUT, DECAY
    )
    weight, first, second = states[3:6]
    for j in range(2):
        if groups == 1:
            grad = keyval[0][:, j * KVD : (j + 1) * KVD]
        else:
            grad = jnp.concatenate(keyval[j * groups // 2 : (j + 1) * groups // 2], 1)
        outs[3][j], outs[4][j], outs[5][j] = adamw(
            weight[j], first[j], second[j], grad, RATE_KEYVAL, DECAY
        )
    weight, first, second = states[6:]
    outs[6][...], outs[7][...], outs[8][...] = adamw(
        weight[...], first[...], second[...], total[-16:, :piece][:2], RATE_GAINS, 0.0
    )


def tail_adamw(parts, states, block, piece):
    vmem = pl.BlockSpec(memory_space=pltpu.VMEM)
    shapes = [states[3 * i].shape for i in range(3) for _ in range(3)]
    return pl.pallas_call(
        functools.partial(tail_adamw_kernel, block, piece, len(parts)),
        in_specs=[vmem] * (len(parts) + 9),
        out_specs=[vmem] * 9,
        out_shape=[jax.ShapeDtypeStruct(shape, F32) for shape in shapes],
        compiler_params=pltpu.CompilerParams(vmem_limit_bytes=VMEM_LIMIT),
        cost_estimate=lasting(3.0),
        name="tail_adamw",
    )(*parts, *states)


def weight_grad_kernel(count, summed, order_ref, rows_ref, x_ref, *rest):
    out_ref, left = rest[-2:]
    tall = left.shape[0] // count

    @pl.when(pl.program_id(0) == 0)
    def _():
        for i in range(count):
            start = pl.multiple_of(order_ref[i] * tall, tall)
            left[i * tall : (i + 1) * tall, :] = rows_ref[:, pl.ds(start, tall)].T

    grad = contract(left[...], x_ref[...], 1, 1)
    if summed:
        grad = grad + rest[0][...].astype(F32)
    out_ref[...] = grad.astype(LOW)


def weight_grad(
    rows, x_t, total, wide, steps, source, target, order=None, base=None, add=None, place=None
):
    tokens, width = rows.shape
    if order is None:
        order = jnp.arange(width // TALL, dtype=jnp.int32)
    count = order.shape[0]
    out_spec = pl.BlockSpec((count * TALL, wide), lambda i, o: (0, target(i)))
    in_specs = [
        pl.BlockSpec((tokens, width), lambda i, o: (0, 0)),
        pl.BlockSpec((wide, tokens), lambda i, o: (source(i), 0)),
    ]
    args, aliases = [order, rows, x_t], {}
    if add is not None:
        in_specs.append(pl.BlockSpec((count * TALL, wide), lambda i, o: (0, place(i))))
        args.append(add)
    if base is not None:
        in_specs.append(pl.BlockSpec(memory_space=pl.ANY))
        aliases = {len(args): 0}
        args.append(base)
    return pl.pallas_call(
        functools.partial(weight_grad_kernel, count, add is not None),
        grid_spec=pltpu.PrefetchScalarGridSpec(
            num_scalar_prefetch=1,
            grid=(steps,),
            in_specs=in_specs,
            out_specs=out_spec,
            scratch_shapes=[pltpu.VMEM((count * TALL, tokens), LOW)],
        ),
        out_shape=jax.ShapeDtypeStruct((count * TALL, total), LOW),
        input_output_aliases=aliases,
        compiler_params=pltpu.CompilerParams(vmem_limit_bytes=VMEM_LIMIT),
        cost_estimate=lasting(steps * wide * count / 4800),
        name="weight_grad",
    )(*args)


def turned_kernel(x_ref, out_ref):
    out_ref[...] = x_ref[...].T


def turned(x):
    vmem = pl.BlockSpec(memory_space=pltpu.VMEM)
    return pl.pallas_call(
        turned_kernel,
        in_specs=[vmem],
        out_specs=vmem,
        out_shape=jax.ShapeDtypeStruct(x.shape[::-1], x.dtype),
        compiler_params=pltpu.CompilerParams(vmem_limit_bytes=VMEM_LIMIT),
        cost_estimate=lasting(1.5),
        name="turned",
    )(x)


def feed_kernel(pieces, count, *refs):
    rows_refs, grad_refs = refs[:count], refs[count : 2 * count]
    weight_ref, acts_ref, back_ref = refs[2 * count : 2 * count + 3]
    gate_v, up_v, down_v, rows_v, grad_v, sems = refs[2 * count + 3 :]
    copies = []
    for i, here in enumerate(pieces):
        copies.append(
            [
                pltpu.make_async_copy(weight_ref.at[j, :, here], held.at[:, here], sems.at[j, i])
                for j, held in enumerate((gate_v, up_v, down_v))
            ]
        )
        for copy in copies[-1]:
            copy.start()
    tokens = rows_refs[0].shape[0]
    for s in range(count):
        rows_v[s * tokens : (s + 1) * tokens, :] = rows_refs[s][...]
        grad_v[s * tokens : (s + 1) * tokens, :] = grad_refs[s][...]
    for here, (gate_copy, up_copy, down_copy) in zip(pieces, copies):
        gate_copy.wait()
        gate = jnp.dot(rows_v[...], gate_v[:, here], preferred_element_type=F32)
        up_copy.wait()
        up = jnp.dot(rows_v[...], up_v[:, here], preferred_element_type=F32)
        down_copy.wait()
        grad_hidden = jnp.dot(grad_v[...], down_v[:, here], preferred_element_type=F32)
        sigmoid = jax.nn.sigmoid(gate)
        silu = gate * sigmoid
        acts_ref[2, :, here] = (silu * up).astype(LOW)
        acts_ref[1, :, here] = (grad_hidden * silu).astype(LOW)
        acts_ref[0, :, here] = (
            grad_hidden * up * sigmoid * (1.0 + gate * (1.0 - sigmoid))
        ).astype(LOW)
    width = rows_v.shape[1]
    tall = 1024
    for lo in range(0, width, tall):
        some = slice(lo, lo + tall)
        back_ref[:, some] = (
            contract(acts_ref[0], gate_v[some, :], 1, 1)
            + contract(acts_ref[1], up_v[some, :], 1, 1)
        ).astype(LOW)


def feed(rows, grads, weight):
    count = len(rows)
    tokens, width = rows[0].shape
    units = weight.shape[2]
    half = units // 256 * 128 + 128
    pieces = [slice(0, half), slice(half, units)] if units % 128 == 0 else [slice(0, units)]
    vmem = pl.BlockSpec(memory_space=pltpu.VMEM)
    anywhere = pl.BlockSpec(memory_space=pl.ANY)
    total = count * tokens
    return pl.pallas_call(
        functools.partial(feed_kernel, pieces, count),
        in_specs=[vmem] * (2 * count) + [anywhere],
        out_specs=[vmem, vmem],
        out_shape=[
            jax.ShapeDtypeStruct((3, total, units), LOW),
            jax.ShapeDtypeStruct((total, width), LOW),
        ],
        scratch_shapes=[
            pltpu.VMEM((width, units), LOW),
            pltpu.VMEM((width, units), LOW),
            pltpu.VMEM((width, units), LOW),
            pltpu.VMEM((total, width), LOW),
            pltpu.VMEM((total, width), LOW),
            pltpu.SemaphoreType.DMA((3, len(pieces))),
        ],
        compiler_params=pltpu.CompilerParams(vmem_limit_bytes=VMEM_LIMIT),
        cost_estimate=lasting(1.0),
        name="feed",
    )(*rows, *grads, weight)


def feed_grad_kernel(halves, n, *refs):
    acts, rows = refs[:halves], refs[halves : halves + n]
    out_ref, left, right = refs[-3:]
    tokens = rows[0].shape[1]

    @pl.when(pl.program_id(1) == 0)
    def _():
        at = 0
        for act in acts:
            right[at : at + act.shape[1], :] = act[0]
            at += act.shape[1]

    for s in range(n):
        left[:, s * tokens : (s + 1) * tokens] = rows[s][...]
    out_ref[0] = jnp.dot(left[...], right[...], preferred_element_type=F32).astype(LOW)


def feed_grad(acts, rows_t, first, parts, base=None):
    n, halves = len(rows_t), len(acts)
    width, tokens = rows_t[0].shape
    units = acts[0].shape[2]
    tall = 1024
    in_specs = [
        pl.BlockSpec((1, act.shape[1], units), lambda p, r: (first + p, 0, 0)) for act in acts
    ]
    in_specs += [pl.BlockSpec((tall, tokens), lambda p, r: (r, 0))] * n
    args, aliases = list(acts) + list(rows_t), {}
    if base is not None:
        in_specs.append(pl.BlockSpec(memory_space=pl.ANY))
        aliases = {len(args): 0}
        args.append(base)
    return pl.pallas_call(
        functools.partial(feed_grad_kernel, halves, n),
        grid=(parts, width // tall),
        in_specs=in_specs,
        out_specs=pl.BlockSpec((1, tall, units), lambda p, r: (first + p, r, 0)),
        out_shape=jax.ShapeDtypeStruct((3, width, units), LOW),
        scratch_shapes=[
            pltpu.VMEM((tall, n * tokens), LOW),
            pltpu.VMEM((n * tokens, units), LOW),
        ],
        input_output_aliases=aliases,
        compiler_params=pltpu.CompilerParams(vmem_limit_bytes=VMEM_LIMIT),
        cost_estimate=lasting(1.0),
        name="feed_grad",
    )(*args)


def adamw_turned_kernel(rate, weight, first, second, grad, first_out, second_out, weight_out):
    first_out[...], second_out[...], weight_out[...] = adamw(
        weight[...], first[...], second[...], grad[...].astype(F32).T, rate, DECAY
    )


def adamw_turned(weight, first, second, grad, rate):
    rows, cols = weight.shape
    tall = 128 if rows % 128 == 0 else rows
    block = pl.BlockSpec((tall, cols), lambda i: (i, 0))
    return tuple(
        pl.pallas_call(
            functools.partial(adamw_turned_kernel, rate),
            grid=(rows // tall,),
            in_specs=[block] * 3 + [pl.BlockSpec((cols, tall), lambda i: (0, i))],
            out_specs=[block] * 3,
            out_shape=[jax.ShapeDtypeStruct(weight.shape, F32)] * 3,
            compiler_params=pltpu.CompilerParams(vmem_limit_bytes=VMEM_LIMIT),
            cost_estimate=pl.CostEstimate(
                flops=12 * rows * cols, bytes_accessed=28 * rows * cols, transcendentals=0
            ),
            name="adamw_turned",
        )(weight, first, second, grad)
    )


def on_device(
    sizes,
    tokens,
    positions,
    cotangent,
    query_weight,
    query_first,
    query_second,
    keyval_weight,
    keyval_first,
    keyval_second,
    output_weight,
    output_first,
    output_second,
    gateup_weight,
    gateup_first,
    gateup_second,
    down_weight,
    down_first,
    down_second,
    gains,
    gains_first,
    gains_second,
):
    n = sizes["tensor"]
    rank = lax.axis_index("tensor")
    offsets = ring_offsets(n)
    chunk_ids = [(rank + off + n) % n for off in offsets]
    rows, width = tokens.shape
    piece = keyval_weight.shape[1]
    block, cols = query_weight.shape

    ids = jnp.stack(chunk_ids).astype(jnp.int32)
    first_slots = ring_gather(first_pack(query_weight, keyval_weight, gains), n)
    attn_in = first_join(ids, first_slots, block, piece)
    feed_in = jnp.concatenate(
        [gateup_weight.astype(LOW), down_weight.T.astype(LOW)[None]], 0
    )
    attn_in, feed_in = after(attn_in, feed_in)
    attn_low = lax.all_gather(attn_in, "dp", axis=0, tiled=True)
    output_piece, _ = after(output_weight.T.astype(LOW), first_slots)
    output_slots = ring_gather(output_piece, n)
    grad_start, _ = after(cotangent, output_slots)
    grad_slots = ring_gather(grad_start, n, 1)
    feed_in, _ = after(feed_in, output_slots)
    feed_low = lax.all_gather(feed_in, "dp", axis=1, tiled=True)
    out_halves = dp_spread(
        jnp.concatenate(output_slots, 1), sizes["dp"], (attn_low, grad_slots)
    )
    out_order = jnp.concatenate([dp_order(sizes["dp"], block, odd) for odd in (0, 1)])

    span = H * HD + 2 * KVD
    own_positions = lax.dynamic_slice_in_dim(positions, rank * rows, rows, 0)
    freqs = 10000.0 ** (-jnp.arange(0, HD, 2, dtype=F32) / HD)
    angles = freqs[:, None] * own_positions.astype(F32)[None, :]
    cosine, sine = lax.optimization_barrier((jnp.cos(angles), jnp.sin(angles)))
    x = tokens.astype(F32)
    kv_t, first_normalized, gain_rows, first_inverse = begin(tokens, attn_low, cosine, sine)
    first_gain, second_gain = gain_rows[:1], gain_rows[1:2]
    q_t = project(first_normalized, attn_low, cosine, sine)
    kv_slots = jnp.stack(ring_gather(kv_t, n))
    grad_slots, kv_slots = after(grad_slots, kv_slots)
    grad_slots = ring_gather(grad_start, n, n, grad_slots)
    per_block = H // n
    meta = jnp.stack(
        [c * rows for c in chunk_ids]
        + [(c * per_block) // GROUP for c in chunk_ids]
        + [rank * rows]
    ).astype(jnp.int32)
    meta = jnp.concatenate([meta, out_order])
    pos_row = own_positions[None, :]
    mixed_t, mixed, lse = attend(meta, pos_row, q_t, kv_slots, n)
    out_halves, _ = after(out_halves, (mixed, grad_slots))
    out_pieces = out_halves + [swap(held, sizes["dp"], 1) for held in out_halves]
    residual, second_normalized, second_inverse = mix(
        out_order, mixed, tokens, second_gain, out_pieces
    )
    second_normalized, grad_slots = after(second_normalized, grad_slots)

    rows_slots = ring_gather(second_normalized, n, 1)
    grads_t = [turned(x) for x in grad_slots]
    groups = [[s for s in range(n) if abs(offsets[s]) == k] for k in range(n // 2 + 1)]
    order = sum(groups, [])
    rows_t, acts, part_slots, last = [None] * n, [], [None] * n, [grads_t]
    for k, group in enumerate(groups):
        if k == 2:
            rows_slots = ring_gather(second_normalized, n, n, rows_slots)
        chunks, _ = after([rows_slots[s] for s in group], last)
        for i, s in enumerate(group):
            rows_t[s] = turned(chunks[i])
        if k + 1 < len(groups):
            chunks, _ = after(chunks, [rows_t[s] for s in group])
        act, part = feed(chunks, [grad_slots[s] for s in group], feed_low)
        acts.append(act)
        last = part
        for i, s in enumerate(group):
            part_slots[s] = part[i * rows : (i + 1) * rows]
        if k == 0:
            for s in groups[1]:
                rows_slots[s], _ = after(rows_slots[s], part)
    acts, _ = after(acts, last)
    grad_mlp = feed_grad(acts, [rows_t[s] for s in order], 0, 2)
    from_left = ring_way(part_slots, n, 1)
    passed = []
    from_right = ring_way(part_slots, n, -1, passed, grad_mlp[0, :8, :128])
    acts, _ = after(acts, passed)
    grad_mlp = feed_grad(acts, [grads_t[s] for s in order], 2, 1, grad_mlp)
    second_grad = ring_sum(part_slots[0], from_left, from_right)
    mlp_parts = [contract(act[2], feed_low[2], 1, 1).astype(LOW) for act in acts]
    second_grad, (_, mlp_parts) = after(second_grad, (grad_mlp, mlp_parts))
    owned_mlp = lax.psum_scatter(grad_mlp, "dp", scatter_dimension=1, tiled=True)

    second_unit = residual * second_inverse
    residual_grad = cotangent.astype(F32) + norm_backward(
        second_grad, second_unit, second_inverse, second_gain
    )
    second_gain_grad = jnp.sum(second_grad * second_unit, 0)
    back = residual_grad.astype(LOW)
    mlp_slots = [None] * n
    for group, part in zip(groups, mlp_parts):
        for i, s in enumerate(group):
            mlp_slots[s] = part[i * rows : (i + 1) * rows]
    block_far, block_left = ring_most(mlp_slots, n), ring_way(mlp_slots, n, 1)
    grad_q_t, grad_kv = attend_back(
        meta, pos_row, q_t, kv_slots, back, out_pieces, mixed_t, lse, cosine, sine, n
    )
    (grad_q_t, grad_kv), _ = after((grad_q_t, grad_kv), (block_far, block_left))

    places = [dp_order(sizes["dp"], block, odd) for odd in (0, 1)]
    kv_parts = [grad_kv[s] for s in range(n)]
    kv_left = ring_way(kv_parts, n, 1)
    block_right = ring_last(mlp_slots, n, block_far, grad_kv)
    kv_far = ring_most(kv_parts, n)
    own_kv = ring_sum(kv_parts[0], ring_last(kv_parts, n, kv_far, block_right), kv_left)
    query_rows, _ = after(first_normalized, kv_far)
    partner = weight_grad(
        query_rows, grad_q_t, n * cols, cols, n, lambda i: i, lambda i: i, places[1]
    )
    partner = swap(partner, sizes["dp"], 1)
    out_rows, _ = after(back, grad_q_t)
    heads_cols = H * HD // (2 * KVD)
    grad_pack = weight_grad(
        out_rows, mixed_t, span, 2 * KVD, heads_cols, lambda i: i, lambda i: i
    )

    grad_k = own_kv[:KVD].reshape(KVH, 2, HD // 2, rows)
    upper, lower = grad_k[:, 0], grad_k[:, 1]
    grad_k = jnp.stack([upper * cosine + lower * sine, lower * cosine - upper * sine], 1)
    grad_kv_t = jnp.concatenate(
        [grad_k.reshape(KVD, rows).astype(LOW), own_kv[KVD:].astype(LOW)], 0
    )
    grad_pack = weight_grad(
        first_normalized, grad_kv_t, span, 2 * KVD, 1, lambda i: 0, lambda i: heads_cols,
        None, grad_pack,
    )
    grad_pack, owned_mlp = after(grad_pack, owned_mlp)
    owned_pack = lax.psum_scatter(grad_pack, "dp", scatter_dimension=0, tiled=True)

    query_slots, last = [None] * n, grad_pack
    for s in order[::-1]:
        query_rows, _ = after(first_normalized, last)
        last = query_slots[s] = weight_grad(
            query_rows, grad_q_t, cols, cols, 1, lambda i, s=s: s, lambda i: 0, places[0], None,
            partner, lambda i, s=s: s,
        )
    query_far, query_left = ring_most(query_slots, n), ring_way(query_slots, n, 1)
    owned_gateup, owned_down = owned_mlp[:2], owned_mlp[2]
    gateup_up = adamw(
        gateup_weight, gateup_first, gateup_second, owned_gateup.astype(F32), RATE_GATEUP, DECAY
    )
    down_up = adamw_turned(down_weight, down_first, down_second, owned_down, RATE_DOWN)
    query_right = ring_last(query_slots, n, query_far, (gateup_up, down_up))
    query_sum = ring_sum(query_slots[0], query_left, query_right).astype(LOW)
    block_out = residual + ring_sum(mlp_slots[0], block_left, block_right)
    (back_q_t, back_kv_t), _ = after((grad_q_t, grad_kv_t), query_slots)
    grad_qkv_t = jnp.concatenate(
        [back_q_t, back_kv_t, jnp.zeros((attn_low.shape[1] - span, rows), LOW)], 0
    )
    first_grad = contract(grad_qkv_t, attn_low, 0, 1)
    first_unit = x * first_inverse
    first_gain_grad = jnp.sum(first_grad * first_unit, 0)
    layer_input_gradient = residual_grad + norm_backward(
        first_grad, first_unit, first_inverse, first_gain
    )
    gain_grads, bit = jnp.stack([first_gain_grad, second_gain_grad]), 1
    while bit < sizes["dp"]:
        gain_grads = gain_grads + swap(gain_grads, sizes["dp"], bit)
        bit *= 2
    gain_grads = lax.dynamic_slice_in_dim(gain_grads, lax.axis_index("dp") * block, block, 1)
    gain_cols = jnp.pad(gain_grads.T, ((0, 0), (0, 126)))

    slots = tail_pack(ids, owned_pack, gain_cols, piece, cols)
    query_sum, _ = after(query_sum, slots[0])
    own_query = dp_scatter(query_sum, sizes["dp"], ()).astype(F32)
    query_up = adamw(query_weight, query_first, query_second, own_query, RATE_QUERY, DECAY)
    parts = [slots[0], ring_way(slots, n, -1), ring_way(slots, n, 1)]
    states = [output_weight, output_first, output_second, keyval_weight, keyval_first]
    states += [keyval_second, gains, gains_first, gains_second]
    parts = [part for part in parts if part is not None]
    last = tail_adamw(parts, states, block, piece)
    output_up, keyval_up, gains_up = tuple(last[:3]), tuple(last[3:6]), tuple(last[6:])
    return (
        (block_out, layer_input_gradient)
        + query_up
        + keyval_up
        + output_up
        + gateup_up
        + down_up
        + gains_up
    )


def solution(mesh):
    rows = P(("dp", "tensor"), None)
    grid = P("dp", "tensor")
    cross = P("tensor", "dp")
    pair = P(None, ("dp", "tensor"), None)
    stacked = P(None, "dp", "tensor")
    narrow = P(None, ("dp", "tensor"))
    states = (grid,) * 3 + (pair,) * 3 + (cross,) * 3 + (stacked,) * 3 + (cross,) * 3 + (narrow,) * 3
    return jax.shard_map(
        functools.partial(on_device, dict(mesh.shape)),
        mesh=mesh,
        in_specs=(rows, P("dp"), rows) + states,
        out_specs=(rows, rows) + states,
        check_vma=False,
    )
```

```python
import functools

import jax
import jax.numpy as jnp
from jax import lax
from jax.experimental import pallas as pl
from jax.experimental.pallas import tpu as pltpu
from jax.sharding import PartitionSpec as P

H = 32
KVH = 4
HD = 64
GROUP = 8
KVD = KVH * HD
STEP = 10
EPS = 1e-05
BETA_ONE = 0.9
BETA_TWO = 0.999
ADAM_EPS = 1e-08
DECAY = 0.1
RATE_QUERY = 0.06
RATE_KEYVAL = 0.06
RATE_OUTPUT = 0.5
RATE_GATEUP = 0.06
RATE_DOWN = 0.04
RATE_GAINS = 1.5
LOW = jnp.bfloat16
F32 = jnp.float32
TALL = 128
VMEM_LIMIT = 56 * 1024 * 1024
LONG = pl.CostEstimate(flops=2 * 10**14, bytes_accessed=10**6, transcendentals=0)


def lasting(us):
    return pl.CostEstimate(flops=int(us * 1.15e9), bytes_accessed=10**6, transcendentals=0)


def contract(left, right, dim_left, dim_right):
    return lax.dot_general(
        left, right, (((dim_left,), (dim_right,)), ((), ())), preferred_element_type=F32
    )


def ring_offsets(n):
    return [0] + [-k for k in range(1, n // 2 + 1)] + [k for k in range(1, (n - 1) // 2 + 1)]


def shift(x, n, by):
    return lax.ppermute(x, "tensor", [(i, (i + by) % n) for i in range(n)])


def ring_gather(x, n, steps=None, known=None):
    slots, used = [x], 1
    for by, hops in ((1, n // 2), (-1, (n - 1) // 2)):
        held = x
        for hop in range(hops):
            if steps is not None and hop >= steps:
                slots.append(None)
                continue
            if known is not None and known[used + hop] is not None:
                held = known[used + hop]
            else:
                held = shift(held, n, by)
            slots.append(held)
        used += hops
    return slots


def after(late, early):
    return lax.optimization_barrier((late, early))


def ring_way(slots, n, by, passed=None, hold=None):
    first, hops = (1, n // 2) if by < 0 else (1 + n // 2, (n - 1) // 2)
    held = None
    for k in range(hops, 0, -1):
        part = slots[first + k - 1]
        if held is not None:
            part = (part.astype(F32) + held.astype(F32)).astype(LOW)
            if hold is not None and k == 1:
                part, _ = after(part, hold)
            if passed is not None:
                passed.append(part)
        held = shift(part.astype(LOW), n, by)
    return held


def ring_most(slots, n):
    held = None
    for k in range(n // 2, 1, -1):
        part = slots[k] if held is None else ring_sum(slots[k], held)
        held = shift(part.astype(LOW), n, -1)
    return held


def ring_last(slots, n, held, hold=None):
    part = (slots[1] if held is None else ring_sum(slots[1], held)).astype(LOW)
    if hold is not None:
        part, _ = after(part, hold)
    return shift(part, n, -1)


def ring_sum(own, *arrived):
    total = own.astype(F32)
    for held in arrived:
        if held is not None:
            total = total + held.astype(F32)
    return total


def ring_scatter(slots, n):
    return ring_sum(slots[0], ring_way(slots, n, -1), ring_way(slots, n, 1))


def swap(x, size, bit):
    return lax.ppermute(x, "dp", [(i, i ^ bit) for i in range(size)])


def dp_plan(size, block):
    bits = [1 << i for i in range(1, size.bit_length() - 1)]
    return [bits, bits[::-1]] if block >= 256 else [bits]


def dp_order(size, block, odd):
    plan = dp_plan(size, block)
    me = lax.axis_index("dp")
    places = []
    for h, bits in enumerate(plan):
        partners = [odd]
        for bit in bits:
            partners += [p | bit for p in partners]
        places += [(me ^ p) * len(plan) + h for p in partners]
    return jnp.stack(places).astype(jnp.int32)


def dp_spread(x, size, hold):
    block = x.shape[0]
    plan = dp_plan(size, block)
    tall = block // len(plan)
    even = [x[h * tall : (h + 1) * tall] for h in range(len(plan))]
    for i in range(len(plan[0])):
        got = [swap(held, size, bits[i]) for held, bits in zip(even, plan)]
        even = [jnp.concatenate(pair, 0) for pair in zip(even, got)]
        if i == 0:
            even, _ = after(even, hold)
    return even


def dp_scatter(held, size, hold):
    plan = dp_plan(size, 2 * held.shape[0] // size)
    tall = held.shape[0] // len(plan)
    parts = [held[h * tall : (h + 1) * tall] for h in range(len(plan))]
    for i in reversed(range(len(plan[0]))):
        half = parts[0].shape[0] // 2
        got = [swap(part[half:], size, bits[i]) for part, bits in zip(parts, plan)]
        if i == len(plan[0]) - 1:
            got, _ = after(got, hold)
        parts = [ring_sum(part[:half], new).astype(LOW) for part, new in zip(parts, got)]
    return jnp.concatenate(parts, 0)


def norm_statistics(rows_in):
    inverse = lax.rsqrt(jnp.mean(rows_in * rows_in, -1, keepdims=True) + EPS)
    return rows_in * inverse, inverse


def norm_backward(grad, unit, inverse, gain):
    scaled = grad * gain
    return inverse * (scaled - unit * jnp.mean(scaled * unit, -1, keepdims=True))


def adamw(weight, first, second, grad, rate, decay):
    first_new = BETA_ONE * first + (1.0 - BETA_ONE) * grad
    second_new = BETA_TWO * second + (1.0 - BETA_TWO) * grad * grad
    fix_one = 1.0 - BETA_ONE**STEP
    fix_two = 1.0 - BETA_TWO**STEP
    direction = first_new / fix_one / (jnp.sqrt(second_new / fix_two) + ADAM_EPS)
    return first_new, second_new, weight - rate * (direction + decay * weight)


def turn(values, cosine, sine):
    upper, lower = values[: HD // 2], values[HD // 2 :]
    return jnp.concatenate([upper * cosine - lower * sine, lower * cosine + upper * sine], 0)


def first_pack_kernel(cols, query_ref, keyval_ref, gains_ref, out_ref):
    block, piece = query_ref.shape[0], keyval_ref.shape[1]
    out_ref[block:, :] = jnp.zeros((out_ref.shape[0] - block, cols), LOW)
    out_ref[:block, :] = query_ref[...].astype(LOW)
    row = block
    for lo in range(0, 2 * KVD, cols):
        for j in range(0, cols, KVD):
            at = (lo + j) // KVD
            out_ref[row : row + piece, j : j + KVD] = keyval_ref[at].astype(LOW)
        row += piece
    out_ref[row : row + 2, :piece] = gains_ref[...].astype(LOW)


def first_pack(query, keyval, gains):
    block, cols = query.shape
    piece = keyval.shape[1]
    vmem = pl.BlockSpec(memory_space=pltpu.VMEM)
    height = block + piece * (2 * KVD // cols) + 16
    return pl.pallas_call(
        functools.partial(first_pack_kernel, cols),
        in_specs=[vmem] * 3,
        out_specs=vmem,
        out_shape=jax.ShapeDtypeStruct((height, cols), LOW),
        compiler_params=pltpu.CompilerParams(vmem_limit_bytes=VMEM_LIMIT),
        cost_estimate=lasting(2.0),
        name="first_pack",
    )(query, keyval, gains)


def first_join_kernel(n, piece, ids_ref, *refs):
    slots, out_ref = refs[:n], refs[n]
    block, cols = out_ref.shape[0], slots[0].shape[1]
    span = n * cols + 2 * KVD
    out_ref[:, span:] = jnp.zeros((block, out_ref.shape[1] - span), LOW)
    for s, slot in enumerate(slots):
        at = pl.multiple_of(ids_ref[s] * piece, piece)
        out_ref[:, s * cols : (s + 1) * cols] = slot[:block, :]
        row = block
        for lo in range(n * cols, span, cols):
            out_ref[pl.ds(at, piece), lo : lo + cols] = slot[row : row + piece, :]
            row += piece
        gains = slot[row : row + 16, :128].astype(F32).T.astype(LOW)
        out_ref[pl.ds(at, piece), span : span + 16] = gains[:piece]


def first_join(ids, slots, block, piece):
    n = len(slots)
    cols = slots[0].shape[1]
    width = n * cols + 2 * KVD + 128
    return pl.pallas_call(
        functools.partial(first_join_kernel, n, piece),
        grid_spec=pltpu.PrefetchScalarGridSpec(
            num_scalar_prefetch=1,
            grid=(1,),
            in_specs=[pl.BlockSpec(slots[0].shape, lambda i, o: (0, 0))] * n,
            out_specs=pl.BlockSpec((block, width), lambda i, o: (0, 0)),
        ),
        out_shape=jax.ShapeDtypeStruct((block, width), LOW),
        compiler_params=pltpu.CompilerParams(vmem_limit_bytes=VMEM_LIMIT),
        cost_estimate=lasting(2.0),
        name="first_join",
    )(ids, *slots)


def begin_kernel(
    x_ref, gain_ref, weight_ref, cos_ref, sin_ref, out_ref, rows_ref, gains_ref, inverse_ref
):
    gains = gain_ref[...].astype(F32).T[: gains_ref.shape[0]]
    unit, inverse = norm_statistics(x_ref[...].astype(F32))
    rows = (unit * gains[:1]).astype(LOW)
    rows_ref[...], gains_ref[...], inverse_ref[...] = rows, gains, inverse
    wide = jnp.dot(rows, weight_ref[...], preferred_element_type=F32).T
    cosine, sine = cos_ref[...], sin_ref[...]
    for h in range(KVH):
        here = slice(h * HD, (h + 1) * HD)
        out_ref[here, :] = turn(wide[here], cosine, sine).astype(LOW)
    out_ref[KVD:, :] = wide[KVD:].astype(LOW)


def begin(x, weight, cosine, sine):
    tokens, width = x.shape
    cols = 2 * KVD
    return pl.pallas_call(
        begin_kernel,
        grid=(1,),
        in_specs=[
            pl.BlockSpec((tokens, width), lambda b: (0, 0)),
            pl.BlockSpec((width, TALL), lambda b: (0, (H * HD + cols) // TALL)),
            pl.BlockSpec((width, cols), lambda b: (0, H * HD // cols)),
            pl.BlockSpec(cosine.shape, lambda b: (0, 0)),
            pl.BlockSpec(sine.shape, lambda b: (0, 0)),
        ],
        out_specs=[
            pl.BlockSpec((cols, tokens), lambda b: (0, 0)),
            pl.BlockSpec((tokens, width), lambda b: (0, 0)),
            pl.BlockSpec((8, width), lambda b: (0, 0)),
            pl.BlockSpec((tokens, 1), lambda b: (0, 0)),
        ],
        out_shape=[
            jax.ShapeDtypeStruct((cols, tokens), LOW),
            jax.ShapeDtypeStruct((tokens, width), LOW),
            jax.ShapeDtypeStruct((8, width), F32),
            jax.ShapeDtypeStruct((tokens, 1), F32),
        ],
        compiler_params=pltpu.CompilerParams(vmem_limit_bytes=VMEM_LIMIT),
        cost_estimate=lasting(5.0),
        name="begin",
    )(x, weight, weight, cosine, sine)


def project_kernel(rows_ref, weight_ref, cos_ref, sin_ref, out_ref):
    wide = jnp.dot(rows_ref[...], weight_ref[...], preferred_element_type=F32).T
    cosine, sine = cos_ref[...], sin_ref[...]
    for h in range(wide.shape[0] // HD):
        here = slice(h * HD, (h + 1) * HD)
        out_ref[here, :] = (turn(wide[here], cosine, sine) * HD ** (-0.5)).astype(LOW)


def project(rows, weight, cosine, sine):
    tokens, width = rows.shape
    cols = 2 * KVD
    blocks = H * HD // cols
    return pl.pallas_call(
        project_kernel,
        grid=(blocks,),
        in_specs=[
            pl.BlockSpec((tokens, width), lambda b: (0, 0)),
            pl.BlockSpec((width, cols), lambda b: (0, b)),
            pl.BlockSpec(cosine.shape, lambda b: (0, 0)),
            pl.BlockSpec(sine.shape, lambda b: (0, 0)),
        ],
        out_specs=pl.BlockSpec((cols, tokens), lambda b: (b, 0)),
        out_shape=jax.ShapeDtypeStruct((blocks * cols, tokens), LOW),
        compiler_params=pltpu.CompilerParams(vmem_limit_bytes=VMEM_LIMIT),
        cost_estimate=lasting(8.0),
        name="project",
    )(rows, weight, cosine, sine)


def fill_bias(meta_ref, pos_ref, bias_ref, slots, tokens):
    query = meta_ref[2 * slots] + lax.broadcasted_iota(jnp.int32, (tokens, tokens), 1)
    least = query - pos_ref[...]
    row = lax.broadcasted_iota(jnp.int32, (tokens, tokens), 0)
    for c in range(slots):
        key = meta_ref[c] + row
        bias_ref[c] = jnp.where((key <= query) & (key >= least), 0.0, -1e30)


def attend_kernel(
    slots, heads, meta_ref, pos_ref, q_ref, kv_ref, out_ref, rows_ref, lse_ref, bias_ref
):
    tokens = q_ref.shape[1]
    block = pl.program_id(0)

    @pl.when(block == 0)
    def _():
        fill_bias(meta_ref, pos_ref, bias_ref, slots, tokens)

    start = pl.multiple_of(meta_ref[slots + block] * HD, HD)
    keys = [kv_ref[c, pl.ds(start, HD), :].T for c in range(slots)]
    values = [kv_ref[c, pl.ds(KVD + start, HD), :] for c in range(slots)]
    for h in range(heads):
        query = q_ref[h * HD : (h + 1) * HD, :]
        scores = [
            jnp.dot(keys[c], query, preferred_element_type=F32) + bias_ref[c] for c in range(slots)
        ]
        peak = functools.reduce(jnp.maximum, [jnp.max(s, 0, keepdims=True) for s in scores])
        total = jnp.zeros_like(peak)
        mixed = jnp.zeros((HD, tokens), F32)
        for c in range(slots):
            expo = jnp.exp(scores[c] - peak)
            total = total + jnp.sum(expo, 0, keepdims=True)
            mixed = mixed + jnp.dot(values[c], expo.astype(LOW), preferred_element_type=F32)
        out_ref[h * HD : (h + 1) * HD, :] = (mixed / total).astype(LOW)
        lse_ref[0, h : h + 1, :] = peak + jnp.log(total)
    rows_ref[...] = out_ref[...].T


def attend(meta, pos_row, q_t, kv_slots, slots):
    tokens = q_t.shape[1]
    heads = H // slots
    rows = heads * HD
    return pl.pallas_call(
        functools.partial(attend_kernel, slots, heads),
        grid_spec=pltpu.PrefetchScalarGridSpec(
            num_scalar_prefetch=1,
            grid=(slots,),
            in_specs=[
                pl.BlockSpec((1, tokens), lambda b, m: (0, 0)),
                pl.BlockSpec((rows, tokens), lambda b, m: (b, 0)),
                pl.BlockSpec((slots, 2 * KVD, tokens), lambda b, m: (0, 0, 0)),
            ],
            out_specs=[
                pl.BlockSpec((rows, tokens), lambda b, m: (b, 0)),
                pl.BlockSpec((tokens, rows), lambda b, m: (0, b)),
                pl.BlockSpec((1, heads, tokens), lambda b, m: (b, 0, 0)),
            ],
            scratch_shapes=[pltpu.VMEM((slots, tokens, tokens), F32)],
        ),
        out_shape=[
            jax.ShapeDtypeStruct((H * HD, tokens), LOW),
            jax.ShapeDtypeStruct((tokens, H * HD), LOW),
            jax.ShapeDtypeStruct((slots, heads, tokens), F32),
        ],
        compiler_params=pltpu.CompilerParams(vmem_limit_bytes=VMEM_LIMIT),
        cost_estimate=pl.CostEstimate(
            flops=16 * H * HD * tokens * tokens * slots,
            bytes_accessed=4 * H * HD * tokens,
            transcendentals=H * tokens * tokens * slots,
        ),
        name="attend",
    )(meta, pos_row, q_t, kv_slots)


def attend_back_kernel(slots, heads, count, meta_ref, pos_ref, q_ref, kv_ref, back_ref, *refs):
    weights, refs = refs[:count], refs[count:]
    o_ref, lse_ref, cos_ref, sin_ref, dq_ref, dkv_out_ref = refs[:6]
    bias_ref, dkv_ref, do_ref, moved_ref = refs[6:]
    tokens = q_ref.shape[1]
    block = pl.program_id(0)

    @pl.when(block == 0)
    def _():
        fill_bias(meta_ref, pos_ref, bias_ref, slots, tokens)
        dkv_ref[...] = jnp.zeros_like(dkv_ref)
        for i in range(back_ref.shape[1] // TALL):
            at = pl.multiple_of(meta_ref[2 * slots + 1 + i] * TALL, TALL)
            moved_ref[:, i * TALL : (i + 1) * TALL] = back_ref[:, pl.ds(at, TALL)]

    grad_mixed, at = 0.0, 0
    for weight in weights:
        here = slice(at, at + weight.shape[0])
        grad_mixed += jnp.dot(moved_ref[:, here], weight[...], preferred_element_type=F32)
        at += weight.shape[0]
    do_ref[...] = grad_mixed.T.astype(LOW)
    start = pl.multiple_of(meta_ref[slots + block] * HD, HD)
    keys_t = [kv_ref[c, pl.ds(start, HD), :] for c in range(slots)]
    keys = [k.T for k in keys_t]
    values = [kv_ref[c, pl.ds(KVD + start, HD), :].T for c in range(slots)]
    cosine, sine = cos_ref[...], -sin_ref[...]
    grad_keys = [jnp.zeros((HD, tokens), F32) for _ in range(slots)]
    grad_values = [jnp.zeros((HD, tokens), F32) for _ in range(slots)]
    for h in range(heads):
        here = slice(h * HD, (h + 1) * HD)
        query, grad = q_ref[here, :], do_ref[here, :]
        delta = jnp.sum(grad.astype(F32) * o_ref[here, :].astype(F32), 0, keepdims=True)
        log_total = lse_ref[0, h : h + 1, :]
        grad_query = jnp.zeros((HD, tokens), F32)
        for c in range(slots):
            scores = jnp.dot(keys[c], query, preferred_element_type=F32) + bias_ref[c]
            prob = jnp.exp(scores - log_total)
            grad_prob = jnp.dot(values[c], grad, preferred_element_type=F32)
            grad_score = (prob * (grad_prob - delta)).astype(LOW)
            grad_values[c] = grad_values[c] + contract(grad, prob.astype(LOW), 1, 1)
            grad_keys[c] = grad_keys[c] + contract(query, grad_score, 1, 1)
            grad_query = grad_query + jnp.dot(keys_t[c], grad_score, preferred_element_type=F32)
        dq_ref[here, :] = (turn(grad_query, cosine, sine) * HD ** (-0.5)).astype(LOW)
    for c in range(slots):
        dkv_ref[c, pl.ds(start, HD), :] += grad_keys[c]
        dkv_ref[c, pl.ds(KVD + start, HD), :] += grad_values[c]

    @pl.when(block == pl.num_programs(0) - 1)
    def _():
        dkv_out_ref[...] = dkv_ref[...].astype(LOW)


def attend_back(meta, pos_row, q_t, kv_slots, back, weights, o_t, lse, cosine, sine, slots):
    tokens = q_t.shape[1]
    heads = H // slots
    rows = heads * HD
    head_block = pl.BlockSpec((rows, tokens), lambda b, m: (b, 0))
    table = pl.BlockSpec(cosine.shape, lambda b, m: (0, 0))
    whole = pl.BlockSpec((slots, 2 * KVD, tokens), lambda b, m: (0, 0, 0))
    return pl.pallas_call(
        functools.partial(attend_back_kernel, slots, heads, len(weights)),
        grid_spec=pltpu.PrefetchScalarGridSpec(
            num_scalar_prefetch=1,
            grid=(slots,),
            in_specs=[
                pl.BlockSpec((1, tokens), lambda b, m: (0, 0)),
                head_block,
                whole,
                pl.BlockSpec(back.shape, lambda b, m: (0, 0)),
                *[pl.BlockSpec((w.shape[0], rows), lambda b, m: (0, b)) for w in weights],
                head_block,
                pl.BlockSpec((1, heads, tokens), lambda b, m: (b, 0, 0)),
                table,
                table,
            ],
            out_specs=[head_block, whole],
            scratch_shapes=[
                pltpu.VMEM((slots, tokens, tokens), F32),
                pltpu.VMEM((slots, 2 * KVD, tokens), F32),
                pltpu.VMEM((rows, tokens), LOW),
                pltpu.VMEM(back.shape, LOW),
            ],
        ),
        out_shape=[
            jax.ShapeDtypeStruct((H * HD, tokens), LOW),
            jax.ShapeDtypeStruct((slots, 2 * KVD, tokens), LOW),
        ],
        compiler_params=pltpu.CompilerParams(vmem_limit_bytes=VMEM_LIMIT),
        cost_estimate=LONG,
        name="attend_back",
    )(meta, pos_row, q_t, kv_slots, back, *weights, o_t, lse, cosine, sine)


def mix_kernel(count, order_ref, o_ref, x_ref, gain_ref, *refs):
    weights, (h_ref, n_ref, inverse_ref) = refs[:count], refs[count : count + 3]
    held, sems = refs[count + 3 : -1], refs[-1]
    copies = [
        pltpu.make_async_copy(src, dst, sems.at[i]) for i, (src, dst) in enumerate(zip(weights, held))
    ]
    for copy in copies:
        copy.start()
    at = 0
    for copy, weight in zip(copies, held):
        copy.wait()
        mixed = contract(o_ref[...], weight[...], 1, 1)
        for i in range(weight.shape[0] // TALL):
            here = pl.ds(pl.multiple_of(order_ref[at] * TALL, TALL), TALL)
            h_ref[:, here] = x_ref[:, here].astype(F32) + mixed[:, i * TALL : (i + 1) * TALL]
            at += 1
    unit, inverse = norm_statistics(h_ref[...])
    n_ref[...] = (unit * gain_ref[...]).astype(LOW)
    inverse_ref[...] = inverse


def mix(order, o, x, gain, weights):
    tokens, width = x.shape
    count = len(weights)
    full = pl.BlockSpec((tokens, width), lambda i, o: (0, 0))
    return pl.pallas_call(
        functools.partial(mix_kernel, count),
        grid_spec=pltpu.PrefetchScalarGridSpec(
            num_scalar_prefetch=1,
            grid=(1,),
            in_specs=[
                pl.BlockSpec(o.shape, lambda i, o: (0, 0)),
                full,
                pl.BlockSpec((1, width), lambda i, o: (0, 0)),
            ]
            + [pl.BlockSpec(memory_space=pl.ANY)] * count,
            out_specs=[full, full, pl.BlockSpec((tokens, 1), lambda i, o: (0, 0))],
            scratch_shapes=[pltpu.VMEM(weight.shape, LOW) for weight in weights]
            + [pltpu.SemaphoreType.DMA((count,))],
        ),
        out_shape=[
            jax.ShapeDtypeStruct((tokens, width), F32),
            jax.ShapeDtypeStruct((tokens, width), LOW),
            jax.ShapeDtypeStruct((tokens, 1), F32),
        ],
        compiler_params=pltpu.CompilerParams(vmem_limit_bytes=VMEM_LIMIT),
        cost_estimate=lasting(6.0),
        name="mix",
    )(order, o, x, gain, *weights)


def tail_pack_kernel(n, piece, cols, ids_ref, owned_ref, gain_ref, *outs):
    block, start = owned_ref.shape[0], H * HD
    span = start + 2 * KVD
    for s, out_ref in enumerate(outs):
        at = pl.multiple_of(ids_ref[s] * piece, piece)
        out_ref[:block, :] = owned_ref[:, s * cols : (s + 1) * cols]
        row = block
        for lo in range(start, span, cols):
            out_ref[row : row + piece, :] = owned_ref[pl.ds(at, piece), lo : lo + cols]
            row += piece
        gains = gain_ref[pl.ds(at, piece), :].T.astype(LOW)
        out_ref[row:, :] = jnp.zeros((16, cols), LOW)
        out_ref[row : row + 16, :piece] = gains[:16]


def tail_pack(ids, owned, gain_cols, piece, cols):
    n, block = ids.shape[0], owned.shape[0]
    height = block + piece * (2 * KVD // cols) + 16
    return pl.pallas_call(
        functools.partial(tail_pack_kernel, n, piece, cols),
        grid_spec=pltpu.PrefetchScalarGridSpec(
            num_scalar_prefetch=1,
            grid=(1,),
            in_specs=[
                pl.BlockSpec(owned.shape, lambda i, o: (0, 0)),
                pl.BlockSpec(gain_cols.shape, lambda i, o: (0, 0)),
            ],
            out_specs=[pl.BlockSpec((height, cols), lambda i, o: (0, 0))] * n,
        ),
        out_shape=[jax.ShapeDtypeStruct((height, cols), LOW)] * n,
        compiler_params=pltpu.CompilerParams(vmem_limit_bytes=VMEM_LIMIT),
        cost_estimate=lasting(2.0),
        name="tail_pack",
    )(ids, owned, gain_cols)


def tail_adamw_kernel(block, piece, parts, *refs):
    total = ring_sum(*[ref[...] for ref in refs[:parts]])
    states, outs = refs[parts : parts + 9], refs[parts + 9 :]
    groups = 2 * KVD // total.shape[1]
    keyval = [total[block + g * piece : block + (g + 1) * piece] for g in range(groups)]
    weight, first, second = states[:3]
    outs[0][...], outs[1][...], outs[2][...] = adamw(
        weight[...], first[...], second[...], total[:block].T, RATE_OUTPUT, DECAY
    )
    weight, first, second = states[3:6]
    for j in range(2):
        if groups == 1:
            grad = keyval[0][:, j * KVD : (j + 1) * KVD]
        else:
            grad = jnp.concatenate(keyval[j * groups // 2 : (j + 1) * groups // 2], 1)
        outs[3][j], outs[4][j], outs[5][j] = adamw(
            weight[j], first[j], second[j], grad, RATE_KEYVAL, DECAY
        )
    weight, first, second = states[6:]
    outs[6][...], outs[7][...], outs[8][...] = adamw(
        weight[...], first[...], second[...], total[-16:, :piece][:2], RATE_GAINS, 0.0
    )


def tail_adamw(parts, states, block, piece):
    vmem = pl.BlockSpec(memory_space=pltpu.VMEM)
    shapes = [states[3 * i].shape for i in range(3) for _ in range(3)]
    return pl.pallas_call(
        functools.partial(tail_adamw_kernel, block, piece, len(parts)),
        in_specs=[vmem] * (len(parts) + 9),
        out_specs=[vmem] * 9,
        out_shape=[jax.ShapeDtypeStruct(shape, F32) for shape in shapes],
        compiler_params=pltpu.CompilerParams(vmem_limit_bytes=VMEM_LIMIT),
        cost_estimate=lasting(3.0),
        name="tail_adamw",
    )(*parts, *states)


def weight_grad_kernel(count, summed, order_ref, rows_ref, x_ref, *rest):
    out_ref, left = rest[-2:]
    tall = left.shape[0] // count

    @pl.when(pl.program_id(0) == 0)
    def _():
        for i in range(count):
            start = pl.multiple_of(order_ref[i] * tall, tall)
            left[i * tall : (i + 1) * tall, :] = rows_ref[:, pl.ds(start, tall)].T

    grad = contract(left[...], x_ref[...], 1, 1)
    if summed:
        grad = grad + rest[0][...].astype(F32)
    out_ref[...] = grad.astype(LOW)


def weight_grad(
    rows, x_t, total, wide, steps, source, target, order=None, base=None, add=None, place=None
):
    tokens, width = rows.shape
    if order is None:
        order = jnp.arange(width // TALL, dtype=jnp.int32)
    count = order.shape[0]
    out_spec = pl.BlockSpec((count * TALL, wide), lambda i, o: (0, target(i)))
    in_specs = [
        pl.BlockSpec((tokens, width), lambda i, o: (0, 0)),
        pl.BlockSpec((wide, tokens), lambda i, o: (source(i), 0)),
    ]
    args, aliases = [order, rows, x_t], {}
    if add is not None:
        in_specs.append(pl.BlockSpec((count * TALL, wide), lambda i, o: (0, place(i))))
        args.append(add)
    if base is not None:
        in_specs.append(pl.BlockSpec(memory_space=pl.ANY))
        aliases = {len(args): 0}
        args.append(base)
    return pl.pallas_call(
        functools.partial(weight_grad_kernel, count, add is not None),
        grid_spec=pltpu.PrefetchScalarGridSpec(
            num_scalar_prefetch=1,
            grid=(steps,),
            in_specs=in_specs,
            out_specs=out_spec,
            scratch_shapes=[pltpu.VMEM((count * TALL, tokens), LOW)],
        ),
        out_shape=jax.ShapeDtypeStruct((count * TALL, total), LOW),
        input_output_aliases=aliases,
        compiler_params=pltpu.CompilerParams(vmem_limit_bytes=VMEM_LIMIT),
        cost_estimate=lasting(steps * wide * count / 4800),
        name="weight_grad",
    )(*args)


def turned_kernel(x_ref, out_ref):
    out_ref[...] = x_ref[...].T


def turned(x):
    vmem = pl.BlockSpec(memory_space=pltpu.VMEM)
    return pl.pallas_call(
        turned_kernel,
        in_specs=[vmem],
        out_specs=vmem,
        out_shape=jax.ShapeDtypeStruct(x.shape[::-1], x.dtype),
        compiler_params=pltpu.CompilerParams(vmem_limit_bytes=VMEM_LIMIT),
        cost_estimate=lasting(1.5),
        name="turned",
    )(x)


def feed_kernel(pieces, count, *refs):
    rows_refs, grad_refs = refs[:count], refs[count : 2 * count]
    weight_ref, acts_ref, back_ref = refs[2 * count : 2 * count + 3]
    gate_v, up_v, down_v, rows_v, grad_v, sems = refs[2 * count + 3 :]
    copies = []
    for i, here in enumerate(pieces):
        copies.append(
            [
                pltpu.make_async_copy(weight_ref.at[j, :, here], held.at[:, here], sems.at[j, i])
                for j, held in enumerate((gate_v, up_v, down_v))
            ]
        )
        for copy in copies[-1]:
            copy.start()
    tokens = rows_refs[0].shape[0]
    for s in range(count):
        rows_v[s * tokens : (s + 1) * tokens, :] = rows_refs[s][...]
        grad_v[s * tokens : (s + 1) * tokens, :] = grad_refs[s][...]
    for here, (gate_copy, up_copy, down_copy) in zip(pieces, copies):
        gate_copy.wait()
        gate = jnp.dot(rows_v[...], gate_v[:, here], preferred_element_type=F32)
        up_copy.wait()
        up = jnp.dot(rows_v[...], up_v[:, here], preferred_element_type=F32)
        down_copy.wait()
        grad_hidden = jnp.dot(grad_v[...], down_v[:, here], preferred_element_type=F32)
        sigmoid = jax.nn.sigmoid(gate)
        silu = gate * sigmoid
        acts_ref[2, :, here] = (silu * up).astype(LOW)
        acts_ref[1, :, here] = (grad_hidden * silu).astype(LOW)
        acts_ref[0, :, here] = (
            grad_hidden * up * sigmoid * (1.0 + gate * (1.0 - sigmoid))
        ).astype(LOW)
    width = rows_v.shape[1]
    tall = 1024
    for lo in range(0, width, tall):
        some = slice(lo, lo + tall)
        back_ref[:, some] = (
            contract(acts_ref[0], gate_v[some, :], 1, 1)
            + contract(acts_ref[1], up_v[some, :], 1, 1)
        ).astype(LOW)


def feed(rows, grads, weight):
    count = len(rows)
    tokens, width = rows[0].shape
    units = weight.shape[2]
    half = units // 256 * 128 + 128
    pieces = [slice(0, half), slice(half, units)] if units % 128 == 0 else [slice(0, units)]
    vmem = pl.BlockSpec(memory_space=pltpu.VMEM)
    anywhere = pl.BlockSpec(memory_space=pl.ANY)
    total = count * tokens
    return pl.pallas_call(
        functools.partial(feed_kernel, pieces, count),
        in_specs=[vmem] * (2 * count) + [anywhere],
        out_specs=[vmem, vmem],
        out_shape=[
            jax.ShapeDtypeStruct((3, total, units), LOW),
            jax.ShapeDtypeStruct((total, width), LOW),
        ],
        scratch_shapes=[
            pltpu.VMEM((width, units), LOW),
            pltpu.VMEM((width, units), LOW),
            pltpu.VMEM((width, units), LOW),
            pltpu.VMEM((total, width), LOW),
            pltpu.VMEM((total, width), LOW),
            pltpu.SemaphoreType.DMA((3, len(pieces))),
        ],
        compiler_params=pltpu.CompilerParams(vmem_limit_bytes=VMEM_LIMIT),
        cost_estimate=lasting(1.0),
        name="feed",
    )(*rows, *grads, weight)


def feed_grad_kernel(halves, n, *refs):
    acts, rows = refs[:halves], refs[halves : halves + n]
    out_ref, left, right = refs[-3:]
    tokens = rows[0].shape[1]

    @pl.when(pl.program_id(1) == 0)
    def _():
        at = 0
        for act in acts:
            right[at : at + act.shape[1], :] = act[0]
            at += act.shape[1]

    for s in range(n):
        left[:, s * tokens : (s + 1) * tokens] = rows[s][...]
    out_ref[0] = jnp.dot(left[...], right[...], preferred_element_type=F32).astype(LOW)


def feed_grad(acts, rows_t, first, parts, base=None):
    n, halves = len(rows_t), len(acts)
    width, tokens = rows_t[0].shape
    units = acts[0].shape[2]
    tall = 1024
    in_specs = [
        pl.BlockSpec((1, act.shape[1], units), lambda p, r: (first + p, 0, 0)) for act in acts
    ]
    in_specs += [pl.BlockSpec((tall, tokens), lambda p, r: (r, 0))] * n
    args, aliases = list(acts) + list(rows_t), {}
    if base is not None:
        in_specs.append(pl.BlockSpec(memory_space=pl.ANY))
        aliases = {len(args): 0}
        args.append(base)
    return pl.pallas_call(
        functools.partial(feed_grad_kernel, halves, n),
        grid=(parts, width // tall),
        in_specs=in_specs,
        out_specs=pl.BlockSpec((1, tall, units), lambda p, r: (first + p, r, 0)),
        out_shape=jax.ShapeDtypeStruct((3, width, units), LOW),
        scratch_shapes=[
            pltpu.VMEM((tall, n * tokens), LOW),
            pltpu.VMEM((n * tokens, units), LOW),
        ],
        input_output_aliases=aliases,
        compiler_params=pltpu.CompilerParams(vmem_limit_bytes=VMEM_LIMIT),
        cost_estimate=lasting(1.0),
        name="feed_grad",
    )(*args)


def adamw_turned_kernel(rate, weight, first, second, grad, first_out, second_out, weight_out):
    first_out[...], second_out[...], weight_out[...] = adamw(
        weight[...], first[...], second[...], grad[...].astype(F32).T, rate, DECAY
    )


def adamw_turned(weight, first, second, grad, rate):
    rows, cols = weight.shape
    tall = 128 if rows % 128 == 0 else rows
    block = pl.BlockSpec((tall, cols), lambda i: (i, 0))
    return tuple(
        pl.pallas_call(
            functools.partial(adamw_turned_kernel, rate),
            grid=(rows // tall,),
            in_specs=[block] * 3 + [pl.BlockSpec((cols, tall), lambda i: (0, i))],
            out_specs=[block] * 3,
            out_shape=[jax.ShapeDtypeStruct(weight.shape, F32)] * 3,
            compiler_params=pltpu.CompilerParams(vmem_limit_bytes=VMEM_LIMIT),
            cost_estimate=pl.CostEstimate(
                flops=12 * rows * cols, bytes_accessed=28 * rows * cols, transcendentals=0
            ),
            name="adamw_turned",
        )(weight, first, second, grad)
    )


def on_device(
    sizes,
    tokens,
    positions,
    cotangent,
    query_weight,
    query_first,
    query_second,
    keyval_weight,
    keyval_first,
    keyval_second,
    output_weight,
    output_first,
    output_second,
    gateup_weight,
    gateup_first,
    gateup_second,
    down_weight,
    down_first,
    down_second,
    gains,
    gains_first,
    gains_second,
):
    n = sizes["tensor"]
    rank = lax.axis_index("tensor")
    offsets = ring_offsets(n)
    chunk_ids = [(rank + off + n) % n for off in offsets]
    rows, width = tokens.shape
    piece = keyval_weight.shape[1]
    block, cols = query_weight.shape

    ids = jnp.stack(chunk_ids).astype(jnp.int32)
    first_slots = ring_gather(first_pack(query_weight, keyval_weight, gains), n)
    attn_in = first_join(ids, first_slots, block, piece)
    feed_in = jnp.concatenate(
        [gateup_weight.astype(LOW), down_weight.T.astype(LOW)[None]], 0
    )
    attn_in, feed_in = after(attn_in, feed_in)
    attn_low = lax.all_gather(attn_in, "dp", axis=0, tiled=True)
    output_piece, _ = after(output_weight.T.astype(LOW), first_slots)
    output_slots = ring_gather(output_piece, n)
    grad_start, _ = after(cotangent, output_slots)
    grad_slots = ring_gather(grad_start, n, 1)
    feed_in, _ = after(feed_in, output_slots)
    feed_low = lax.all_gather(feed_in, "dp", axis=1, tiled=True)
    out_halves = dp_spread(
        jnp.concatenate(output_slots, 1), sizes["dp"], (attn_low, grad_slots)
    )
    out_order = jnp.concatenate([dp_order(sizes["dp"], block, odd) for odd in (0, 1)])

    span = H * HD + 2 * KVD
    own_positions = lax.dynamic_slice_in_dim(positions, rank * rows, rows, 0)
    freqs = 10000.0 ** (-jnp.arange(0, HD, 2, dtype=F32) / HD)
    angles = freqs[:, None] * own_positions.astype(F32)[None, :]
    cosine, sine = lax.optimization_barrier((jnp.cos(angles), jnp.sin(angles)))
    x = tokens.astype(F32)
    kv_t, first_normalized, gain_rows, first_inverse = begin(tokens, attn_low, cosine, sine)
    first_gain, second_gain = gain_rows[:1], gain_rows[1:2]
    q_t = project(first_normalized, attn_low, cosine, sine)
    kv_slots = jnp.stack(ring_gather(kv_t, n))
    grad_slots, kv_slots = after(grad_slots, kv_slots)
    grad_slots = ring_gather(grad_start, n, n, grad_slots)
    per_block = H // n
    meta = jnp.stack(
        [c * rows for c in chunk_ids]
        + [(c * per_block) // GROUP for c in chunk_ids]
        + [rank * rows]
    ).astype(jnp.int32)
    meta = jnp.concatenate([meta, out_order])
    pos_row = own_positions[None, :]
    mixed_t, mixed, lse = attend(meta, pos_row, q_t, kv_slots, n)
    out_halves, _ = after(out_halves, (mixed, grad_slots))
    out_pieces = out_halves + [swap(held, sizes["dp"], 1) for held in out_halves]
    residual, second_normalized, second_inverse = mix(
        out_order, mixed, tokens, second_gain, out_pieces
    )
    second_normalized, grad_slots = after(second_normalized, grad_slots)

    rows_slots = ring_gather(second_normalized, n, 1)
    grads_t = [turned(x) for x in grad_slots]
    groups = [[s for s in range(n) if abs(offsets[s]) == k] for k in range(n // 2 + 1)]
    order = sum(groups, [])
    rows_t, acts, part_slots, last = [None] * n, [], [None] * n, [grads_t]
    for k, group in enumerate(groups):
        if k == 2:
            rows_slots = ring_gather(second_normalized, n, n, rows_slots)
        chunks, _ = after([rows_slots[s] for s in group], last)
        for i, s in enumerate(group):
            rows_t[s] = turned(chunks[i])
        if k + 1 < len(groups):
            chunks, _ = after(chunks, [rows_t[s] for s in group])
        act, part = feed(chunks, [grad_slots[s] for s in group], feed_low)
        acts.append(act)
        last = part
        for i, s in enumerate(group):
            part_slots[s] = part[i * rows : (i + 1) * rows]
        if k == 0:
            for s in groups[1]:
                rows_slots[s], _ = after(rows_slots[s], part)
    acts, _ = after(acts, last)
    grad_mlp = feed_grad(acts, [rows_t[s] for s in order], 0, 2)
    from_left = ring_way(part_slots, n, 1)
    passed = []
    from_right = ring_way(part_slots, n, -1, passed, grad_mlp[0, :8, :128])
    acts, _ = after(acts, passed)
    grad_mlp = feed_grad(acts, [grads_t[s] for s in order], 2, 1, grad_mlp)
    second_grad = ring_sum(part_slots[0], from_left, from_right)
    mlp_parts = [contract(act[2], feed_low[2], 1, 1).astype(LOW) for act in acts]
    second_grad, (_, mlp_parts) = after(second_grad, (grad_mlp, mlp_parts))
    owned_mlp = lax.psum_scatter(grad_mlp, "dp", scatter_dimension=1, tiled=True)

    second_unit = residual * second_inverse
    residual_grad = cotangent.astype(F32) + norm_backward(
        second_grad, second_unit, second_inverse, second_gain
    )
    second_gain_grad = jnp.sum(second_grad * second_unit, 0)
    back = residual_grad.astype(LOW)
    mlp_slots = [None] * n
    for group, part in zip(groups, mlp_parts):
        for i, s in enumerate(group):
            mlp_slots[s] = part[i * rows : (i + 1) * rows]
    block_far, block_left = ring_most(mlp_slots, n), ring_way(mlp_slots, n, 1)
    grad_q_t, grad_kv = attend_back(
        meta, pos_row, q_t, kv_slots, back, out_pieces, mixed_t, lse, cosine, sine, n
    )
    (grad_q_t, grad_kv), _ = after((grad_q_t, grad_kv), (block_far, block_left))

    places = [dp_order(sizes["dp"], block, odd) for odd in (0, 1)]
    kv_parts = [grad_kv[s] for s in range(n)]
    kv_left = ring_way(kv_parts, n, 1)
    block_right = ring_last(mlp_slots, n, block_far, grad_kv)
    kv_far = ring_most(kv_parts, n)
    own_kv = ring_sum(kv_parts[0], ring_last(kv_parts, n, kv_far, block_right), kv_left)
    partner = weight_grad(
        first_normalized, grad_q_t, n * cols, cols, n, lambda i: i, lambda i: i, places[1]
    )
    partner = swap(partner, sizes["dp"], 1)
    out_rows, _ = after(back, grad_q_t)
    heads_cols = H * HD // (2 * KVD)
    grad_pack = weight_grad(
        out_rows, mixed_t, span, 2 * KVD, heads_cols, lambda i: i, lambda i: i
    )

    own_kv, _ = after(own_kv, partner)
    grad_k = own_kv[:KVD].reshape(KVH, 2, HD // 2, rows)
    upper, lower = grad_k[:, 0], grad_k[:, 1]
    grad_k = jnp.stack([upper * cosine + lower * sine, lower * cosine - upper * sine], 1)
    grad_kv_t = jnp.concatenate(
        [grad_k.reshape(KVD, rows).astype(LOW), own_kv[KVD:].astype(LOW)], 0
    )
    grad_pack = weight_grad(
        first_normalized, grad_kv_t, span, 2 * KVD, 1, lambda i: 0, lambda i: heads_cols,
        None, grad_pack,
    )
    grad_pack, owned_mlp = after(grad_pack, owned_mlp)
    owned_pack = lax.psum_scatter(grad_pack, "dp", scatter_dimension=0, tiled=True)

    query_slots, last = [None] * n, grad_pack
    for s in order[::-1]:
        query_rows, _ = after(first_normalized, last)
        last = query_slots[s] = weight_grad(
            query_rows, grad_q_t, cols, cols, 1, lambda i, s=s: s, lambda i: 0, places[0], None,
            partner, lambda i, s=s: s,
        )
    query_far, query_left = ring_most(query_slots, n), ring_way(query_slots, n, 1)
    owned_gateup, owned_down = owned_mlp[:2], owned_mlp[2]
    gateup_up = adamw(
        gateup_weight, gateup_first, gateup_second, owned_gateup.astype(F32), RATE_GATEUP, DECAY
    )
    down_up = adamw_turned(down_weight, down_first, down_second, owned_down, RATE_DOWN)
    query_right = ring_last(query_slots, n, query_far, (gateup_up, down_up))
    query_sum = ring_sum(query_slots[0], query_left, query_right).astype(LOW)
    block_out = residual + ring_sum(mlp_slots[0], block_left, block_right)
    (back_q_t, back_kv_t), _ = after((grad_q_t, grad_kv_t), query_slots)
    grad_qkv_t = jnp.concatenate(
        [back_q_t, back_kv_t, jnp.zeros((attn_low.shape[1] - span, rows), LOW)], 0
    )
    first_grad = contract(grad_qkv_t, attn_low, 0, 1)
    first_unit = x * first_inverse
    first_gain_grad = jnp.sum(first_grad * first_unit, 0)
    layer_input_gradient = residual_grad + norm_backward(
        first_grad, first_unit, first_inverse, first_gain
    )
    gain_grads, bit = jnp.stack([first_gain_grad, second_gain_grad]), 1
    while bit < sizes["dp"]:
        gain_grads = gain_grads + swap(gain_grads, sizes["dp"], bit)
        bit *= 2
    gain_grads = lax.dynamic_slice_in_dim(gain_grads, lax.axis_index("dp") * block, block, 1)
    gain_cols = jnp.pad(gain_grads.T, ((0, 0), (0, 126)))

    slots = tail_pack(ids, owned_pack, gain_cols, piece, cols)
    query_sum, _ = after(query_sum, slots[0])
    own_query = dp_scatter(query_sum, sizes["dp"], ()).astype(F32)
    query_up = adamw(query_weight, query_first, query_second, own_query, RATE_QUERY, DECAY)
    parts = [slots[0], ring_way(slots, n, -1), ring_way(slots, n, 1)]
    states = [output_weight, output_first, output_second, keyval_weight, keyval_first]
    states += [keyval_second, gains, gains_first, gains_second]
    parts = [part for part in parts if part is not None]
    last = tail_adamw(parts, states, block, piece)
    output_up, keyval_up, gains_up = tuple(last[:3]), tuple(last[3:6]), tuple(last[6:])
    return (
        (block_out, layer_input_gradient)
        + query_up
        + keyval_up
        + output_up
        + gateup_up
        + down_up
        + gains_up
    )


def solution(mesh):
    rows = P(("dp", "tensor"), None)
    grid = P("dp", "tensor")
    cross = P("tensor", "dp")
    pair = P(None, ("dp", "tensor"), None)
    stacked = P(None, "dp", "tensor")
    narrow = P(None, ("dp", "tensor"))
    states = (grid,) * 3 + (pair,) * 3 + (cross,) * 3 + (stacked,) * 3 + (cross,) * 3 + (narrow,) * 3
    return jax.shard_map(
        functools.partial(on_device, dict(mesh.shape)),
        mesh=mesh,
        in_specs=(rows, P("dp"), rows) + states,
        out_specs=(rows, rows) + states,
        check_vma=False,
    )
```
